128 devices in a mesh: dp: 64 (over y, x, z_hi, core), seq: 2 (over z_lo).
Axes of the slice: x: 4, y: 4, z: 4 (z_hi: 2, z_lo: 2; z = z_hi * 2 + z_lo), core: 2. Of those that a mesh axis runs over, the one named last changes fastest.
Arguments:
- inputs: bfloat16 [64, 258, 768], P('dp', 'seq'), may hold values from -6 to 6
- skipped: bfloat16 [64, 258, 768], P('dp', 'seq'), may hold values from -6 to 6
- cotangent: bfloat16 [64, 258, 768], P('dp', 'seq'), may hold values from -6 to 6
- timestep: int32 [64], P('dp'), may hold values from 0 to 999
- class_ids: int32 [64], P('dp'), may hold values from 0 to 1000
- time_weight: float32 [1000], replicated, may hold values from 0.3 to 3
- class_weight: float32 [1001], replicated, may hold values from 0.3 to 3
- skip_weight: bfloat16 [1179648], P(('dp', 'seq')), may hold values from -0.15625 to 0.15625
- skip_bias: bfloat16 [768], P(('dp', 'seq')), may hold values from -1.796875 to 1.796875
- first_gain: bfloat16 [768], P(('dp', 'seq')), may hold values from 0.25 to 1.75
- first_shift: bfloat16 [768], P(('dp', 'seq')), may hold values from -1.796875 to 1.796875
- triple_weight: bfloat16 [1769472], P(('dp', 'seq')), may hold values from -0.21875 to 0.21875
- merge_weight: bfloat16 [589824], P(('dp', 'seq')), may hold values from -1.75 to 1.75
- merge_bias: bfloat16 [768], P(('dp', 'seq')), may hold values from -1.796875 to 1.796875
- second_gain: bfloat16 [768], P(('dp', 'seq')), may hold values from 0.25 to 1.75
- second_shift: bfloat16 [768], P(('dp', 'seq')), may hold values from -1.796875 to 1.796875
- expand_weight: bfloat16 [2359296], P(('dp', 'seq')), may hold values from -0.21875 to 0.21875
- expand_bias: bfloat16 [3072], P(('dp', 'seq')), may hold values from -1.796875 to 1.796875
- contract_weight: bfloat16 [2359296], P(('dp', 'seq')), may hold values from -0.109375 to 0.109375
- contract_bias: bfloat16 [768], P(('dp', 'seq')), may hold values from -1.796875 to 1.796875
Outputs:
- block_output: bfloat16 [64, 258, 768], P('dp', 'seq')
- input_grad: bfloat16 [64, 258, 768], P('dp', 'seq')
- skip_grad: bfloat16 [64, 258, 768], P('dp', 'seq')
- skip_weight_grad: float32 [1179648], P(('dp', 'seq'))
- skip_bias_grad: float32 [768], P(('dp', 'seq'))
- first_gain_grad: float32 [768], P(('dp', 'seq'))
- first_shift_grad: float32 [768], P(('dp', 'seq'))
- triple_weight_grad: float32 [1769472], P(('dp', 'seq'))
- merge_weight_grad: float32 [589824], P(('dp', 'seq'))
- merge_bias_grad: float32 [768], P(('dp', 'seq'))
- second_gain_grad: float32 [768], P(('dp', 'seq'))
- second_shift_grad: float32 [768], P(('dp', 'seq'))
- expand_weight_grad: float32 [2359296], P(('dp', 'seq'))
- expand_bias_grad: float32 [3072], P(('dp', 'seq'))
- contract_weight_grad: float32 [2359296], P(('dp', 'seq'))
- contract_bias_grad: float32 [768], P(('dp', 'seq'))
The draws below stay inside these ranges and needn't reach their ends.
All inputs are finite; a program needn't handle non-finite values.
Results may differ from the reference program's by a relative error of at most 0.017.
Values may be sent and summed in bfloat16 or wider, within the bound.
No kernel may reach another device: no remote copies, remote signals or barrier semaphores. Data moves between devices by JAX's collectives and lax.ppermute only.
A program may use at most 192 MiB of HBM per device.

```python
import math
import jax
import jax.numpy as jnp
from jax import lax

D = 768
HEADS = 12
HEAD_DIM = 64
FF = 3072
LEN = 258
STEPS = 1000
CLASSES = 1001
IMAGES = 64


def with_ends(entries, rng, low, high):
    longest = entries.shape.index(max(entries.shape))
    spots = []
    for shift in (0, 1):
        where = [jax.random.randint(jax.random.fold_in(rng, axis), (), 0, length) for axis, length in enumerate(entries.shape)]
        where[longest] = (where[longest] + shift) % entries.shape[longest]
        spots.append(tuple(where))
    return entries.at[spots[0]].set(low).at[spots[1]].set(high)


def steps_of(own_key, extent, split, smallest, high):
    def one(dim, shards_of):
        draws = jax.random.uniform(jax.random.fold_in(jax.random.fold_in(own_key, 6), dim), (shards_of,), jnp.float32, smallest / len(split), high / len(split))
        return jnp.repeat(jnp.exp(draws), extent[dim] // shards_of).reshape((-1,) + (1,) * (len(extent) - dim - 1))

    level = one(*split[0])
    for cut in split[1:]:
        level = level * one(*cut)
    return level


def noise(stream_key, extent, spread, reach, cuts=(), held_as=jnp.bfloat16):
    loudness = steps_of(stream_key, extent, cuts, -0.22, 0.18) if cuts else 1.0
    entries = jax.random.normal(stream_key, extent, jnp.float32) * spread * loudness
    return jnp.minimum(jnp.maximum(entries, -reach), reach).astype(held_as)


def setup_inputs(seed: int = 0) -> dict:
    arg_keys = jax.random.split(jax.random.key(seed), 21)
    inputs = noise(arg_keys[0], (IMAGES, LEN, D), 1.0, 6.0, ((0, 64), (1, 2)))
    skipped = noise(arg_keys[1], (IMAGES, LEN, D), 1.0, 6.0, ((0, 64), (1, 2)))
    cotangent = noise(arg_keys[2], (IMAGES, LEN, D), 1.0, 6.0, ((0, 64), (1, 2)))
    timestep = with_ends(jax.random.randint(arg_keys[3], (IMAGES,), 0, STEPS), jax.random.fold_in(arg_keys[3], 1), 0, STEPS - 1).astype(jnp.int32)
    class_ids = with_ends(jax.random.randint(arg_keys[4], (IMAGES,), 0, CLASSES), jax.random.fold_in(arg_keys[4], 1), 0, CLASSES - 1).astype(jnp.int32)
    time_weight = jnp.clip(jnp.exp(jax.random.uniform(arg_keys[5], (STEPS,), jnp.float32, math.log(0.3), math.log(3.0))), 0.3, 3.0)
    class_weight = jnp.clip(jnp.exp(jax.random.uniform(arg_keys[6], (CLASSES,), jnp.float32, math.log(0.3), math.log(3.0))), 0.3, 3.0)
    skip_weight = noise(arg_keys[7], (2 * D * D,), (2 * D) ** -0.5, 0.15625, ((0, 128),))
    skip_bias = noise(arg_keys[8], (D,), 0.3, 1.796875, ((0, 128),))
    first_gain = jnp.clip(1.0 + 0.15 * jax.random.normal(arg_keys[9], (D,), jnp.float32), 0.25, 1.75).astype(jnp.bfloat16)
    first_shift = noise(arg_keys[10], (D,), 0.3, 1.796875, ((0, 128),))
    triple_weight = noise(arg_keys[11], (3 * D * D,), D ** -0.5, 0.21875, ((0, 128),))
    merge_weight = noise(arg_keys[12], (D * D,), (D // 64) ** -0.5, 1.75, ((0, 128),))
    merge_bias = noise(arg_keys[13], (D,), 0.3, 1.796875, ((0, 128),))
    second_gain = jnp.clip(1.0 + 0.15 * jax.random.normal(arg_keys[14], (D,), jnp.float32), 0.25, 1.75).astype(jnp.bfloat16)
    second_shift = noise(arg_keys[15], (D,), 0.3, 1.796875, ((0, 128),))
    expand_weight = noise(arg_keys[16], (D * FF,), D ** -0.5, 0.21875, ((0, 128),))
    expand_bias = noise(arg_keys[17], (FF,), 0.3, 1.796875, ((0, 128),))
    contract_weight = noise(arg_keys[18], (FF * D,), FF ** -0.5, 0.109375, ((0, 128),))
    contract_bias = noise(arg_keys[19], (D,), 0.3, 1.796875, ((0, 128),))
    return {"inputs": inputs, "skipped": skipped, "cotangent": cotangent, "timestep": timestep, "class_ids": class_ids, "time_weight": time_weight, "class_weight": class_weight, "skip_weight": skip_weight, "skip_bias": skip_bias, "first_gain": first_gain, "first_shift": first_shift, "triple_weight": triple_weight, "merge_weight": merge_weight, "merge_bias": merge_bias, "second_gain": second_gain, "second_shift": second_shift, "expand_weight": expand_weight, "expand_bias": expand_bias, "contract_weight": contract_weight, "contract_bias": contract_bias}


@jax.custom_vjp
def low(v):
    return lax.optimization_barrier(v.astype(jnp.bfloat16)).astype(jnp.float32)

@jax.custom_vjp
def low_back(v):
    return v

def low_keep(v):
    return (low(v), None)

def low_pass(kept, grad):
    return (grad,)

def back_keep(v):
    return (v, None)

def back_low(kept, grad):
    return (low(grad),)
low.defvjp(low_keep, low_pass)
low_back.defvjp(back_keep, back_low)
epsilon = 1e-05
highest = lax.Precision.HIGHEST

def matmul(left, right):
    return jnp.matmul(left, right, precision=highest)

def norm_apply(values, gain, shift):
    mean_value = lax.optimization_barrier(jnp.mean(values, axis=-1, keepdims=True))
    centered = values - mean_value
    variance = lax.optimization_barrier(jnp.mean(centered * centered, axis=-1, keepdims=True))
    return centered * lax.rsqrt(variance + epsilon) * gain + shift

def gelu_exact(values):
    return 0.5 * values * (1.0 + lax.erf(values * (1.0 / math.sqrt(2.0))))

def block_forward(params, inputs, skipped):
    skip_mat, skip_add, first_scale, first_move, triple_mat, merge_mat, merge_add, second_scale, second_move, expand_mat, expand_add, contract_mat, contract_add = params
    group_size, seq_len = (inputs.shape[0], inputs.shape[1])
    joined = jnp.concatenate([inputs, skipped], axis=-1)
    united = low_back(matmul(joined, skip_mat) + skip_add)
    normed = low(norm_apply(united, first_scale, first_move))
    triple = low_back(low(matmul(normed, triple_mat)))
    split_heads = triple.reshape(group_size, seq_len, 3, HEADS, HEAD_DIM)
    scores = jnp.einsum('gqhd,gkhd->ghqk', split_heads[:, :, 0], split_heads[:, :, 1], precision=highest)
    scores = low_back(scores * (1.0 / math.sqrt(HEAD_DIM)))
    largest = lax.optimization_barrier(jnp.max(scores, axis=-1, keepdims=True))
    powered = jnp.exp(scores - largest)
    attention = low(powered / lax.optimization_barrier(jnp.sum(powered, axis=-1, keepdims=True)))
    mixed_heads = jnp.einsum('ghqk,gkhd->gqhd', attention, split_heads[:, :, 2], precision=highest)
    mixed_heads = low_back(low(mixed_heads.reshape(group_size, seq_len, D)))
    attended = low_back(matmul(mixed_heads, merge_mat) + merge_add)
    middle = united + attended
    normed_two = low(norm_apply(middle, second_scale, second_move))
    before = low_back(matmul(normed_two, expand_mat) + expand_add)
    active = low(gelu_exact(before))
    branch_out = low_back(matmul(active, contract_mat) + contract_add)
    return middle + branch_out

def reference(inputs, skipped, cotangent, timestep, class_ids, time_weight, class_weight, skip_weight, skip_bias, first_gain, first_shift, triple_weight, merge_weight, merge_bias, second_gain, second_shift, expand_weight, expand_bias, contract_weight, contract_bias):
    flat_all = (skip_weight, skip_bias, first_gain, first_shift, triple_weight, merge_weight, merge_bias, second_gain, second_shift, expand_weight, expand_bias, contract_weight, contract_bias)
    target_shapes = ((2 * D, D), (D,), (D,), (D,), (D, 3 * D), (D, D), (D,), (D,), (D,), (D, FF), (FF,), (FF, D), (D,))
    params = tuple((flat_piece.astype(jnp.float32).reshape(target_shape) for flat_piece, target_shape in zip(flat_all, target_shapes)))
    group_size = math.gcd(IMAGES, 16)
    groups = IMAGES // group_size

    def forward_all(weights_all, inputs_all, skipped_all):

        def one_group(pair):
            return block_forward(weights_all, pair[0], pair[1])
        stacked = (inputs_all.reshape(groups, group_size, LEN, D), skipped_all.reshape(groups, group_size, LEN, D))
        result = lax.map(jax.checkpoint(one_group), stacked)
        return result.reshape(IMAGES, LEN, D)
    output, pullback = jax.vjp(forward_all, params, inputs.astype(jnp.float32), skipped.astype(jnp.float32))
    image_scale = time_weight[timestep] * class_weight[class_ids]
    seed_grad = cotangent.astype(jnp.float32) * image_scale[:, None, None]
    weight_grads, input_grad, skip_grad = pullback(seed_grad)
    return (output.astype(jnp.bfloat16), input_grad.astype(jnp.bfloat16), skip_grad.astype(jnp.bfloat16), weight_grads[0].reshape(-1), weight_grads[1].reshape(-1), weight_grads[2].reshape(-1), weight_grads[3].reshape(-1), weight_grads[4].reshape(-1), weight_grads[5].reshape(-1), weight_grads[6].reshape(-1), weight_grads[7].reshape(-1), weight_grads[8].reshape(-1), weight_grads[9].reshape(-1), weight_grads[10].reshape(-1), weight_grads[11].reshape(-1), weight_grads[12].reshape(-1))
```

```python
import math

import jax
import jax.numpy as jnp
from jax import lax
from jax.sharding import PartitionSpec as P

D = 768
HEADS = 12
HEAD_DIM = 64
FF = 3072


epsilon = 1e-05


def product(left, right):
    return jnp.dot(left, right, preferred_element_type=jnp.float32)


def left_contract(left, right):
    return lax.dot_general(
        left, right, (((0,), (0,)), ((), ())), preferred_element_type=jnp.float32
    )


def right_contract(left, right):
    return lax.dot_general(
        left, right, (((1,), (1,)), ((), ())), preferred_element_type=jnp.float32
    )


def norm_forward(values, gain, shift):
    mean_value = jnp.mean(values, axis=-1, keepdims=True)
    centered = values - mean_value
    variance = jnp.mean(centered * centered, axis=-1, keepdims=True)
    inverse = lax.rsqrt(variance + epsilon)
    scaled = centered * inverse
    return (scaled * gain + shift, scaled, inverse)


def norm_backward(incoming, scaled, inverse, gain):
    weighted = incoming * gain
    first_mean = jnp.mean(weighted, axis=-1, keepdims=True)
    second_mean = jnp.mean(weighted * scaled, axis=-1, keepdims=True)
    value_grad = inverse * (weighted - first_mean - scaled * second_mean)
    return (value_grad, jnp.sum(incoming * scaled, axis=0), jnp.sum(incoming, axis=0))


def gelu_exact(values):
    return 0.5 * values * (1.0 + lax.erf(values * (1.0 / math.sqrt(2.0))))


def gelu_slope(values):
    cumulative = 0.5 * (1.0 + lax.erf(values * (1.0 / math.sqrt(2.0))))
    density = jnp.exp(-0.5 * values * values) * (1.0 / math.sqrt(2.0 * math.pi))
    return cumulative + values * density


def pick_table(indices, table):
    match = indices[:, None] == jnp.arange(table.shape[0], dtype=jnp.int32)[None, :]
    return jnp.sum(jnp.where(match, table[None, :], 0.0), axis=1)


HALF = D // 2
PLANE = ("y", "x")
COLUMN = ("h", "c", "l")
ROWS = (12, 6, 6, 6, 6, 6, 6, 6, 6, 24, 4)
VECTORS = (6, 6, 6, 6, 6, 6, 24, 6)


def swap(block, axis):
    return lax.ppermute(block, axis, [(0, 1), (1, 0)])


def cut(block, axis):
    at, parts = 0, []
    for rows in ROWS:
        size = rows if axis == 1 else 8 * rows
        parts.append(lax.slice_in_dim(block, at, at + size, axis=axis))
        at += size
    return parts


def gather_all(weights, vectors):
    skip, triple, merge, expand, contract = weights
    row = jnp.pad(jnp.concatenate(vectors)[None, :], ((0, ROWS[10] - 1), (0, HALF - sum(VECTORS))))

    def half(side):
        columns = lambda block: block[:, side * HALF : (side + 1) * HALF]
        pieces = [columns(skip)]
        pieces += [columns(triple[:, k * D : (k + 1) * D]) for k in range(3)]
        pieces += [columns(merge)]
        pieces += [expand[:, (4 * side + k) * HALF : (4 * side + k + 1) * HALF] for k in range(4)]
        pieces += [columns(contract), row]
        return jnp.concatenate(pieces, axis=0)

    packed = jnp.stack([half(0), half(1)])
    to_all = jnp.broadcast_to(packed[None, :, None], (2, 2, 2) + packed.shape[1:]).reshape((8,) + packed.shape[1:])
    column = lax.all_to_all(to_all, COLUMN, 0, 0, tiled=True)
    group = jnp.concatenate([p.reshape(-1, HALF) for p in cut(column, 1)], axis=0)
    own = lax.all_gather(group, PLANE, axis=0, tiled=False).reshape((16,) + group.shape)
    other = swap(own, "c")
    core = lax.axis_index("c")
    first = cut2(jnp.where(core == 0, own, other))
    second = cut2(jnp.where(core == 0, other, own))
    pair = lambda k: jnp.concatenate([first[k], second[k]], axis=1)
    flat = first[10].reshape(128, ROWS[10], HALF)[:, 0]
    spots, at = [], 0
    for size in VECTORS:
        spots.append(flat[:, at : at + size].reshape(-1))
        at += size
    triple_mat = jnp.concatenate([pair(1), pair(2), pair(3)], axis=1)
    expand_mat = jnp.concatenate([first[k] for k in range(5, 9)] + [second[k] for k in range(5, 9)], axis=1)
    return (pair(0), triple_mat, pair(4), expand_mat, pair(9)), spots


def cut2(block):
    at, parts = 0, []
    for rows in ROWS:
        parts.append(block[:, at : at + 8 * rows].reshape(-1, HALF))
        at += 8 * rows
    return parts


def scatter_all(grads, vector_grads):
    skip, triple, merge, expand, contract = grads
    rows = [v.reshape(128, -1) for v in vector_grads]
    flat = jnp.pad(jnp.concatenate(rows, axis=1)[:, None], ((0, 0), (0, ROWS[10] - 1), (0, HALF - sum(VECTORS))))

    def half(side):
        columns = lambda block: block[:, side * HALF : (side + 1) * HALF]
        pieces = [columns(skip)]
        pieces += [columns(triple[:, k * D : (k + 1) * D]) for k in range(3)]
        pieces += [columns(merge)]
        pieces += [expand[:, (4 * side + k) * HALF : (4 * side + k + 1) * HALF] for k in range(4)]
        pieces += [columns(contract), flat if side == 0 else jnp.zeros_like(flat)]
        return jnp.concatenate([p.reshape(16, -1, HALF) for p in pieces], axis=1).astype(jnp.bfloat16)

    core = lax.axis_index("c")
    low, high = half(0), half(1)
    own = jnp.where(core == 0, low, high)
    sent = jnp.where(core == 0, high, low)
    chip = (own.astype(jnp.float32) + swap(sent, "c").astype(jnp.float32)).astype(jnp.bfloat16)
    plane = lax.psum_scatter(chip.reshape(-1, HALF), PLANE, scatter_dimension=0, tiled=True)
    column = jnp.concatenate([p.reshape(2, 2, 2, -1, HALF) for p in cut(plane, 0)], axis=3)
    column = column.transpose(0, 2, 1, 3, 4).reshape((4, 2) + column.shape[3:])
    parts = lax.all_to_all(column, ("h", "l"), 0, 0, tiled=True)
    total = jnp.sum(parts.astype(jnp.float32), axis=0)
    mine = jnp.where(core == 0, total[0], total[1])
    theirs = swap(jnp.where(core == 0, total[1], total[0]), "c")
    low = jnp.where(core == 0, mine, theirs)
    high = jnp.where(core == 0, theirs, mine)
    firsts, seconds, at = [], [], 0
    for size in ROWS:
        firsts.append(low[at : at + size])
        seconds.append(high[at : at + size])
        at += size
    pair = lambda k: jnp.concatenate([firsts[k], seconds[k]], axis=1)
    triple_out = jnp.concatenate([pair(1), pair(2), pair(3)], axis=1)
    expand_out = jnp.concatenate(firsts[5:9] + seconds[5:9], axis=1)
    weights = [p.reshape(-1) for p in (pair(0), triple_out, pair(4), expand_out, pair(9))]
    spots, at = [], 0
    for size in VECTORS:
        spots.append(firsts[10][0, at : at + size])
        at += size
    return weights, spots


def per_device(
    inputs,
    skipped,
    cotangent,
    timestep,
    class_ids,
    time_weight,
    class_weight,
    skip_weight,
    skip_bias,
    first_gain,
    first_shift,
    triple_weight,
    merge_weight,
    merge_bias,
    second_gain,
    second_shift,
    expand_weight,
    expand_bias,
    contract_weight,
    contract_bias,
):
    (skip_mat, triple_mat, merge_mat, expand_mat, contract_mat), spots = gather_all(
        (
            skip_weight.reshape(-1, D),
            triple_weight.reshape(-1, 3 * D),
            merge_weight.reshape(-1, D),
            expand_weight.reshape(-1, FF),
            contract_weight.reshape(-1, D),
        ),
        (skip_bias, first_gain, first_shift, merge_bias, second_gain, second_shift, expand_bias, contract_bias),
    )
    skip_add, first_scale, first_move, merge_add, second_scale, second_move, expand_add, contract_add = spots
    images, half_len = (inputs.shape[0], inputs.shape[1])
    tok_rows = images * half_len
    score_scale = 1.0 / math.sqrt(HEAD_DIM)
    joined = jnp.concatenate([inputs.reshape(tok_rows, D), skipped.reshape(tok_rows, D)], axis=1)
    united = product(joined, skip_mat) + skip_add.astype(jnp.float32)
    normed, first_hat, first_inv = norm_forward(
        united, first_scale.astype(jnp.float32), first_move.astype(jnp.float32)
    )
    normed_low = normed.astype(jnp.bfloat16)
    triple = product(normed_low, triple_mat).astype(jnp.bfloat16)
    query = triple[:, :D].reshape(images, half_len, HEADS, HEAD_DIM)
    pair_all = triple[:, D:].reshape(images, half_len, 2 * D)
    pair_all = jnp.concatenate([pair_all, swap(pair_all, "l")], axis=1)
    key_all, value_all = pair_all[:, :, :D], pair_all[:, :, D:]
    seq_len = key_all.shape[1]
    key_heads = key_all.reshape(images, seq_len, HEADS, HEAD_DIM)
    value_heads = value_all.reshape(images, seq_len, HEADS, HEAD_DIM)
    scores = (
        jnp.einsum("iqhd,ikhd->ihqk", query, key_heads, preferred_element_type=jnp.float32)
        * score_scale
    )
    largest = jnp.max(scores, axis=-1, keepdims=True)
    powered = jnp.exp(scores - largest)
    totals = jnp.sum(powered, axis=-1, keepdims=True)
    log_total = largest + jnp.log(totals)
    attention = (powered / totals).astype(jnp.bfloat16)
    mixed_heads = jnp.einsum(
        "ihqk,ikhd->iqhd", attention, value_heads, preferred_element_type=jnp.float32
    )
    mixed_low = mixed_heads.reshape(tok_rows, D).astype(jnp.bfloat16)
    middle = united + product(mixed_low, merge_mat) + merge_add.astype(jnp.float32)
    normed_two, second_hat, second_inv = norm_forward(
        middle, second_scale.astype(jnp.float32), second_move.astype(jnp.float32)
    )
    normed_two_low = normed_two.astype(jnp.bfloat16)
    before = product(normed_two_low, expand_mat) + expand_add.astype(jnp.float32)
    active = gelu_exact(before).astype(jnp.bfloat16)
    output = middle + product(active, contract_mat) + contract_add.astype(jnp.float32)
    image_scale = pick_table(timestep, time_weight) * pick_table(class_ids, class_weight)
    out_grad = (cotangent.astype(jnp.float32) * image_scale[:, None, None]).reshape(tok_rows, D)
    after_low = out_grad.astype(jnp.bfloat16)
    contract_bias_grad = jnp.sum(after_low.astype(jnp.float32), axis=0)
    contract_weight_grad = left_contract(active, after_low)
    before_low = (right_contract(after_low, contract_mat) * gelu_slope(before)).astype(jnp.bfloat16)
    expand_bias_grad = jnp.sum(before_low.astype(jnp.float32), axis=0)
    expand_weight_grad = left_contract(normed_two_low, before_low)
    back_two, second_gain_grad, second_shift_grad = norm_backward(
        right_contract(before_low, expand_mat),
        second_hat,
        second_inv,
        second_scale.astype(jnp.float32),
    )
    middle_grad = out_grad + back_two
    attend_low = middle_grad.astype(jnp.bfloat16)
    merge_bias_grad = jnp.sum(attend_low.astype(jnp.float32), axis=0)
    merge_weight_grad = left_contract(mixed_low, attend_low)
    mixed_grad = right_contract(attend_low, merge_mat).astype(jnp.bfloat16)
    mixed_grad = mixed_grad.reshape(images, half_len, HEADS, HEAD_DIM)
    scores_again = (
        jnp.einsum("iqhd,ikhd->ihqk", query, key_heads, preferred_element_type=jnp.float32)
        * score_scale
    )
    soft_again = jnp.exp(scores_again - log_total)
    soft_low = soft_again.astype(jnp.bfloat16)
    soft_grad = jnp.einsum(
        "iqhd,ikhd->ihqk", mixed_grad, value_heads, preferred_element_type=jnp.float32
    )
    inner_sum = jnp.sum(soft_again * soft_grad, axis=-1, keepdims=True)
    scores_grad = (soft_again * (soft_grad - inner_sum)).astype(jnp.bfloat16)
    query_grad = (
        jnp.einsum("ihqk,ikhd->iqhd", scores_grad, key_heads, preferred_element_type=jnp.float32)
        * score_scale
    )
    query_grad = query_grad.reshape(tok_rows, D).astype(jnp.bfloat16)
    key_part = (
        jnp.einsum("ihqk,iqhd->ikhd", scores_grad, query, preferred_element_type=jnp.float32)
        * score_scale
    )
    value_part = jnp.einsum(
        "ihqk,iqhd->ikhd", soft_low, mixed_grad, preferred_element_type=jnp.float32
    )
    pair_part = jnp.concatenate(
        [key_part.reshape(images, seq_len, D), value_part.reshape(images, seq_len, D)], axis=2
    )
    came = swap(pair_part[:, half_len:].astype(jnp.bfloat16), "l")
    pair_grad = pair_part[:, :half_len] + came.astype(jnp.float32)
    triple_grad = jnp.concatenate(
        [query_grad, pair_grad.reshape(tok_rows, 2 * D).astype(jnp.bfloat16)], axis=1
    )
    triple_weight_grad = left_contract(normed_low, triple_grad)
    back_one, first_gain_grad, first_shift_grad = norm_backward(
        right_contract(triple_grad, triple_mat),
        first_hat,
        first_inv,
        first_scale.astype(jnp.float32),
    )
    united_low = (middle_grad + back_one).astype(jnp.bfloat16)
    skip_bias_grad = jnp.sum(united_low.astype(jnp.float32), axis=0)
    skip_weight_grad = left_contract(joined, united_low)
    joined_grad = right_contract(united_low, skip_mat)
    input_grad = joined_grad[:, :D].reshape(images, half_len, D).astype(jnp.bfloat16)
    skip_grad = joined_grad[:, D:].reshape(images, half_len, D).astype(jnp.bfloat16)
    weight_grads, spot_grads = scatter_all(
        (skip_weight_grad, triple_weight_grad, merge_weight_grad, expand_weight_grad, contract_weight_grad),
        (
            skip_bias_grad,
            first_gain_grad,
            first_shift_grad,
            merge_bias_grad,
            second_gain_grad,
            second_shift_grad,
            expand_bias_grad,
            contract_bias_grad,
        ),
    )
    owned = (
        weight_grads[0],
        spot_grads[0],
        spot_grads[1],
        spot_grads[2],
        weight_grads[1],
        weight_grads[2],
        spot_grads[3],
        spot_grads[4],
        spot_grads[5],
        weight_grads[3],
        spot_grads[6],
        weight_grads[4],
        spot_grads[7],
    )
    block_output = output.reshape(images, half_len, D).astype(jnp.bfloat16)
    return (block_output, input_grad, skip_grad) + tuple(owned)


def solution(mesh):
    fine = jax.sharding.Mesh(mesh.devices.reshape(4, 4, 2, 2, 2), ("y", "x", "h", "c", "l"))
    images = ("y", "x", "h", "c")
    everything = images + ("l",)
    tokens, shard = P(images, "l", None), P(everything)
    return jax.shard_map(
        per_device,
        mesh=fine,
        in_specs=(tokens,) * 3 + (P(images),) * 2 + (P(),) * 2 + (shard,) * 13,
        out_specs=(tokens,) * 3 + (shard,) * 13,
        check_vma=False,
    )
```

```python
import functools
import math

import jax
import jax.numpy as jnp
from jax import lax
from jax.experimental import pallas as pl
from jax.experimental.pallas import tpu as pltpu
from jax.sharding import PartitionSpec as P

D = 768
HEADS = 12
HEAD_DIM = 64
FF = 3072
HALF = D // 2
STRIPS = FF // D
TOKENS = 129
PAD = 144
KEYS = 2 * PAD
PLANES = 16
PLANE = ("y", "x")
COLUMN = ("h", "c", "l")
SKIP, MERGE, SPOTS, TRIPLE = 0, 96, 144, 160
FIRST_ROWS = 304
ONE_ROWS = 160
TWO_ROWS = 144
EXPAND, CONTRACT = 0, 192
SECOND_ROWS = 384
ONE_PACK = (12, 6, 1)
TWO_PACK = (6, 6, 6)
SECOND_PACK = (6, 6, 6, 6, 24)
SPOT_WIDTH = 66
epsilon = 1e-05
score_scale = 1.0 / math.sqrt(HEAD_DIM)
BF, F32 = jnp.bfloat16, jnp.float32
ROOM = 56 * 2**20


def mm(left, right):
    return jnp.dot(left, right, preferred_element_type=F32)


def mm_t(left, right):
    return lax.dot_general(left, right, (((1,), (1,)), ((), ())), preferred_element_type=F32)


def t_mm(left, right):
    return lax.dot_general(left, right, (((0,), (0,)), ((), ())), preferred_element_type=F32)


def order(core, one, two):
    return jnp.where(core == 0, one, two), jnp.where(core == 0, two, one)


def split(core, block):
    return order(core, block[:, :HALF], block[:, HALF:])


def norm_stats(values):
    mean_value = jnp.mean(values, axis=-1, keepdims=True)
    centered = values - mean_value
    variance = jnp.mean(centered * centered, axis=-1, keepdims=True)
    inverse = lax.rsqrt(variance + epsilon)
    return centered * inverse, inverse


def norm_backward(incoming, scaled, inverse, gain):
    weighted = incoming * gain
    first_mean = jnp.mean(weighted, axis=-1, keepdims=True)
    second_mean = jnp.mean(weighted * scaled, axis=-1, keepdims=True)
    value_grad = inverse * (weighted - first_mean - scaled * second_mean)
    return (
        value_grad,
        jnp.sum(incoming * scaled, axis=0, keepdims=True),
        jnp.sum(incoming, axis=0, keepdims=True),
    )


def padded(block):
    return jnp.concatenate([block, jnp.zeros((PAD - TOKENS, block.shape[1]), block.dtype)], axis=0)


def load(pairs, sems):
    copies = [pltpu.make_async_copy(s, d, sems.at[k]) for k, (s, d) in enumerate(pairs)]
    for copy in copies:
        copy.start()
    return copies


def matrix(ref, at, rows):
    return ref[:, at : at + rows, :].reshape(PLANES * rows, HALF)


def spot_masks(width):
    lanes = lax.broadcasted_iota(jnp.int32, (128, D), 0)
    spots = lax.broadcasted_iota(jnp.int32, (128, D), 1)
    return lanes, lax.rem(spots, width), lax.div(spots, width)


def steps_to(place_ref, plane):
    return (plane // 4 - place_ref[1]) & 3, (plane % 4 - place_ref[2]) & 3


def wait(copies):
    for copy in copies:
        copy.wait()


def spots_kernel(first_ref, out_ref, rows_ref, sems):
    wait(load([(first_ref.at[:, SPOTS : SPOTS + 16, :], rows_ref)], sems))
    held = rows_ref[:, :, :128].astype(F32)[:, :8].reshape(128, 128).astype(BF)
    for j in range(7):
        lanes, place, owner = spot_masks(6)
        one_hot = (lanes - 6 * j == place).astype(BF)
        spread = jnp.where(owner == lanes, mm(held, one_hot), 0.0)
        out_ref[j : j + 1, :] = jnp.sum(spread, axis=0, keepdims=True)
    out_ref[7:8, :] = jnp.zeros((1, D), F32)
    lanes, place, owner = spot_masks(24)
    spread = mm(held, (lanes - 42 == place).astype(BF))
    for m in range(STRIPS):
        out_ref[8 + m : 9 + m, :] = jnp.sum(jnp.where(owner + 32 * m == lanes, spread, 0.0), axis=0, keepdims=True)
    out_ref[12:16, :] = jnp.zeros((4, D), F32)


def first_kernel(core_ref, in_ref, skip_ref, own_ref, other_ref, spots_ref, united_ref, normed_ref, query_ref, pair_ref, so, ss, to, ts, sems):
    core = core_ref[0]
    copies = load(
        [
            (own_ref.at[:, SKIP : SKIP + 96, :], so),
            (other_ref.at[:, SKIP : SKIP + 96, :], ss),
            (own_ref.at[:, TRIPLE : TRIPLE + 144, :], to),
            (other_ref.at[:, TRIPLE : TRIPLE + 144, :], ts),
        ],
        sems,
    )
    joined = jnp.concatenate([padded(in_ref[...]), padded(skip_ref[...])], axis=1)
    copies[0].wait()
    one = mm(joined, matrix(so, 0, 96))
    copies[1].wait()
    two = mm(joined, matrix(ss, 0, 96))
    united = jnp.concatenate(order(core, one, two), axis=1) + spots_ref[0:1, :]
    united_ref[...] = united
    scaled, _ = norm_stats(united)
    normed = (scaled * spots_ref[1:2, :] + spots_ref[2:3, :]).astype(BF)
    normed_ref[...] = normed
    copies[2].wait()
    copies[3].wait()
    for k in range(3):
        one = mm(normed, matrix(to, 48 * k, 48))
        two = mm(normed, matrix(ts, 48 * k, 48))
        block = jnp.concatenate(order(core, one, two), axis=1).astype(BF)
        if k == 0:
            query_ref[...] = block
        else:
            pair_ref[:, (k - 1) * D : k * D] = block


def key_mask():
    spots = lax.broadcasted_iota(jnp.int32, (1, KEYS), 1)
    return (spots < TOKENS) | ((spots >= PAD) & (spots < PAD + TOKENS))


def attend_kernel(core_ref, query_ref, pair_ref, came_ref, united_ref, own_ref, other_ref, spots_ref, mixed_ref, middle_ref, normed_ref, total_ref, mo, ms, sems):
    core = core_ref[0]
    copies = load(
        [(own_ref.at[:, MERGE : MERGE + 48, :], mo), (other_ref.at[:, MERGE : MERGE + 48, :], ms)], sems
    )
    mask = key_mask()
    total_ref[...] = jnp.zeros((PAD, 128), F32)
    for pair in range(HEADS // 2):
        at = slice(128 * pair, 128 * pair + 128)
        late = slice(D + 128 * pair, D + 128 * pair + 128)
        query = query_ref[:, at]
        keys = jnp.concatenate([pair_ref[:, at], came_ref[:, at]], axis=0)
        values = jnp.concatenate([pair_ref[:, late], came_ref[:, late]], axis=0)
        done = []
        for side in range(2):
            head = slice(HEAD_DIM * side, HEAD_DIM * side + HEAD_DIM)
            scores = mm_t(query[:, head], keys[:, head]) * score_scale
            scores = jnp.where(mask, scores, -1e30)
            largest = jnp.max(scores, axis=-1, keepdims=True)
            powered = jnp.exp(scores - largest)
            totals = jnp.sum(powered, axis=-1, keepdims=True)
            total_ref[:, 2 * pair + side : 2 * pair + side + 1] = largest + jnp.log(totals)
            soft_low = (powered / totals).astype(BF)
            done.append(mm(soft_low, values[:, head]))
        mixed_ref[:, at] = jnp.concatenate(done, axis=1).astype(BF)
    mixed = mixed_ref[...]
    copies[0].wait()
    copies[1].wait()
    one, two = mm(mixed, matrix(mo, 0, 48)), mm(mixed, matrix(ms, 0, 48))
    middle = united_ref[...] + jnp.concatenate(order(core, one, two), axis=1) + spots_ref[3:4, :]
    middle_ref[...] = middle
    scaled, _ = norm_stats(middle)
    normed_ref[...] = (scaled * spots_ref[4:5, :] + spots_ref[5:6, :]).astype(BF)


def forward_kernel(core_ref, scale_ref, normed_ref, middle_ref, cotangent_ref, own_ref, other_ref, spots_ref, out_ref, middle_grad_ref, vector_ref, grad_own, grad_sent, eo, es, co, cs, before_ref, active_ref, low_ref, go, gs, sems, out_sems):
    core = core_ref[0]
    copies = load(
        [
            (own_ref.at[:, EXPAND : EXPAND + 192, :], eo),
            (other_ref.at[:, EXPAND : EXPAND + 192, :], es),
            (own_ref.at[:, CONTRACT : CONTRACT + 192, :], co),
            (other_ref.at[:, CONTRACT : CONTRACT + 192, :], cs),
        ],
        sems,
    )
    normed = normed_ref[...]
    out_grad = padded(cotangent_ref[...].astype(F32) * scale_ref[0])
    after = out_grad.astype(BF)
    vector_ref[...] = jnp.zeros((16, D), F32)
    vector_ref[6:7, :] = jnp.sum(after.astype(F32), axis=0, keepdims=True)
    copies[0].wait()
    copies[1].wait()
    for k in range(STRIPS):
        one, two = order(core, mm(normed, matrix(eo, 48 * k, 48)), mm(normed, matrix(es, 48 * k, 48)))
        for side, block in ((0, one), (1, two)):
            at = side * STRIPS * HALF + k * HALF
            bias = spots_ref[8 + at // D : 9 + at // D, at % D : at % D + HALF]
            block = block + bias
            before_ref[:, at : at + HALF] = block
            active_ref[:, at : at + HALF] = (0.5 * block * (1.0 + lax.erf(block * (1.0 / math.sqrt(2.0))))).astype(BF)
    copies[2].wait()
    copies[3].wait()
    active = active_ref[...]
    one, two = mm(active, matrix(co, 0, 192)), mm(active, matrix(cs, 0, 192))
    output = middle_ref[...] + jnp.concatenate(order(core, one, two), axis=1) + spots_ref[6:7, :]
    out_ref[...] = output[:TOKENS].astype(BF)
    after_own, after_other = split(core, after)
    for j in range(2 * STRIPS):
        at, planes = slice(HALF * j, HALF * j + HALF), slice(2 * j, 2 * j + 2)
        one, two = split(core, t_mm(active_ref[:, at], after).astype(BF))
        go[planes, CONTRACT : CONTRACT + 192, :] = one.reshape(2, 192, HALF)
        gs[planes, CONTRACT : CONTRACT + 192, :] = two.reshape(2, 192, HALF)
        back = mm_t(after_own, co[planes, :, :].reshape(HALF, HALF)) + mm_t(after_other, cs[planes, :, :].reshape(HALF, HALF))
        before = before_ref[:, at]
        cumulative = 0.5 * (1.0 + lax.erf(before * (1.0 / math.sqrt(2.0))))
        density = jnp.exp(-0.5 * before * before) * (1.0 / math.sqrt(2.0 * math.pi))
        low = (back * (cumulative + before * density)).astype(BF)
        low_ref[:, at] = low
        row = 8 + j // 2
        vector_ref[row : row + 1, HALF * (j % 2) : HALF * (j % 2) + HALF] = jnp.sum(low.astype(F32), axis=0, keepdims=True)
    incoming = jnp.zeros((PAD, D), F32)
    for k in range(STRIPS):
        one, two = order(
            core,
            low_ref[:, k * HALF : (k + 1) * HALF],
            low_ref[:, (STRIPS + k) * HALF : (STRIPS + k + 1) * HALF],
        )
        go[:, EXPAND + 48 * k : EXPAND + 48 * (k + 1), :] = t_mm(normed, one).astype(BF).reshape(PLANES, 48, HALF)
        gs[:, EXPAND + 48 * k : EXPAND + 48 * (k + 1), :] = t_mm(normed, two).astype(BF).reshape(PLANES, 48, HALF)
        incoming = incoming + mm_t(one, matrix(eo, 48 * k, 48)) + mm_t(two, matrix(es, 48 * k, 48))
    sends = load([(gs, grad_sent), (go, grad_own)], out_sems)
    scaled, inverse = norm_stats(middle_ref[...])
    back_two, gain_grad, shift_grad = norm_backward(incoming, scaled, inverse, spots_ref[4:5, :])
    vector_ref[4:5, :] = gain_grad
    vector_ref[5:6, :] = shift_grad
    middle_grad_ref[...] = out_grad + back_two
    for copy in sends:
        copy.wait()


def backward_kernel(core_ref, middle_grad_ref, query_ref, pair_ref, came_ref, total_ref, own_ref, other_ref, query_grad_ref, pair_grad_ref, sent_ref, mixed_grad_ref, mo, ms, sems):
    core = core_ref[0]
    copies = load(
        [(own_ref.at[:, MERGE : MERGE + 48, :], mo), (other_ref.at[:, MERGE : MERGE + 48, :], ms)], sems
    )
    attend_own, attend_other = split(core, middle_grad_ref[...].astype(BF))
    mask = key_mask()
    copies[0].wait()
    copies[1].wait()
    mixed_grad_ref[...] = (mm_t(attend_own, matrix(mo, 0, 48)) + mm_t(attend_other, matrix(ms, 0, 48))).astype(BF)
    for pair in range(HEADS // 2):
        at = slice(128 * pair, 128 * pair + 128)
        late = slice(D + 128 * pair, D + 128 * pair + 128)
        query, mixed_grad = query_ref[:, at], mixed_grad_ref[:, at]
        keys = jnp.concatenate([pair_ref[:, at], came_ref[:, at]], axis=0)
        values = jnp.concatenate([pair_ref[:, late], came_ref[:, late]], axis=0)
        query_parts, key_parts, value_parts = [], [], []
        for side in range(2):
            head = slice(HEAD_DIM * side, HEAD_DIM * side + HEAD_DIM)
            scores = mm_t(query[:, head], keys[:, head]) * score_scale
            scores = jnp.where(mask, scores, -1e30)
            soft = jnp.exp(scores - total_ref[:, 2 * pair + side : 2 * pair + side + 1])
            soft_grad = mm_t(mixed_grad[:, head], values[:, head])
            inner = jnp.sum(soft * soft_grad, axis=-1, keepdims=True)
            scores_grad = (soft * (soft_grad - inner)).astype(BF)
            query_parts.append(mm(scores_grad, keys[:, head]))
            key_parts.append(t_mm(scores_grad, query[:, head]))
            value_parts.append(t_mm(soft.astype(BF), mixed_grad[:, head]))
        query_grad_ref[:, at] = (jnp.concatenate(query_parts, axis=1) * score_scale).astype(BF)
        key_grad = jnp.concatenate(key_parts, axis=1) * score_scale
        value_grad = jnp.concatenate(value_parts, axis=1)
        pair_grad_ref[:, at] = key_grad[:PAD]
        pair_grad_ref[:, late] = value_grad[:PAD]
        sent_ref[:, at] = key_grad[PAD:].astype(BF)
        sent_ref[:, late] = value_grad[PAD:].astype(BF)


def scatter(place_ref, refs, blocks, at, planes, by_y):
    rows = blocks[0].shape[0] // len(planes)
    for n, plane in enumerate(planes):
        step_y, step_x = steps_to(place_ref, plane)
        spot = 4 * step_y + step_x if by_y else 4 * step_x + step_y
        for ref, block in zip(refs, blocks):
            ref[spot, at : at + rows, :] = block[n * rows : (n + 1) * rows]


def triple_kernel(place_ref, united_ref, normed_ref, middle_grad_ref, query_grad_ref, pair_grad_ref, came_ref, own_ref, other_ref, spots_ref, low_ref, vector_ref, grad_own, grad_sent, to, ts, go, gs, sems, out_sems):
    core = place_ref[0]
    copies = load(
        [(own_ref.at[:, TRIPLE : TRIPLE + 144, :], to), (other_ref.at[:, TRIPLE : TRIPLE + 144, :], ts)], sems
    )
    middle_grad = middle_grad_ref[...]
    normed = normed_ref[...]
    incoming = jnp.zeros((PAD, D), F32)
    wait(copies)
    for k in range(3):
        if k == 0:
            block = query_grad_ref[...]
        else:
            at = slice((k - 1) * D, k * D)
            block = (pair_grad_ref[:, at] + came_ref[:, at].astype(F32)).astype(BF)
        one, two = split(core, block)
        grads = split(core, t_mm(normed, block).astype(BF))
        scatter(place_ref, (go, gs), grads, 48 * k, range(PLANES), True)
        incoming = incoming + mm_t(one, matrix(to, 48 * k, 48)) + mm_t(two, matrix(ts, 48 * k, 48))
    sends = load([(gs, grad_sent), (go, grad_own)], out_sems)
    scaled, inverse = norm_stats(united_ref[...])
    back_one, gain_grad, shift_grad = norm_backward(incoming, scaled, inverse, spots_ref[1:2, :])
    united_low = (middle_grad + back_one).astype(BF)
    low_ref[...] = united_low
    vector_ref[0:1, :] = jnp.sum(united_low.astype(F32), axis=0, keepdims=True)
    vector_ref[1:2, :] = gain_grad
    vector_ref[2:3, :] = shift_grad
    vector_ref[3:8, :] = jnp.zeros((5, D), F32)
    wait(sends)


def skip_kernel(place_ref, in_ref, skip_ref, mixed_ref, middle_grad_ref, low_ref, early_ref, vector_ref, own_ref, other_ref, in_grad_ref, skip_grad_ref, grad_own, grad_sent, so, ss, go, gs, sems, out_sems):
    core = place_ref[0]
    copies = load(
        [(own_ref.at[:, SKIP : SKIP + 96, :], so), (other_ref.at[:, SKIP : SKIP + 96, :], ss)], sems
    )
    attend = middle_grad_ref[...].astype(BF)
    merge_bias_grad = jnp.sum(attend.astype(F32), axis=0, keepdims=True)
    grads = split(core, t_mm(mixed_ref[...], attend).astype(BF))
    scatter(place_ref, (go, gs), grads, MERGE, range(PLANES), False)
    vectors = [vector_ref[j : j + 1, :] for j in range(3)] + [merge_bias_grad] + [early_ref[j : j + 1, :] for j in (4, 5, 6)]
    rows = jnp.zeros((128, 128), F32)
    for j, vector in enumerate(vectors):
        lanes, place, owner = spot_masks(6)
        spread = jnp.where(owner == lanes, vector, 0.0).astype(BF)
        rows = rows + mm_t(spread, (lanes - 6 * j == place).astype(BF))
    lanes, place, owner = spot_masks(24)
    for m in range(STRIPS):
        spread = jnp.where(owner + 32 * m == lanes, early_ref[8 + m : 9 + m, :], 0.0).astype(BF)
        rows = rows + mm_t(spread, (lanes - 42 == place).astype(BF))
    rows = rows.reshape(PLANES, 8, 128)
    rows = jnp.concatenate([rows, jnp.zeros((PLANES, 8, 128), F32)], axis=1)
    rows = jnp.concatenate([rows, jnp.zeros((PLANES, 16, HALF - 128), F32)], axis=2).reshape(PLANES * 16, HALF).astype(BF)
    scatter(place_ref, (go, gs), (rows, rows), SPOTS, range(PLANES), False)
    united_low = low_ref[...]
    low_own, low_other = split(core, united_low)
    wait(copies)
    for half, block_ref, grad_ref in ((0, in_ref, in_grad_ref), (1, skip_ref, skip_grad_ref)):
        block = padded(block_ref[...])
        for part in range(2):
            first = 8 * half + 4 * part
            at = slice(HALF * part, HALF * part + HALF)
            grads = split(core, t_mm(block[:, at], united_low).astype(BF))
            scatter(place_ref, (go, gs), grads, SKIP, range(first, first + 4), False)
            planes = slice(first, first + 4)
            back = mm_t(low_own, so[planes, :, :].reshape(HALF, HALF)) + mm_t(low_other, ss[planes, :, :].reshape(HALF, HALF))
            grad_ref[:, at] = back[:TOKENS].astype(BF)
    wait(load([(gs, grad_sent), (go, grad_own)], out_sems))


def call(kernel, name, args, outs, scratch, flops):
    place = {
        "s": pl.BlockSpec(memory_space=pltpu.SMEM),
        "v": pl.BlockSpec(memory_space=pltpu.VMEM),
        "a": pl.BlockSpec(memory_space=pl.ANY),
    }
    moved = sum(a.size * a.dtype.itemsize for a, _ in args)
    return pl.pallas_call(
        kernel,
        out_shape=[jax.ShapeDtypeStruct(shape, dtype) for shape, dtype, _ in outs],
        in_specs=[place[w] for _, w in args],
        out_specs=[place[w] for _, _, w in outs],
        scratch_shapes=scratch,
        compiler_params=pltpu.CompilerParams(vmem_limit_bytes=ROOM),
        cost_estimate=pl.CostEstimate(flops=int(flops), bytes_accessed=int(moved), transcendentals=0),
        name=name,
    )(*[a for a, _ in args])


def swap(block, axis):
    return lax.ppermute(block, axis, [(0, 1), (1, 0)])


def step(block, axis, steps):
    return lax.ppermute(block, axis, [((i + steps) % 4, i) for i in range(4)])


def sum_part(kept, came, first, second):
    kept, came = (a.reshape((4, 4) + a.shape[1:]) for a in (kept, came))
    chip = [kept[k].astype(F32) + came[k].astype(F32) for k in range(4)]
    line = chip[0]
    for k in (1, 2, 3):
        line = line + step(chip[k].astype(BF), first, 4 - k).astype(F32)
    total = line[0]
    for k in (1, 2, 3):
        total = total + step(line[k].astype(BF), second, 4 - k).astype(F32)
    return total.astype(BF)


def halves(matrix_rows, strips):
    cut = [matrix_rows[:, k * HALF : (k + 1) * HALF] for k in range(2 * strips)]
    return cut[:strips], cut[strips:]


def column_gather(first_half, second_half):
    packed = jnp.stack([first_half, second_half])
    shape = packed.shape[1:]
    to_all = jnp.broadcast_to(packed[None, :, None], (2, 2, 2) + shape).reshape((8,) + shape)
    return lax.all_to_all(to_all, COLUMN, 0, 0, tiled=True)


def regroup(block, pack):
    at, parts = 0, []
    for rows in pack:
        parts.append(block[:, at : at + rows].reshape(-1, HALF))
        at += rows
    return parts


def pick_table(indices, table):
    match = indices[:, None] == jnp.arange(table.shape[0], dtype=jnp.int32)[None, :]
    return jnp.sum(jnp.where(match, table[None, :], 0.0), axis=1)


def per_device(
    inputs,
    skipped,
    cotangent,
    timestep,
    class_ids,
    time_weight,
    class_weight,
    skip_weight,
    skip_bias,
    first_gain,
    first_shift,
    triple_weight,
    merge_weight,
    merge_bias,
    second_gain,
    second_shift,
    expand_weight,
    expand_bias,
    contract_weight,
    contract_bias,
):
    core_index = lax.axis_index("c").astype(jnp.int32)
    core = core_index[None]
    place = jnp.stack([core_index, lax.axis_index("y").astype(jnp.int32), lax.axis_index("x").astype(jnp.int32)])

    scale = pick_table(timestep, time_weight) * pick_table(class_ids, class_weight)

    skip0, skip1 = halves(skip_weight.reshape(-1, D), 1)
    triple_cut = triple_weight.reshape(-1, 3 * D)
    triple0 = [triple_cut[:, k * D : k * D + HALF] for k in range(3)]
    triple1 = [triple_cut[:, k * D + HALF : (k + 1) * D] for k in range(3)]
    merge0, merge1 = halves(merge_weight.reshape(-1, D), 1)
    expand0, expand1 = halves(expand_weight.reshape(-1, FF), STRIPS)
    contract0, contract1 = halves(contract_weight.reshape(-1, D), 1)
    vectors = jnp.concatenate(
        [skip_bias, first_gain, first_shift, merge_bias, second_gain, second_shift, contract_bias, expand_bias]
    )
    row = jnp.pad(vectors[None, :], ((0, 0), (0, HALF - SPOT_WIDTH)))
    column = column_gather(
        jnp.concatenate(skip0 + merge0 + [row] + triple0 + expand0 + contract0, axis=0),
        jnp.concatenate(skip1 + merge1 + [row] + triple1 + expand1 + contract1, axis=0),
    )
    group = regroup(column, ONE_PACK + TWO_PACK + SECOND_PACK)
    first = jnp.concatenate(group[:3] + [jnp.zeros((8, HALF), BF)] + group[3:6], axis=0)
    second = jnp.concatenate(group[6:], axis=0)
    first, second, scale = lax.optimization_barrier((first, second, scale))
    second_own = lax.all_gather(second, PLANE, axis=0, tiled=True).reshape(PLANES, SECOND_ROWS, HALF)
    first_own = lax.all_to_all(
        jnp.broadcast_to(first[None], (PLANES, FIRST_ROWS, HALF)), PLANE, 0, 0, tiled=True
    )
    first_other = swap(first_own, "c")

    inputs, skipped, cotangent = (a.reshape(TOKENS, D) for a in (inputs, skipped, cotangent))
    sem = pltpu.SemaphoreType.DMA
    weight = lambda rows: pltpu.VMEM((PLANES, rows, HALF), BF)
    tokens = lambda width, dtype=BF, where="v": ((PAD, width), dtype, where)

    (spots,) = call(
        spots_kernel, "vectors", [(first_own, "a")], [((16, D), F32, "v")], [weight(16), sem((1,))], 2e8
    )
    plane = lambda rows: ((PLANES, rows, HALF), BF, "a")
    united, normed, query, pair = call(
        first_kernel,
        "skip_and_triple",
        [(core, "s"), (inputs, "v"), (skipped, "v"), (first_own, "a"), (first_other, "a"), (spots, "v")],
        [tokens(D, F32), tokens(D), tokens(D), tokens(2 * D)],
        [weight(96), weight(96), weight(144), weight(144), sem((4,))],
        2 * PAD * D * (2 * D + 3 * D),
    )
    pair_came = swap(pair, "l")
    second_own, pair_came = lax.optimization_barrier((second_own, pair_came))
    second_other = swap(second_own, "c")
    mixed, middle, normed_two, totals = call(
        attend_kernel,
        "attention",
        [
            (core, "s"),
            (query, "v"),
            (pair, "v"),
            (pair_came, "v"),
            (united, "v"),
            (first_own, "a"),
            (first_other, "a"),
            (spots, "v"),
        ],
        [tokens(D), tokens(D, F32), tokens(D), tokens(128, F32)],
        [weight(48), weight(48), sem((2,))],
        2 * PAD * D * (D + 2 * KEYS),
    )
    output, middle_grad, vector_grads, second_kept, second_sent = call(
        forward_kernel,
        "feed_forward",
        [
            (core, "s"),
            (scale, "s"),
            (normed_two, "v"),
            (middle, "v"),
            (cotangent, "v"),
            (second_own, "a"),
            (second_other, "a"),
            (spots, "v"),
        ],
        [
            ((TOKENS, D), BF, "v"),
            tokens(D, F32),
            ((16, D), F32, "v"),
            plane(SECOND_ROWS),
            plane(SECOND_ROWS),
        ],
        [weight(192)] * 4
        + [pltpu.VMEM((PAD, FF), F32), pltpu.VMEM((PAD, FF), BF), pltpu.VMEM((PAD, FF), BF)]
        + [weight(SECOND_ROWS)] * 2
        + [sem((4,)), sem((2,))],
        2 * PAD * D * FF * 6,
    )
    second_came = swap(second_sent, "c")
    query_grad, pair_grad, pair_sent = call(
        backward_kernel,
        "attention_backward",
        [
            (core, "s"),
            (middle_grad, "v"),
            (query, "v"),
            (pair, "v"),
            (pair_came, "v"),
            (totals, "v"),
            (first_own, "a"),
            (first_other, "a"),
        ],
        [tokens(D), tokens(2 * D, F32), tokens(2 * D)],
        [pltpu.VMEM((PAD, D), BF), weight(48), weight(48), sem((2,))],
        2 * PAD * D * (D + 5 * KEYS),
    )
    grad_came = swap(pair_sent, "l")
    rows = PLANES * SECOND_ROWS
    second_chip = (second_kept.astype(F32) + second_came.astype(F32)).astype(BF).reshape(rows, HALF)
    second_chip, pair_grad = lax.optimization_barrier((second_chip, pair_grad))
    second_sum = lax.psum_scatter(second_chip, PLANE, scatter_dimension=0, tiled=True)
    united_low, late_grads, two_kept, two_sent = call(
        triple_kernel,
        "triple_backward",
        [
            (place, "s"),
            (united, "v"),
            (normed, "v"),
            (middle_grad, "v"),
            (query_grad, "v"),
            (pair_grad, "v"),
            (grad_came, "v"),
            (first_own, "a"),
            (first_other, "a"),
            (spots, "v"),
        ],
        [tokens(D), ((8, D), F32, "v"), plane(TWO_ROWS), plane(TWO_ROWS)],
        [weight(TWO_ROWS)] * 4 + [sem((2,)), sem((2,))],
        2 * PAD * D * (3 * D) * 2,
    )
    two_came = swap(two_sent, "c")
    input_grad, skip_grad, one_kept, one_sent = call(
        skip_kernel,
        "skip_backward",
        [
            (place, "s"),
            (inputs, "v"),
            (skipped, "v"),
            (mixed, "v"),
            (middle_grad, "v"),
            (united_low, "v"),
            (vector_grads, "v"),
            (late_grads, "v"),
            (first_own, "a"),
            (first_other, "a"),
        ],
        [((TOKENS, D), BF, "v"), ((TOKENS, D), BF, "v"), plane(ONE_ROWS), plane(ONE_ROWS)],
        [weight(96), weight(96), weight(ONE_ROWS), weight(ONE_ROWS), sem((2,)), sem((2,))],
        2 * PAD * D * (2 * D + D) * 2,
    )
    one_came = swap(one_sent, "c")
    two_sum = sum_part(two_kept, two_came, "y", "x")
    one_sum = sum_part(one_kept, one_came, "x", "y")

    pack = ONE_PACK + TWO_PACK + SECOND_PACK
    parts = []
    for block, sizes in ((one_sum, ONE_PACK), (two_sum, TWO_PACK), (second_sum, SECOND_PACK)):
        at = 0
        for size in sizes:
            parts.append(block[at : at + 8 * size].reshape(2, 2, 2, size, HALF))
            at += 8 * size
    column = jnp.concatenate(parts, axis=3).transpose(0, 2, 1, 3, 4)
    column = column.reshape((4, 2) + column.shape[3:])
    total = jnp.sum(lax.all_to_all(column, ("h", "l"), 0, 0, tiled=True).astype(F32), axis=0)
    mine, sent = order(core_index, total[0], total[1])
    low, high = order(core_index, mine, swap(sent, "c"))
    lows, highs, at = [], [], 0
    for size in pack:
        lows.append(low[at : at + size])
        highs.append(high[at : at + size])
        at += size
    skip_out = jnp.concatenate([lows[0], highs[0]], axis=1)
    merge_out = jnp.concatenate([lows[1], highs[1]], axis=1)
    vector_out = lows[2][0]
    triple_out = jnp.concatenate([b for k in range(3, 6) for b in (lows[k], highs[k])], axis=1)
    expand_out = jnp.concatenate(lows[6:10] + highs[6:10], axis=1)
    contract_out = jnp.concatenate([lows[10], highs[10]], axis=1)
    spot = lambda j: vector_out[6 * j : 6 * j + 6]
    return (
        output[None],
        input_grad[None],
        skip_grad[None],
        skip_out.reshape(-1),
        spot(0),
        spot(1),
        spot(2),
        triple_out.reshape(-1),
        merge_out.reshape(-1),
        spot(3),
        spot(4),
        spot(5),
        expand_out.reshape(-1),
        vector_out[42:66],
        contract_out.reshape(-1),
        spot(6),
    )


def solution(mesh):
    fine = jax.sharding.Mesh(mesh.devices.reshape(4, 4, 2, 2, 2), ("y", "x", "h", "c", "l"))
    images = ("y", "x", "h", "c")
    everything = images + ("l",)
    tokens, shard = P(images, "l", None), P(everything)
    return jax.shard_map(
        per_device,
        mesh=fine,
        in_specs=(tokens,) * 3 + (P(images),) * 2 + (P(),) * 2 + (shard,) * 13,
        out_specs=(tokens,) * 3 + (shard,) * 13,
        check_vma=False,
    )
```

```python
import functools
import math

import jax
import jax.numpy as jnp
import numpy as np
from jax import lax
from jax.experimental import pallas as pl
from jax.experimental.pallas import tpu as pltpu
from jax.sharding import PartitionSpec as P

D = 768
HEADS = 12
HEAD_DIM = 64
FF = 3072
HALF = D // 2
STRIPS = FF // D
TOKENS = 129
PAD = 144
KEYS = 2 * PAD
PLANES = 16
PLANE = ("y", "x")
COLUMN = ("h", "c", "l")
SKIP, SPOTS, TRIPLE = 0, 96, 112
EXPAND, CONTRACT, MERGE = 0, 192, 384
FIRST_ROWS, SECOND_ROWS = 256, 432
ONE_ROWS, TWO_ROWS = 112, 144
EARLY_ROWS = 448
FIRST_PACK, SECOND_PACK = (12, 1, 6, 6, 6), (6, 6, 6, 6, 24, 6)
PACK = FIRST_PACK + SECOND_PACK
PACK_ROWS = 88
NAMES = ("skip", "triple", "expand", "contract", "merge")
SUM_ROWS = ONE_ROWS + TWO_ROWS + EARLY_ROWS
SUM_STARTS = (0, 96, 112, 160, 208) + tuple(256 + at for at in (0, 48, 96, 144, 192, 384))
epsilon = 1e-05
score_scale = 1.0 / math.sqrt(HEAD_DIM)
BF, F32 = jnp.bfloat16, jnp.float32
ATTEND = FF + FF // 2
NORMED = ATTEND + HALF
GIFT = NORMED + D


def mm(left, right):
    return jnp.dot(left, right, preferred_element_type=F32)


def mm_t(left, right):
    return lax.dot_general(left, right, (((1,), (1,)), ((), ())), preferred_element_type=F32)


def t_mm(left, right):
    return lax.dot_general(left, right, (((0,), (0,)), ((), ())), preferred_element_type=F32)


def order(core, one, two):
    return jnp.where(core == 0, one, two), jnp.where(core == 0, two, one)


def split(core, block):
    return order(core, block[:, :HALF], block[:, HALF:])


def norm_stats(values):
    mean_value = jnp.mean(values, axis=-1, keepdims=True)
    centered = values - mean_value
    variance = jnp.mean(centered * centered, axis=-1, keepdims=True)
    inverse = lax.rsqrt(variance + epsilon)
    return centered * inverse, inverse


def norm_backward(incoming, scaled, inverse, gain):
    weighted = incoming * gain
    first_mean = jnp.mean(weighted, axis=-1, keepdims=True)
    second_mean = jnp.mean(weighted * scaled, axis=-1, keepdims=True)
    value_grad = inverse * (weighted - first_mean - scaled * second_mean)
    return (
        value_grad,
        jnp.sum(incoming * scaled, axis=0, keepdims=True),
        jnp.sum(incoming, axis=0, keepdims=True),
    )


def padded(block):
    return jnp.concatenate([block, jnp.zeros((PAD - TOKENS, block.shape[1]), block.dtype)], axis=0)


def load(pairs, sems):
    copies = [pltpu.make_async_copy(s, d, sems.at[k]) for k, (s, d) in enumerate(pairs)]
    for copy in copies:
        copy.start()
    return copies


def matrix(ref, at, rows):
    return ref[:, at : at + rows, :].reshape(PLANES * rows, HALF)


def spot_masks(width):
    lanes = lax.broadcasted_iota(jnp.int32, (128, D), 0)
    spots = lax.broadcasted_iota(jnp.int32, (128, D), 1)
    return lanes, lax.rem(spots, width), lax.div(spots, width)


def steps_to(place_ref, plane):
    return (plane // 4 - place_ref[1]) & 3, (plane % 4 - place_ref[2]) & 3


def wait(copies):
    for copy in copies:
        copy.wait()


def tiles_of(matrix_name):
    count, strips, across = {"skip": (6, 1, 6), "triple": (18, 1, 6), "merge": (6, 1, 6), "expand": (24, STRIPS, 24), "contract": (6, 1, 6)}[matrix_name]
    for tile in range(count):
        block, inside = divmod(tile, across)
        half, rest = divmod(inside, across // 2)
        yield tile, half, block + rest // 3, rest % 3


def pack_kernel(*refs):
    count = len(NAMES)
    sources, (row_ref, out_ref, rows_ref), scratch = refs[:count], refs[count : count + 3], refs[count + 3 :]
    low, scratch, sems = scratch[:count], scratch[count : 2 * count], scratch[2 * count]
    copies = load(list(zip(sources, low)), sems)
    at = 0
    for name, held, ref, copy in zip(NAMES, scratch, low, copies):
        copy.wait()
        held[...] = ref[...].astype(F32)
        tiles = list(tiles_of(name))
        rows = held.shape[0] // len(tiles)
        for tile, half, strip, spot in tiles:
            first = at + strip * rows
            rows_ref[half, first : first + rows, 128 * spot : 128 * spot + 128] = held[pl.ds(tile, rows, stride=len(tiles)), :]
        at += rows * (1 + max(t[2] for t in tiles))
        if name == "skip":
            rows_ref[0, at : at + 1, :] = row_ref[...]
            rows_ref[1, at : at + 1, :] = row_ref[...]
            at += 1
    rows_ref[:, at:PACK_ROWS, :] = jnp.zeros((2, PACK_ROWS - at, HALF), F32)
    for half in range(2):
        packed = rows_ref[half].astype(BF)
        for device in range(8):
            if device // 2 % 2 == half:
                out_ref[device] = packed


def unpack_kernel(low_ref, high_ref, *refs):
    outs = dict(zip(NAMES, refs))
    at = 0
    for name in NAMES:
        tiles = list(tiles_of(name))
        rows = outs[name].shape[0] // len(tiles)
        for tile, half, strip, spot in tiles:
            first = at + strip * rows
            source = high_ref if half else low_ref
            outs[name][pl.ds(tile, rows, stride=len(tiles)), :] = source[first : first + rows, 128 * spot : 128 * spot + 128]
        at += rows * (1 + max(t[2] for t in tiles))
        if name == "skip":
            refs[5][...] = low_ref[at : at + 1, :128] + high_ref[at : at + 1, :128]
            at += 1


def prepare_kernel(core_ref, scale_ref, in_ref, skip_ref, cotangent_ref, after_ref, gift_ref):
    gift_ref[:, :D] = padded(in_ref[...])
    gift_ref[:, D : 2 * D] = padded(skip_ref[...])
    after = padded(cotangent_ref[...].astype(F32) * scale_ref[0]).astype(BF)
    after_ref[...] = after
    gift_ref[:, 2 * D :] = split(core_ref[0], after)[1]


def spots_kernel(first_ref, out_ref, rows_ref, sems):
    wait(load([(first_ref.at[:, SPOTS : SPOTS + 16, :], rows_ref)], sems))
    held = rows_ref[:, :, :128].astype(F32)[:, :8].reshape(128, 128).astype(BF)
    for j in range(7):
        lanes, place, owner = spot_masks(6)
        one_hot = (lanes - 6 * j == place).astype(BF)
        spread = jnp.where(owner == lanes, mm(held, one_hot), 0.0)
        out_ref[j : j + 1, :] = jnp.sum(spread, axis=0, keepdims=True)
    out_ref[7:8, :] = jnp.zeros((1, D), F32)
    lanes, place, owner = spot_masks(24)
    spread = mm(held, (lanes - 42 == place).astype(BF))
    for m in range(STRIPS):
        out_ref[8 + m : 9 + m, :] = jnp.sum(jnp.where(owner + 32 * m == lanes, spread, 0.0), axis=0, keepdims=True)
    out_ref[12:16, :] = jnp.zeros((4, D), F32)


def first_kernel(core_ref, joined_ref, own_ref, other_ref, spots_ref, united_ref, normed_ref, query_ref, pair_ref, so, ss, to, ts, sems):
    core = core_ref[0]
    copies = load(
        [
            (own_ref.at[:, SKIP : SKIP + 96, :], so),
            (other_ref.at[:, SKIP : SKIP + 96, :], ss),
            (own_ref.at[:, TRIPLE : TRIPLE + 144, :], to),
            (other_ref.at[:, TRIPLE : TRIPLE + 144, :], ts),
        ],
        sems,
    )
    joined = joined_ref[:, : 2 * D]
    copies[0].wait()
    one = mm(joined, matrix(so, 0, 96))
    copies[1].wait()
    two = mm(joined, matrix(ss, 0, 96))
    united = jnp.concatenate(order(core, one, two), axis=1) + spots_ref[0:1, :]
    united_ref[...] = united
    scaled, _ = norm_stats(united)
    normed = (scaled * spots_ref[1:2, :] + spots_ref[2:3, :]).astype(BF)
    normed_ref[...] = normed
    copies[2].wait()
    copies[3].wait()
    for k in range(3):
        one = mm(normed, matrix(to, 48 * k, 48))
        two = mm(normed, matrix(ts, 48 * k, 48))
        block = jnp.concatenate(order(core, one, two), axis=1).astype(BF)
        if k == 0:
            query_ref[...] = block
        else:
            pair_ref[:, (k - 1) * D : k * D] = block


def key_mask():
    spots = lax.broadcasted_iota(jnp.int32, (1, KEYS), 1)
    return (spots < TOKENS) | ((spots >= PAD) & (spots < PAD + TOKENS))


def attend_kernel(query_ref, pair_ref, came_ref, mixed_ref, total_ref):
    mask = key_mask()
    total_ref[...] = jnp.zeros((PAD, 128), F32)
    for pair in range(HEADS // 2):
        at = slice(128 * pair, 128 * pair + 128)
        late = slice(D + 128 * pair, D + 128 * pair + 128)
        query = query_ref[:, at]
        keys = jnp.concatenate([pair_ref[:, at], came_ref[:, at]], axis=0)
        values = jnp.concatenate([pair_ref[:, late], came_ref[:, late]], axis=0)
        done = []
        for side in range(2):
            head = slice(HEAD_DIM * side, HEAD_DIM * side + HEAD_DIM)
            scores = mm_t(query[:, head], keys[:, head]) * score_scale
            scores = jnp.where(mask, scores, -1e30)
            largest = jnp.max(scores, axis=-1, keepdims=True)
            powered = jnp.exp(scores - largest)
            totals = jnp.sum(powered, axis=-1, keepdims=True)
            total_ref[:, 2 * pair + side : 2 * pair + side + 1] = largest + jnp.log(totals)
            soft_low = (powered / totals).astype(BF)
            done.append(mm(soft_low, values[:, head]))
        mixed_ref[:, at] = jnp.concatenate(done, axis=1).astype(BF)


def forward_kernel(core_ref, scale_ref, mixed_ref, united_ref, cotangent_ref, after_ref, own_ref, other_ref, spots_ref, out_ref, middle_grad_ref, vector_ref, gift_ref, kept_ref, eo, es, co, cs, mo, ms, slope_ref, low_ref, sems):
    core = core_ref[0]
    copies = load(
        [
            (own_ref.at[:, MERGE : MERGE + 48, :], mo),
            (other_ref.at[:, MERGE : MERGE + 48, :], ms),
            *[
                (ref.at[:, 48 * k : 48 * k + 48, :], to.at[:, 48 * k : 48 * k + 48, :])
                for k in range(STRIPS)
                for ref, to in ((own_ref, eo), (other_ref, es))
            ],
            (own_ref.at[:, CONTRACT : CONTRACT + 192, :], co),
            (other_ref.at[:, CONTRACT : CONTRACT + 192, :], cs),
        ],
        sems,
    )
    after = after_ref[...]
    vector_ref[...] = jnp.zeros((16, D), F32)
    vector_ref[6:7, :] = jnp.sum(after.astype(F32), axis=0, keepdims=True)
    after_own, after_other = split(core, after)
    mixed = mixed_ref[...]
    wait(copies[:2])
    one, two = mm(mixed, matrix(mo, 0, 48)), mm(mixed, matrix(ms, 0, 48))
    middle = united_ref[...] + jnp.concatenate(order(core, one, two), axis=1) + spots_ref[3:4, :]
    scaled, inverse = norm_stats(middle)
    normed = (scaled * spots_ref[4:5, :] + spots_ref[5:6, :]).astype(BF)
    gift_ref[:, NORMED:] = normed
    for k in range(STRIPS):
        wait(copies[2 + 2 * k : 4 + 2 * k])
        one, two = order(core, mm(normed, matrix(eo, 48 * k, 48)), mm(normed, matrix(es, 48 * k, 48)))
        for side, block in ((0, one), (1, two)):
            at = side * STRIPS * HALF + k * HALF
            bias = spots_ref[8 + at // D : 9 + at // D, at % D : at % D + HALF]
            block = block + bias
            cumulative = 0.5 * (1.0 + lax.erf(block * (1.0 / math.sqrt(2.0))))
            density = jnp.exp(-0.5 * block * block) * (1.0 / math.sqrt(2.0 * math.pi))
            gift_ref[:, at : at + HALF] = (block * cumulative).astype(BF)
            slope_ref[:, at : at + HALF] = cumulative + block * density
    wait(copies[2 + 2 * STRIPS :])
    active = gift_ref[:, :FF]
    one, two = mm(active, matrix(co, 0, 192)), mm(active, matrix(cs, 0, 192))
    output = middle + jnp.concatenate(order(core, one, two), axis=1) + spots_ref[6:7, :]
    out_ref[...] = output[:TOKENS].astype(BF)
    for j in range(2 * STRIPS):
        at, planes = slice(HALF * j, HALF * j + HALF), slice(2 * j, 2 * j + 2)
        back = mm_t(after_own, co[planes, :, :].reshape(HALF, HALF)) + mm_t(after_other, cs[planes, :, :].reshape(HALF, HALF))
        low = (back * slope_ref[:, at]).astype(BF)
        low_ref[:, at] = low
        row = 8 + j // 2
        vector_ref[row : row + 1, HALF * (j % 2) : HALF * (j % 2) + HALF] = jnp.sum(low.astype(F32), axis=0, keepdims=True)
    incoming = jnp.zeros((PAD, D), F32)
    for k in range(STRIPS):
        one, two = order(
            core,
            low_ref[:, k * HALF : (k + 1) * HALF],
            low_ref[:, (STRIPS + k) * HALF : (STRIPS + k + 1) * HALF],
        )
        kept_ref[:, k * HALF : (k + 1) * HALF] = one
        gift_ref[:, FF + k * HALF : FF + (k + 1) * HALF] = two
        incoming = incoming + mm_t(one, matrix(eo, 48 * k, 48)) + mm_t(two, matrix(es, 48 * k, 48))
    back_two, gain_grad, shift_grad = norm_backward(incoming, scaled, inverse, spots_ref[4:5, :])
    vector_ref[4:5, :] = gain_grad
    vector_ref[5:6, :] = shift_grad
    middle_grad = padded(cotangent_ref[...].astype(F32) * scale_ref[0]) + back_two
    middle_grad_ref[...] = middle_grad
    attend = middle_grad.astype(BF)
    vector_ref[3:4, :] = jnp.sum(attend.astype(F32), axis=0, keepdims=True)
    gift_ref[:, ATTEND:NORMED] = split(core, attend)[1]


def early_kernel(core_ref, gift_any, came_any, kept_any, after_ref, first_came_ref, mixed_ref, mixed_came_ref, middle_grad_ref, grad_ref, gift_ref, came_ref, kept_ref, go, sems, out_sems):
    core = core_ref[0]
    copies = load(
        [
            (gift_any.at[:, :FF], gift_ref.at[:, :FF]),
            (came_any.at[:, :FF], came_ref.at[:, :FF]),
            (gift_any.at[:, NORMED:], gift_ref.at[:, NORMED:]),
            (came_any.at[:, FF:], came_ref.at[:, FF:]),
            (kept_any, kept_ref),
        ],
        sems,
    )
    after, after_came = split(core, after_ref[...])[0], first_came_ref[:, 2 * D :]
    wait(copies[:2])
    for j in range(2 * STRIPS):
        at, planes = slice(HALF * j, HALF * j + HALF), slice(2 * j, 2 * j + 2)
        grad = t_mm(gift_ref[:, at], after) + t_mm(came_ref[:, at], after_came)
        go[planes, CONTRACT : CONTRACT + 192, :] = grad.astype(BF).reshape(2, 192, HALF)
    rows = lambda at, to: (go.at[:, at:to, :], grad_ref.at[:, at:to, :])
    sends = load([rows(CONTRACT, CONTRACT + 192)], out_sems)
    wait(copies[2:])
    attend = split(core, middle_grad_ref[...].astype(BF))[0]
    grad = t_mm(mixed_ref[...], attend) + t_mm(mixed_came_ref[...], came_ref[:, ATTEND:NORMED])
    go[:, MERGE : MERGE + 48, :] = grad.astype(BF).reshape(PLANES, 48, HALF)
    go[:, MERGE + 48 :, :] = jnp.zeros((PLANES, EARLY_ROWS - MERGE - 48, HALF), BF)
    sends += load([rows(MERGE, EARLY_ROWS)], out_sems.at[1:])
    normed, normed_came = gift_ref[:, NORMED:], came_ref[:, NORMED:]
    for k in range(STRIPS):
        grad = t_mm(normed, kept_ref[:, k * HALF : (k + 1) * HALF]) + t_mm(
            normed_came, came_ref[:, FF + k * HALF : FF + (k + 1) * HALF]
        )
        go[:, EXPAND + 48 * k : EXPAND + 48 * (k + 1), :] = grad.astype(BF).reshape(PLANES, 48, HALF)
        sends += load([rows(EXPAND + 48 * k, EXPAND + 48 * (k + 1))], out_sems.at[2 + k :])
    wait(sends)


def backward_kernel(core_ref, middle_grad_ref, query_ref, pair_ref, came_ref, total_ref, own_ref, other_ref, query_grad_ref, pair_grad_ref, sent_ref, mixed_grad_ref, mo, ms, sems):
    core = core_ref[0]
    copies = load(
        [(own_ref.at[:, MERGE : MERGE + 48, :], mo), (other_ref.at[:, MERGE : MERGE + 48, :], ms)], sems
    )
    attend_own, attend_other = split(core, middle_grad_ref[...].astype(BF))
    mask = key_mask()
    copies[0].wait()
    copies[1].wait()
    mixed_grad_ref[...] = (mm_t(attend_own, matrix(mo, 0, 48)) + mm_t(attend_other, matrix(ms, 0, 48))).astype(BF)
    for pair in range(HEADS // 2):
        at = slice(128 * pair, 128 * pair + 128)
        late = slice(D + 128 * pair, D + 128 * pair + 128)
        query, mixed_grad = query_ref[:, at], mixed_grad_ref[:, at]
        keys = jnp.concatenate([pair_ref[:, at], came_ref[:, at]], axis=0)
        values = jnp.concatenate([pair_ref[:, late], came_ref[:, late]], axis=0)
        query_parts, key_parts, value_parts = [], [], []
        for side in range(2):
            head = slice(HEAD_DIM * side, HEAD_DIM * side + HEAD_DIM)
            scores = mm_t(query[:, head], keys[:, head]) * score_scale
            scores = jnp.where(mask, scores, -1e30)
            soft = jnp.exp(scores - total_ref[:, 2 * pair + side : 2 * pair + side + 1])
            soft_grad = mm_t(mixed_grad[:, head], values[:, head])
            inner = jnp.sum(soft * soft_grad, axis=-1, keepdims=True)
            scores_grad = (soft * (soft_grad - inner)).astype(BF)
            query_parts.append(mm(scores_grad, keys[:, head]))
            key_parts.append(t_mm(scores_grad, query[:, head]))
            value_parts.append(t_mm(soft.astype(BF), mixed_grad[:, head]))
        query_grad_ref[:, at] = (jnp.concatenate(query_parts, axis=1) * score_scale).astype(BF)
        key_grad = jnp.concatenate(key_parts, axis=1) * score_scale
        value_grad = jnp.concatenate(value_parts, axis=1)
        pair_grad_ref[:, at] = key_grad[:PAD]
        pair_grad_ref[:, late] = value_grad[:PAD]
        sent_ref[:, at] = key_grad[PAD:].astype(BF)
        sent_ref[:, late] = value_grad[PAD:].astype(BF)


def scatter(place_ref, ref, block, at, by_y):
    rows = block.shape[0] // PLANES
    for plane in range(PLANES):
        step_y, step_x = steps_to(place_ref, plane)
        spot = 4 * step_y + step_x if by_y else 4 * step_x + step_y
        ref[spot, at : at + rows, :] = block[plane * rows : (plane + 1) * rows]


def vector_rows(vectors, places):
    rows = jnp.zeros((128, 128), F32)
    for vector, at in zip(vectors, places):
        lanes, place, owner = spot_masks(6)
        spread = jnp.where(owner == lanes, vector, 0.0).astype(BF)
        rows = rows + mm_t(spread, (lanes - at == place).astype(BF))
    return rows


def query_kernel(core_ref, query_grad_ref, early_ref, own_ref, other_ref, incoming_ref, rows_ref, to, ts, sems):
    copies = load(
        [(own_ref.at[:, TRIPLE : TRIPLE + 48, :], to), (other_ref.at[:, TRIPLE : TRIPLE + 48, :], ts)], sems
    )
    rows = vector_rows([early_ref[j : j + 1, :] for j in range(3, 7)], (18, 24, 30, 36))
    lanes, place, owner = spot_masks(24)
    for m in range(STRIPS):
        spread = jnp.where(owner + 32 * m == lanes, early_ref[8 + m : 9 + m, :], 0.0).astype(BF)
        rows = rows + mm_t(spread, (lanes - 42 == place).astype(BF))
    rows_ref[...] = rows
    one, two = split(core_ref[0], query_grad_ref[...])
    wait(copies)
    incoming_ref[...] = mm_t(one, matrix(to, 0, 48)) + mm_t(two, matrix(ts, 0, 48))


def triple_kernel(core_ref, united_ref, middle_grad_ref, query_grad_ref, pair_grad_ref, came_ref, incoming_ref, own_ref, other_ref, spots_ref, low_ref, vector_ref, kept_ref, gift_ref, to, ts, sems):
    core = core_ref[0]
    copies = load(
        [(own_ref.at[:, TRIPLE + 48 : TRIPLE + 144, :], to), (other_ref.at[:, TRIPLE + 48 : TRIPLE + 144, :], ts)], sems
    )
    scaled, inverse = norm_stats(united_ref[...])
    incoming = incoming_ref[...]
    wait(copies)
    for k in range(3):
        if k == 0:
            block = query_grad_ref[...]
        else:
            at = slice((k - 1) * D, k * D)
            block = (pair_grad_ref[:, at] + came_ref[:, at].astype(F32)).astype(BF)
        one, two = split(core, block)
        kept_ref[:, k * HALF : (k + 1) * HALF] = one
        gift_ref[:, k * HALF : (k + 1) * HALF] = two
        if k:
            incoming = incoming + mm_t(one, matrix(to, 48 * (k - 1), 48)) + mm_t(two, matrix(ts, 48 * (k - 1), 48))
    back_one, gain_grad, shift_grad = norm_backward(incoming, scaled, inverse, spots_ref[1:2, :])
    united_low = (middle_grad_ref[...] + back_one).astype(BF)
    low_ref[...] = united_low
    gift_ref[:, 3 * HALF :] = split(core, united_low)[1]
    vector_ref[0:1, :] = jnp.sum(united_low.astype(F32), axis=0, keepdims=True)
    vector_ref[1:2, :] = gain_grad
    vector_ref[2:3, :] = shift_grad
    vector_ref[3:8, :] = jnp.zeros((5, D), F32)


def skip_kernel(core_ref, low_ref, own_ref, other_ref, in_grad_ref, skip_grad_ref, so, ss, sems):
    copies = load(
        [(own_ref.at[:, SKIP : SKIP + 96, :], so), (other_ref.at[:, SKIP : SKIP + 96, :], ss)], sems
    )
    low_own, low_other = split(core_ref[0], low_ref[...])
    wait(copies)
    for half, grad_ref in ((0, in_grad_ref), (1, skip_grad_ref)):
        planes = slice(8 * half, 8 * half + 8)
        back = mm_t(low_own, so[planes, :, :].reshape(D, HALF)) + mm_t(low_other, ss[planes, :, :].reshape(D, HALF))
        grad_ref[...] = back[:TOKENS].astype(BF)


def late_kernel(place_ref, joined_ref, first_came_ref, normed_ref, normed_came_ref, low_ref, kept_ref, came_ref, early_ref, vector_ref, *refs):
    one_refs, two_refs, (go, gt, sems) = refs[:4], refs[4:8], refs[8:]
    for k in range(3):
        at = slice(k * HALF, (k + 1) * HALF)
        grad = t_mm(normed_ref[...], kept_ref[:, at]) + t_mm(normed_came_ref[...], came_ref[:, at])
        scatter(place_ref, gt, grad.astype(BF), 48 * k, True)
    sends = load([(gt.at[4 * k : 4 * k + 4], two_refs[k]) for k in range(4)], sems.at[:4])
    low, low_came = split(place_ref[0], low_ref[...])[0], came_ref[:, 3 * HALF :]
    grad = t_mm(joined_ref[:, : 2 * D], low) + t_mm(first_came_ref[:, : 2 * D], low_came)
    scatter(place_ref, go, grad.astype(BF), SKIP, False)
    rows = early_ref[...] + vector_rows([vector_ref[j : j + 1, :] for j in range(3)], (0, 6, 12))
    rows = jnp.concatenate([rows.reshape(PLANES, 8, 128), jnp.zeros((PLANES, 8, 128), F32)], axis=1)
    rows = jnp.concatenate([rows, jnp.zeros((PLANES, 16, HALF - 128), F32)], axis=2)
    scatter(place_ref, go, rows.reshape(PLANES * 16, HALF).astype(BF), 96, False)
    wait(sends)
    wait(load([(go.at[4 * k : 4 * k + 4], one_refs[k]) for k in range(4)], sems.at[4:]))


def column_kernel(one_ref, two_ref, early_ref, moves_ref, out_ref, rows_ref):
    rows_ref[:ONE_ROWS] = one_ref[...]
    rows_ref[ONE_ROWS : ONE_ROWS + TWO_ROWS] = two_ref[...]
    rows_ref[ONE_ROWS + TWO_ROWS :] = early_ref[...]
    out_ref[...] = mm(moves_ref[...], rows_ref[...]).astype(BF).reshape(4, 2 * PACK_ROWS, HALF)


def column_moves():
    moves = np.zeros((8 * PACK_ROWS, SUM_ROWS), np.float32)
    for high in range(2):
        for low in range(2):
            for core in range(2):
                at = ((2 * high + low) * 2 + core) * PACK_ROWS
                device = (2 * high + core) * 2 + low
                for rows, start in zip(PACK, SUM_STARTS):
                    for row in range(rows):
                        moves[at + row, start + device * rows + row] = 1.0
                    at += rows
    return moves


def call(kernel, name, args, outs, scratch, flops, room):
    place = {
        "s": pl.BlockSpec(memory_space=pltpu.SMEM),
        "v": pl.BlockSpec(memory_space=pltpu.VMEM),
        "a": pl.BlockSpec(memory_space=pl.ANY),
    }
    moved = sum(a.size * a.dtype.itemsize for a, _ in args)
    return pl.pallas_call(
        kernel,
        out_shape=[jax.ShapeDtypeStruct(shape, dtype) for shape, dtype, _ in outs],
        in_specs=[place[w] for _, w in args],
        out_specs=[place[w] for _, _, w in outs],
        scratch_shapes=scratch,
        compiler_params=pltpu.CompilerParams(vmem_limit_bytes=room * 2**20),
        cost_estimate=pl.CostEstimate(flops=int(flops), bytes_accessed=int(moved), transcendentals=0),
        name=name,
    )(*[a for a, _ in args])


def swap(block, axis):
    return lax.ppermute(block, axis, [(0, 1), (1, 0)])


def step(block, axis, steps):
    return lax.ppermute(block, axis, [((i + steps) % 4, i) for i in range(4)])


def sum_part(blocks, first, second):
    line = blocks[0].astype(F32)
    for k in (1, 2, 3):
        line = line + step(blocks[k], first, 4 - k).astype(F32)
    total = line[0]
    for k in (1, 2, 3):
        total = total + step(line[k].astype(BF), second, 4 - k).astype(F32)
    return total.astype(BF)


def regroup(block, pack):
    at, parts = 0, []
    for rows in pack:
        parts.append(block[:, at : at + rows].reshape(-1, HALF))
        at += rows
    return parts


def pick_table(indices, table):
    match = indices[:, None] == jnp.arange(table.shape[0], dtype=jnp.int32)[None, :]
    return jnp.sum(jnp.where(match, table[None, :], 0.0), axis=1)


def per_device(
    inputs,
    skipped,
    cotangent,
    timestep,
    class_ids,
    time_weight,
    class_weight,
    skip_weight,
    skip_bias,
    first_gain,
    first_shift,
    triple_weight,
    merge_weight,
    merge_bias,
    second_gain,
    second_shift,
    expand_weight,
    expand_bias,
    contract_weight,
    contract_bias,
):
    core_index = lax.axis_index("c").astype(jnp.int32)
    core = core_index[None]
    place = jnp.stack([core_index, lax.axis_index("y").astype(jnp.int32), lax.axis_index("x").astype(jnp.int32)])


    inputs, skipped, cotangent = (a.reshape(TOKENS, D) for a in (inputs, skipped, cotangent))
    sem = pltpu.SemaphoreType.DMA
    weight = lambda rows: pltpu.VMEM((PLANES, rows, HALF), BF)
    tokens = lambda width, dtype=BF, where="v": ((PAD, width), dtype, where)
    plane = lambda rows: ((PLANES, rows, HALF), BF, "a")

    vectors = (skip_bias, first_gain, first_shift, merge_bias, second_gain, second_shift, contract_bias, expand_bias)
    row, at = jnp.zeros((HALF,), F32), 0
    for vector in vectors:
        row = row + jnp.pad(vector.astype(F32), (at, HALF - at - vector.shape[0]))
        at += vector.shape[0]
    flat = dict(
        skip=skip_weight, triple=triple_weight, merge=merge_weight, expand=expand_weight, contract=contract_weight
    )
    flat = {name: a.reshape(-1, 128) for name, a in flat.items()}

    (packed,) = call(
        pack_kernel,
        "pack",
        [(flat[n], "a") for n in NAMES] + [(row[None], "v")],
        [((8, PACK_ROWS, HALF), BF, "v")],
        [pltpu.VMEM((2, PACK_ROWS, HALF), F32)]
        + [pltpu.VMEM(flat[n].shape, dtype) for dtype in (BF, F32) for n in NAMES]
        + [sem((len(NAMES),))],
        1e6,
        58,
    )
    column = regroup(lax.all_to_all(packed, COLUMN, 0, 0, tiled=True), PACK)
    first = jnp.concatenate(column[:2] + [jnp.zeros((8, HALF), BF)] + column[2:5], axis=0)
    second = jnp.concatenate(column[5:], axis=0)
    second_own = lax.all_gather(second, PLANE, axis=0, tiled=True).reshape(PLANES, SECOND_ROWS, HALF)
    first_own = lax.all_to_all(
        jnp.broadcast_to(first[None], (PLANES, FIRST_ROWS, HALF)), PLANE, 0, 0, tiled=True
    )
    first_own, timestep = lax.optimization_barrier((first_own, timestep))
    scale = pick_table(timestep, time_weight) * pick_table(class_ids, class_weight)
    first_other = swap(first_own, "c")
    after, gift = call(
        prepare_kernel,
        "prepare",
        [(core, "s"), (scale, "s"), (inputs, "v"), (skipped, "v"), (cotangent, "v")],
        [tokens(D), tokens(2 * D + HALF)],
        [],
        1e6,
        8,
    )
    gift_came = swap(gift, "c")

    (spots,) = call(
        spots_kernel, "vectors", [(first_own, "a")], [((16, D), F32, "v")], [weight(16), sem((1,))], 2e8, 8
    )
    united, normed, query, pair = call(
        first_kernel,
        "skip_and_triple",
        [(core, "s"), (gift, "v"), (first_own, "a"), (first_other, "a"), (spots, "v")],
        [tokens(D, F32), tokens(D), tokens(D), tokens(2 * D)],
        [weight(96), weight(96), weight(144), weight(144), sem((4,))],
        2 * PAD * D * (2 * D + 3 * D),
        16,
    )
    pair_came = swap(pair, "l")
    second_own, pair_came = lax.optimization_barrier((second_own, pair_came))
    second_other = swap(second_own, "c")
    normed_came = swap(normed, "c")
    mixed, totals = call(
        attend_kernel,
        "attention",
        [(query, "v"), (pair, "v"), (pair_came, "v")],
        [tokens(D), tokens(128, F32)],
        [],
        2 * PAD * D * 2 * KEYS,
        58,
    )
    mixed_came = swap(mixed, "c")
    output, middle_grad, early_vectors, forward_gift, forward_kept = call(
        forward_kernel,
        "feed_forward",
        [
            (core, "s"),
            (scale, "s"),
            (mixed, "v"),
            (united, "v"),
            (cotangent, "v"),
            (after, "v"),
            (second_own, "a"),
            (second_other, "a"),
            (spots, "v"),
        ],
        [((TOKENS, D), BF, "v"), tokens(D, F32), ((16, D), F32, "v"), tokens(GIFT), tokens(FF // 2)],
        [weight(192)] * 4
        + [weight(48)] * 2
        + [pltpu.VMEM((PAD, FF), F32), pltpu.VMEM((PAD, FF), BF), sem((12,))],
        2 * PAD * D * FF * 4,
        58,
    )
    forward_came = swap(forward_gift, "c")
    query_grad, pair_grad, pair_sent = call(
        backward_kernel,
        "attention_backward",
        [
            (core, "s"),
            (middle_grad, "v"),
            (query, "v"),
            (pair, "v"),
            (pair_came, "v"),
            (totals, "v"),
            (second_own, "a"),
            (second_other, "a"),
        ],
        [tokens(D), tokens(2 * D, F32), tokens(2 * D)],
        [pltpu.VMEM((PAD, D), BF), weight(48), weight(48), sem((2,))],
        2 * PAD * D * (D + 5 * KEYS),
        58,
    )
    grad_came = swap(pair_sent, "l")
    (early_grads,) = call(
        early_kernel,
        "early_gradients",
        [
            (core, "s"),
            (forward_gift, "a"),
            (forward_came, "a"),
            (forward_kept, "a"),
            (after, "v"),
            (gift_came, "v"),
            (mixed, "v"),
            (mixed_came, "v"),
            (middle_grad, "v"),
        ],
        [plane(EARLY_ROWS)],
        [pltpu.VMEM((PAD, GIFT), BF)] * 2
        + [pltpu.VMEM((PAD, FF // 2), BF), weight(EARLY_ROWS), sem((5,)), sem((6,))],
        2 * PAD * D * FF * 2,
        58,
    )
    early_sum = lax.psum_scatter(early_grads.reshape(PLANES * EARLY_ROWS, HALF), PLANE, scatter_dimension=0, tiled=True)
    early_vectors, query_grad = lax.optimization_barrier((early_vectors, query_grad))
    query_incoming, early_rows = call(
        query_kernel,
        "query_backward",
        [(core, "s"), (query_grad, "v"), (early_vectors, "v"), (first_own, "a"), (first_other, "a")],
        [tokens(D, F32), ((128, 128), F32, "v")],
        [weight(48)] * 2 + [sem((2,))],
        2 * PAD * D * D,
        12,
    )
    united_low, late_vectors, triple_kept, late_gift = call(
        triple_kernel,
        "triple_backward",
        [
            (core, "s"),
            (united, "v"),
            (middle_grad, "v"),
            (query_grad, "v"),
            (pair_grad, "v"),
            (grad_came, "v"),
            (query_incoming, "v"),
            (first_own, "a"),
            (first_other, "a"),
            (spots, "v"),
        ],
        [tokens(D), ((8, D), F32, "v"), tokens(3 * HALF), tokens(4 * HALF)],
        [weight(96)] * 2 + [sem((2,))],
        2 * PAD * D * (2 * D),
        16,
    )
    late_came = swap(late_gift, "c")
    input_grad, skip_grad = call(
        skip_kernel,
        "skip_backward",
        [(core, "s"), (united_low, "v"), (first_own, "a"), (first_other, "a")],
        [((TOKENS, D), BF, "v"), ((TOKENS, D), BF, "v")],
        [weight(96), weight(96), sem((2,))],
        2 * PAD * D * (2 * D),
        12,
    )
    late_came, input_grad, skip_grad = lax.optimization_barrier((late_came, input_grad, skip_grad))
    late = call(
        late_kernel,
        "late_gradients",
        [
            (place, "s"),
            (gift, "v"),
            (gift_came, "v"),
            (normed, "v"),
            (normed_came, "v"),
            (united_low, "v"),
            (triple_kept, "v"),
            (late_came, "v"),
            (early_rows, "v"),
            (late_vectors, "v"),
        ],
        [((4, ONE_ROWS, HALF), BF, "a")] * 4 + [((4, TWO_ROWS, HALF), BF, "a")] * 4,
        [weight(ONE_ROWS), weight(TWO_ROWS), sem((8,))],
        2 * PAD * D * (5 * D),
        58,
    )
    one_sum, two_sum = sum_part(late[:4], "x", "y"), sum_part(late[4:], "y", "x")

    (column,) = call(
        column_kernel,
        "by_device",
        [(one_sum, "v"), (two_sum, "v"), (early_sum, "v"), (jnp.asarray(column_moves(), BF), "v")],
        [((4, 2 * PACK_ROWS, HALF), BF, "v")],
        [pltpu.VMEM((SUM_ROWS, HALF), BF)],
        2 * SUM_ROWS * SUM_ROWS * HALF,
        12,
    )
    total = jnp.sum(lax.all_to_all(column, ("h", "l"), 0, 0, tiled=True).astype(F32), axis=0)
    mine, sent = order(core_index, total[:PACK_ROWS], total[PACK_ROWS:])
    low, high = order(core_index, mine, swap(sent, "c"))
    rows_of = lambda name: ((flat[name].shape[0], 128), F32, "v")
    skip_out, triple_out, expand_out, contract_out, merge_out, vector_out = call(
        unpack_kernel,
        "by_weight",
        [(low, "v"), (high, "v")],
        [rows_of(name) for name in NAMES] + [((1, 128), F32, "v")],
        [],
        1e6,
        8,
    )
    vector_out = vector_out[0]
    spot = lambda j: vector_out[6 * j : 6 * j + 6]
    return (
        output[None],
        input_grad[None],
        skip_grad[None],
        skip_out.reshape(-1),
        spot(0),
        spot(1),
        spot(2),
        triple_out.reshape(-1),
        merge_out.reshape(-1),
        spot(3),
        spot(4),
        spot(5),
        expand_out.reshape(-1),
        vector_out[42:66],
        contract_out.reshape(-1),
        spot(6),
    )


def solution(mesh):
    fine = jax.sharding.Mesh(mesh.devices.reshape(4, 4, 2, 2, 2), ("y", "x", "h", "c", "l"))
    images = ("y", "x", "h", "c")
    everything = images + ("l",)
    tokens, shard = P(images, "l", None), P(everything)
    return jax.shard_map(
        per_device,
        mesh=fine,
        in_specs=(tokens,) * 3 + (P(images),) * 2 + (P(),) * 2 + (shard,) * 13,
        out_specs=(tokens,) * 3 + (shard,) * 13,
        check_vma=False,
    )
```

```python
import functools
import math

import jax
import jax.numpy as jnp
import numpy as np
from jax import lax
from jax.experimental import pallas as pl
from jax.experimental.pallas import tpu as pltpu
from jax.sharding import PartitionSpec as P

D = 768
HEADS = 12
HEAD_DIM = 64
FF = 3072
HALF = D // 2
STRIPS = FF // D
TOKENS = 129
PAD = 144
KEYS = 2 * PAD
PLANES = 16
PLANE = ("y", "x")
COLUMN = ("h", "c", "l")
SKIP, SPOTS, TRIPLE = 0, 96, 112
EXPAND, CONTRACT, MERGE = 0, 192, 384
FIRST_ROWS, SECOND_ROWS = 256, 432
ONE_ROWS = 112
TWO_SHARE, TWO_GROUP = 3 * D // 4, 48
EARLY_ROWS = 448
FIRST_PACK, SECOND_PACK = (12, 1, 6, 6, 6), (6, 6, 6, 6, 24, 6)
PACK = FIRST_PACK + SECOND_PACK
PACK_ROWS = 88
NAMES = ("skip", "triple", "expand", "contract", "merge")
SUM_ROWS = ONE_ROWS + EARLY_ROWS
SUM_STARTS = (0, 96, None, None, None) + tuple(ONE_ROWS + at for at in (0, 48, 96, 144, 192, 384))
epsilon = 1e-05
score_scale = 1.0 / math.sqrt(HEAD_DIM)
BF, F32 = jnp.bfloat16, jnp.float32
ATTEND = FF + FF // 2
NORMED = ATTEND + HALF
GIFT = NORMED + D


def mm(left, right):
    return jnp.dot(left, right, preferred_element_type=F32)


def mm_t(left, right):
    return lax.dot_general(left, right, (((1,), (1,)), ((), ())), preferred_element_type=F32)


def t_mm(left, right):
    return lax.dot_general(left, right, (((0,), (0,)), ((), ())), preferred_element_type=F32)


def order(core, one, two):
    return jnp.where(core == 0, one, two), jnp.where(core == 0, two, one)


def split(core, block):
    return order(core, block[:, :HALF], block[:, HALF:])


def norm_stats(values):
    mean_value = jnp.mean(values, axis=-1, keepdims=True)
    centered = values - mean_value
    variance = jnp.mean(centered * centered, axis=-1, keepdims=True)
    inverse = lax.rsqrt(variance + epsilon)
    return centered * inverse, inverse


def norm_backward(incoming, scaled, inverse, gain):
    weighted = incoming * gain
    first_mean = jnp.mean(weighted, axis=-1, keepdims=True)
    second_mean = jnp.mean(weighted * scaled, axis=-1, keepdims=True)
    value_grad = inverse * (weighted - first_mean - scaled * second_mean)
    return (
        value_grad,
        jnp.sum(incoming * scaled, axis=0, keepdims=True),
        jnp.sum(incoming, axis=0, keepdims=True),
    )


def padded(block):
    return jnp.concatenate([block, jnp.zeros((PAD - TOKENS, block.shape[1]), block.dtype)], axis=0)


def load(pairs, sems):
    copies = [pltpu.make_async_copy(s, d, sems.at[k]) for k, (s, d) in enumerate(pairs)]
    for copy in copies:
        copy.start()
    return copies


def matrix(ref, at, rows):
    return ref[:, at : at + rows, :].reshape(PLANES * rows, HALF)


def spot_masks(width):
    lanes = lax.broadcasted_iota(jnp.int32, (128, D), 0)
    spots = lax.broadcasted_iota(jnp.int32, (128, D), 1)
    return lanes, lax.rem(spots, width), lax.div(spots, width)


def steps_to(place_ref, plane):
    return (plane // 4 - place_ref[1]) & 3, (plane % 4 - place_ref[2]) & 3


def wait(copies):
    for copy in copies:
        copy.wait()


def tiles_of(matrix_name):
    count, strips, across = {"skip": (6, 1, 6), "triple": (18, 1, 6), "merge": (6, 1, 6), "expand": (24, STRIPS, 24), "contract": (6, 1, 6)}[matrix_name]
    for tile in range(count):
        block, inside = divmod(tile, across)
        half, rest = divmod(inside, across // 2)
        yield tile, half, block + rest // 3, rest % 3


def pack_kernel(*refs):
    count = len(NAMES)
    sources, (row_ref, out_ref, rows_ref), scratch = refs[:count], refs[count : count + 3], refs[count + 3 :]
    low, scratch, sems = scratch[:count], scratch[count : 2 * count], scratch[2 * count]
    copies = load(list(zip(sources, low)), sems)
    at = 0
    for name, held, ref, copy in zip(NAMES, scratch, low, copies):
        copy.wait()
        held[...] = ref[...].astype(F32)
        tiles = list(tiles_of(name))
        rows = held.shape[0] // len(tiles)
        for tile, half, strip, spot in tiles:
            first = at + strip * rows
            rows_ref[half, first : first + rows, 128 * spot : 128 * spot + 128] = held[pl.ds(tile, rows, stride=len(tiles)), :]
        at += rows * (1 + max(t[2] for t in tiles))
        if name == "skip":
            rows_ref[0, at : at + 1, :] = row_ref[...]
            rows_ref[1, at : at + 1, :] = row_ref[...]
            at += 1
    rows_ref[:, at:PACK_ROWS, :] = jnp.zeros((2, PACK_ROWS - at, HALF), F32)
    for half in range(2):
        packed = rows_ref[half].astype(BF)
        for device in range(8):
            if device // 2 % 2 == half:
                out_ref[device] = packed


def unpack_kernel(low_ref, high_ref, *refs):
    outs = dict(zip(NAMES, refs))
    at = 0
    for name in NAMES:
        tiles = list(tiles_of(name))
        rows = outs[name].shape[0] // len(tiles)
        for tile, half, strip, spot in tiles:
            first = at + strip * rows
            source = high_ref if half else low_ref
            outs[name][pl.ds(tile, rows, stride=len(tiles)), :] = source[first : first + rows, 128 * spot : 128 * spot + 128]
        at += rows * (1 + max(t[2] for t in tiles))
        if name == "skip":
            refs[5][...] = low_ref[at : at + 1, :128] + high_ref[at : at + 1, :128]
            at += 1


def prepare_kernel(core_ref, scale_ref, in_ref, skip_ref, cotangent_ref, after_ref, gift_ref):
    gift_ref[:, :D] = padded(in_ref[...])
    gift_ref[:, D : 2 * D] = padded(skip_ref[...])
    after = padded(cotangent_ref[...].astype(F32) * scale_ref[0]).astype(BF)
    after_ref[...] = after
    gift_ref[:, 2 * D :] = split(core_ref[0], after)[1]


def spots_kernel(first_ref, out_ref, rows_ref, sems):
    wait(load([(first_ref.at[:, SPOTS : SPOTS + 16, :], rows_ref)], sems))
    held = rows_ref[:, :, :128].astype(F32)[:, :8].reshape(128, 128).astype(BF)
    for j in range(7):
        lanes, place, owner = spot_masks(6)
        one_hot = (lanes - 6 * j == place).astype(BF)
        spread = jnp.where(owner == lanes, mm(held, one_hot), 0.0)
        out_ref[j : j + 1, :] = jnp.sum(spread, axis=0, keepdims=True)
    out_ref[7:8, :] = jnp.zeros((1, D), F32)
    lanes, place, owner = spot_masks(24)
    spread = mm(held, (lanes - 42 == place).astype(BF))
    for m in range(STRIPS):
        out_ref[8 + m : 9 + m, :] = jnp.sum(jnp.where(owner + 32 * m == lanes, spread, 0.0), axis=0, keepdims=True)
    out_ref[12:16, :] = jnp.zeros((4, D), F32)


def first_kernel(core_ref, joined_ref, own_ref, other_ref, spots_ref, united_ref, normed_ref, query_ref, pair_ref, so, ss, to, ts, sems):
    core = core_ref[0]
    copies = load(
        [
            (own_ref.at[:, SKIP : SKIP + 96, :], so),
            (other_ref.at[:, SKIP : SKIP + 96, :], ss),
            (own_ref.at[:, TRIPLE : TRIPLE + 144, :], to),
            (other_ref.at[:, TRIPLE : TRIPLE + 144, :], ts),
        ],
        sems,
    )
    joined = joined_ref[:, : 2 * D]
    copies[0].wait()
    one = mm(joined, matrix(so, 0, 96))
    copies[1].wait()
    two = mm(joined, matrix(ss, 0, 96))
    united = jnp.concatenate(order(core, one, two), axis=1) + spots_ref[0:1, :]
    united_ref[...] = united
    scaled, _ = norm_stats(united)
    normed = (scaled * spots_ref[1:2, :] + spots_ref[2:3, :]).astype(BF)
    normed_ref[...] = normed
    copies[2].wait()
    copies[3].wait()
    for k in range(3):
        one = mm(normed, matrix(to, 48 * k, 48))
        two = mm(normed, matrix(ts, 48 * k, 48))
        block = jnp.concatenate(order(core, one, two), axis=1).astype(BF)
        if k == 0:
            query_ref[...] = block
        else:
            pair_ref[:, (k - 1) * D : k * D] = block


def key_mask():
    spots = lax.broadcasted_iota(jnp.int32, (1, KEYS), 1)
    return (spots < TOKENS) | ((spots >= PAD) & (spots < PAD + TOKENS))


def attend_kernel(query_ref, pair_ref, came_ref, mixed_ref, total_ref):
    mask = key_mask()
    total_ref[...] = jnp.zeros((PAD, 128), F32)
    for pair in range(HEADS // 2):
        at = slice(128 * pair, 128 * pair + 128)
        late = slice(D + 128 * pair, D + 128 * pair + 128)
        query = query_ref[:, at]
        keys = jnp.concatenate([pair_ref[:, at], came_ref[:, at]], axis=0)
        values = jnp.concatenate([pair_ref[:, late], came_ref[:, late]], axis=0)
        done = []
        for side in range(2):
            head = slice(HEAD_DIM * side, HEAD_DIM * side + HEAD_DIM)
            scores = mm_t(query[:, head], keys[:, head]) * score_scale
            scores = jnp.where(mask, scores, -1e30)
            largest = jnp.max(scores, axis=-1, keepdims=True)
            powered = jnp.exp(scores - largest)
            totals = jnp.sum(powered, axis=-1, keepdims=True)
            total_ref[:, 2 * pair + side : 2 * pair + side + 1] = largest + jnp.log(totals)
            soft_low = (powered / totals).astype(BF)
            done.append(mm(soft_low, values[:, head]))
        mixed_ref[:, at] = jnp.concatenate(done, axis=1).astype(BF)


def forward_kernel(core_ref, scale_ref, mixed_ref, united_ref, cotangent_ref, after_ref, own_ref, other_ref, spots_ref, out_ref, middle_grad_ref, vector_ref, gift_ref, kept_ref, eo, es, co, cs, mo, ms, slope_ref, low_ref, sems):
    core = core_ref[0]
    copies = load(
        [
            (own_ref.at[:, MERGE : MERGE + 48, :], mo),
            (other_ref.at[:, MERGE : MERGE + 48, :], ms),
            *[
                (ref.at[:, 48 * k : 48 * k + 48, :], to.at[:, 48 * k : 48 * k + 48, :])
                for k in range(STRIPS)
                for ref, to in ((own_ref, eo), (other_ref, es))
            ],
            (own_ref.at[:, CONTRACT : CONTRACT + 192, :], co),
            (other_ref.at[:, CONTRACT : CONTRACT + 192, :], cs),
        ],
        sems,
    )
    after = after_ref[...]
    vector_ref[...] = jnp.zeros((16, D), F32)
    vector_ref[6:7, :] = jnp.sum(after.astype(F32), axis=0, keepdims=True)
    after_own, after_other = split(core, after)
    mixed = mixed_ref[...]
    wait(copies[:2])
    one, two = mm(mixed, matrix(mo, 0, 48)), mm(mixed, matrix(ms, 0, 48))
    middle = united_ref[...] + jnp.concatenate(order(core, one, two), axis=1) + spots_ref[3:4, :]
    scaled, inverse = norm_stats(middle)
    normed = (scaled * spots_ref[4:5, :] + spots_ref[5:6, :]).astype(BF)
    gift_ref[:, NORMED:] = normed
    for k in range(STRIPS):
        wait(copies[2 + 2 * k : 4 + 2 * k])
        one, two = order(core, mm(normed, matrix(eo, 48 * k, 48)), mm(normed, matrix(es, 48 * k, 48)))
        for side, block in ((0, one), (1, two)):
            at = side * STRIPS * HALF + k * HALF
            bias = spots_ref[8 + at // D : 9 + at // D, at % D : at % D + HALF]
            block = block + bias
            cumulative = 0.5 * (1.0 + lax.erf(block * (1.0 / math.sqrt(2.0))))
            density = jnp.exp(-0.5 * block * block) * (1.0 / math.sqrt(2.0 * math.pi))
            gift_ref[:, at : at + HALF] = (block * cumulative).astype(BF)
            slope_ref[:, at : at + HALF] = cumulative + block * density
    wait(copies[2 + 2 * STRIPS :])
    active = gift_ref[:, :FF]
    one, two = mm(active, matrix(co, 0, 192)), mm(active, matrix(cs, 0, 192))
    output = middle + jnp.concatenate(order(core, one, two), axis=1) + spots_ref[6:7, :]
    out_ref[...] = output[:TOKENS].astype(BF)
    for j in range(2 * STRIPS):
        at, planes = slice(HALF * j, HALF * j + HALF), slice(2 * j, 2 * j + 2)
        back = mm_t(after_own, co[planes, :, :].reshape(HALF, HALF)) + mm_t(after_other, cs[planes, :, :].reshape(HALF, HALF))
        low = (back * slope_ref[:, at]).astype(BF)
        low_ref[:, at] = low
        row = 8 + j // 2
        vector_ref[row : row + 1, HALF * (j % 2) : HALF * (j % 2) + HALF] = jnp.sum(low.astype(F32), axis=0, keepdims=True)
    incoming = jnp.zeros((PAD, D), F32)
    for k in range(STRIPS):
        one, two = order(
            core,
            low_ref[:, k * HALF : (k + 1) * HALF],
            low_ref[:, (STRIPS + k) * HALF : (STRIPS + k + 1) * HALF],
        )
        kept_ref[:, k * HALF : (k + 1) * HALF] = one
        gift_ref[:, FF + k * HALF : FF + (k + 1) * HALF] = two
        incoming = incoming + mm_t(one, matrix(eo, 48 * k, 48)) + mm_t(two, matrix(es, 48 * k, 48))
    back_two, gain_grad, shift_grad = norm_backward(incoming, scaled, inverse, spots_ref[4:5, :])
    vector_ref[4:5, :] = gain_grad
    vector_ref[5:6, :] = shift_grad
    middle_grad = padded(cotangent_ref[...].astype(F32) * scale_ref[0]) + back_two
    middle_grad_ref[...] = middle_grad
    attend = middle_grad.astype(BF)
    vector_ref[3:4, :] = jnp.sum(attend.astype(F32), axis=0, keepdims=True)
    gift_ref[:, ATTEND:NORMED] = split(core, attend)[1]


def early_kernel(core_ref, gift_any, came_any, kept_any, after_ref, first_came_any, mixed_any, mixed_came_any, middle_grad_any, grad_ref, gift_ref, came_ref, kept_ref, after_came_ref, mixed_ref, mixed_came_ref, middle_grad_ref, go, sems, out_sems):
    core = core_ref[0]
    copies = load(
        [
            (gift_any.at[:, :FF], gift_ref.at[:, :FF]),
            (came_any.at[:, :FF], came_ref.at[:, :FF]),
            (first_came_any.at[:, 2 * D :], after_came_ref),
            (gift_any.at[:, NORMED:], gift_ref.at[:, NORMED:]),
            (came_any.at[:, FF:], came_ref.at[:, FF:]),
            (kept_any, kept_ref),
            (mixed_any, mixed_ref),
            (mixed_came_any, mixed_came_ref),
            (middle_grad_any, middle_grad_ref),
        ],
        sems,
    )
    wait(copies[:3])
    after, after_came = split(core, after_ref[...])[0], after_came_ref[...]
    for j in range(2 * STRIPS):
        at, planes = slice(HALF * j, HALF * j + HALF), slice(2 * j, 2 * j + 2)
        grad = t_mm(gift_ref[:, at], after) + t_mm(came_ref[:, at], after_came)
        go[planes, CONTRACT : CONTRACT + 192, :] = grad.astype(BF).reshape(2, 192, HALF)
    rows = lambda at, to: (go.at[:, at:to, :], grad_ref.at[:, at:to, :])
    sends = load([rows(CONTRACT, CONTRACT + 192)], out_sems)
    wait(copies[3:])
    attend = split(core, middle_grad_ref[...].astype(BF))[0]
    grad = t_mm(mixed_ref[...], attend) + t_mm(mixed_came_ref[...], came_ref[:, ATTEND:NORMED])
    go[:, MERGE : MERGE + 48, :] = grad.astype(BF).reshape(PLANES, 48, HALF)
    go[:, MERGE + 48 :, :] = jnp.zeros((PLANES, EARLY_ROWS - MERGE - 48, HALF), BF)
    sends += load([rows(MERGE, EARLY_ROWS)], out_sems.at[1:])
    normed, normed_came = gift_ref[:, NORMED:], came_ref[:, NORMED:]
    for k in range(STRIPS):
        grad = t_mm(normed, kept_ref[:, k * HALF : (k + 1) * HALF]) + t_mm(
            normed_came, came_ref[:, FF + k * HALF : FF + (k + 1) * HALF]
        )
        go[:, EXPAND + 48 * k : EXPAND + 48 * (k + 1), :] = grad.astype(BF).reshape(PLANES, 48, HALF)
        sends += load([rows(EXPAND + 48 * k, EXPAND + 48 * (k + 1))], out_sems.at[2 + k :])
    wait(sends)


def backward_kernel(core_ref, middle_grad_ref, query_ref, pair_ref, came_ref, total_ref, own_ref, other_ref, query_grad_ref, pair_grad_ref, sent_ref, mixed_grad_ref, mo, ms, sems):
    core = core_ref[0]
    copies = load(
        [(own_ref.at[:, MERGE : MERGE + 48, :], mo), (other_ref.at[:, MERGE : MERGE + 48, :], ms)], sems
    )
    attend_own, attend_other = split(core, middle_grad_ref[...].astype(BF))
    mask = key_mask()
    copies[0].wait()
    copies[1].wait()
    mixed_grad_ref[...] = (mm_t(attend_own, matrix(mo, 0, 48)) + mm_t(attend_other, matrix(ms, 0, 48))).astype(BF)
    for pair in range(HEADS // 2):
        at = slice(128 * pair, 128 * pair + 128)
        late = slice(D + 128 * pair, D + 128 * pair + 128)
        query, mixed_grad = query_ref[:, at], mixed_grad_ref[:, at]
        keys = jnp.concatenate([pair_ref[:, at], came_ref[:, at]], axis=0)
        values = jnp.concatenate([pair_ref[:, late], came_ref[:, late]], axis=0)
        query_parts, key_parts, value_parts = [], [], []
        for side in range(2):
            head = slice(HEAD_DIM * side, HEAD_DIM * side + HEAD_DIM)
            scores = mm_t(query[:, head], keys[:, head]) * score_scale
            scores = jnp.where(mask, scores, -1e30)
            soft = jnp.exp(scores - total_ref[:, 2 * pair + side : 2 * pair + side + 1])
            soft_grad = mm_t(mixed_grad[:, head], values[:, head])
            inner = jnp.sum(soft * soft_grad, axis=-1, keepdims=True)
            scores_grad = (soft * (soft_grad - inner)).astype(BF)
            query_parts.append(mm(scores_grad, keys[:, head]))
            key_parts.append(t_mm(scores_grad, query[:, head]))
            value_parts.append(t_mm(soft.astype(BF), mixed_grad[:, head]))
        query_grad_ref[:, at] = (jnp.concatenate(query_parts, axis=1) * score_scale).astype(BF)
        key_grad = jnp.concatenate(key_parts, axis=1) * score_scale
        value_grad = jnp.concatenate(value_parts, axis=1)
        pair_grad_ref[:, at] = key_grad[:PAD]
        pair_grad_ref[:, late] = value_grad[:PAD]
        sent_ref[:, at] = key_grad[PAD:].astype(BF)
        sent_ref[:, late] = value_grad[PAD:].astype(BF)


def scatter(place_ref, ref, block, at, by_y):
    rows = block.shape[0] // PLANES
    for plane in range(PLANES):
        step_y, step_x = steps_to(place_ref, plane)
        spot = 4 * step_y + step_x if by_y else 4 * step_x + step_y
        ref[spot, at : at + rows, :] = block[plane * rows : (plane + 1) * rows]


def vector_rows(vectors, places):
    rows = jnp.zeros((128, 128), F32)
    for vector, at in zip(vectors, places):
        lanes, place, owner = spot_masks(6)
        spread = jnp.where(owner == lanes, vector, 0.0).astype(BF)
        rows = rows + mm_t(spread, (lanes - at == place).astype(BF))
    return rows


def query_kernel(core_ref, query_grad_ref, early_ref, normed_ref, normed_came_ref, by_z_ref, own_ref, other_ref, incoming_ref, rows_ref, moved_ref, moved_came_ref, to, ts, sems):
    copies = load(
        [(own_ref.at[:, TRIPLE : TRIPLE + 48, :], to), (other_ref.at[:, TRIPLE : TRIPLE + 48, :], ts)], sems
    )
    rows = vector_rows([early_ref[j : j + 1, :] for j in range(3, 7)], (18, 24, 30, 36))
    lanes, place, owner = spot_masks(24)
    for m in range(STRIPS):
        spread = jnp.where(owner + 32 * m == lanes, early_ref[8 + m : 9 + m, :], 0.0).astype(BF)
        rows = rows + mm_t(spread, (lanes - 42 == place).astype(BF))
    rows_ref[...] = rows
    one, two = split(core_ref[0], query_grad_ref[...])
    wait(copies)
    incoming_ref[...] = mm_t(one, matrix(to, 0, 48)) + mm_t(two, matrix(ts, 0, 48))
    moved_ref[...] = mm(normed_ref[...], by_z_ref[...]).astype(BF)
    moved_came_ref[...] = mm(normed_came_ref[...], by_z_ref[...]).astype(BF)


def triple_kernel(core_ref, united_ref, middle_grad_ref, query_grad_ref, pair_grad_ref, came_ref, incoming_ref, own_ref, other_ref, spots_ref, low_ref, vector_ref, kept_ref, gift_ref, to, ts, sems):
    core = core_ref[0]
    copies = load(
        [(own_ref.at[:, TRIPLE + 48 : TRIPLE + 144, :], to), (other_ref.at[:, TRIPLE + 48 : TRIPLE + 144, :], ts)], sems
    )
    scaled, inverse = norm_stats(united_ref[...])
    incoming = incoming_ref[...]
    wait(copies)
    for k in range(3):
        if k == 0:
            block = query_grad_ref[...]
        else:
            at = slice((k - 1) * D, k * D)
            block = (pair_grad_ref[:, at] + came_ref[:, at].astype(F32)).astype(BF)
        one, two = split(core, block)
        kept_ref[:, k * HALF : (k + 1) * HALF] = one
        gift_ref[:, k * HALF : (k + 1) * HALF] = two
        if k:
            incoming = incoming + mm_t(one, matrix(to, 48 * (k - 1), 48)) + mm_t(two, matrix(ts, 48 * (k - 1), 48))
    back_one, gain_grad, shift_grad = norm_backward(incoming, scaled, inverse, spots_ref[1:2, :])
    united_low = (middle_grad_ref[...] + back_one).astype(BF)
    low_ref[...] = united_low
    gift_ref[:, 3 * HALF :] = split(core, united_low)[1]
    vector_ref[0:1, :] = jnp.sum(united_low.astype(F32), axis=0, keepdims=True)
    vector_ref[1:2, :] = gain_grad
    vector_ref[2:3, :] = shift_grad
    vector_ref[3:8, :] = jnp.zeros((5, D), F32)


def skip_kernel(core_ref, low_ref, own_ref, other_ref, in_grad_ref, skip_grad_ref, so, ss, sems):
    copies = load(
        [(own_ref.at[:, SKIP : SKIP + 96, :], so), (other_ref.at[:, SKIP : SKIP + 96, :], ss)], sems
    )
    low_own, low_other = split(core_ref[0], low_ref[...])
    wait(copies)
    for half, grad_ref in ((0, in_grad_ref), (1, skip_grad_ref)):
        planes = slice(8 * half, 8 * half + 8)
        back = mm_t(low_own, so[planes, :, :].reshape(D, HALF)) + mm_t(low_other, ss[planes, :, :].reshape(D, HALF))
        grad_ref[...] = back[:TOKENS].astype(BF)


def late_kernel(place_ref, joined_ref, first_came_ref, normed_ref, normed_came_ref, low_ref, kept_ref, came_ref, early_ref, vector_ref, *refs):
    one_refs, two_refs, (go, gt, sems) = refs[:4], refs[4:8], refs[8:]
    for k in range(3):
        at = slice(k * HALF, (k + 1) * HALF)
        grad = (t_mm(normed_ref[...], kept_ref[:, at]) + t_mm(normed_came_ref[...], came_ref[:, at])).astype(BF)
        for z in range(4):
            gt[(z - place_ref[3]) & 3, 192 * k : 192 * k + 192, :] = grad[192 * z : 192 * z + 192]
    sends = load([(gt.at[k], two_refs[k]) for k in range(4)], sems.at[:4])
    low, low_came = split(place_ref[0], low_ref[...])[0], came_ref[:, 3 * HALF :]
    grad = t_mm(joined_ref[:, : 2 * D], low) + t_mm(first_came_ref[:, : 2 * D], low_came)
    scatter(place_ref, go, grad.astype(BF), SKIP, False)
    rows = early_ref[...] + vector_rows([vector_ref[j : j + 1, :] for j in range(3)], (0, 6, 12))
    rows = jnp.concatenate([rows.reshape(PLANES, 8, 128), jnp.zeros((PLANES, 8, 128), F32)], axis=1)
    rows = jnp.concatenate([rows, jnp.zeros((PLANES, 16, HALF - 128), F32)], axis=2)
    scatter(place_ref, go, rows.reshape(PLANES * 16, HALF).astype(BF), 96, False)
    wait(sends)
    wait(load([(go.at[4 * k : 4 * k + 4], one_refs[k]) for k in range(4)], sems.at[4:]))


def group_kernel(place_ref, share_ref, moves_ref, *refs):
    outs, rows_ref = refs[:4], refs[4]
    rows_ref[...] = mm(moves_ref[...], share_ref[...]).astype(BF).reshape(PLANES, TWO_GROUP, HALF)
    for k, out_ref in enumerate(outs):
        for n in range(4):
            out_ref[n] = rows_ref[4 * ((place_ref[1] + n) & 3) + ((place_ref[2] + k) & 3)]


def moves_of(rows, columns, pairs):
    moves = np.zeros((rows, columns), np.float32)
    for row, column in pairs:
        moves[row, column] = 1.0
    return moves


def features_by_z():
    return moves_of(
        D,
        D,
        (
            (48 * p + 24 * h + 12 * c + 6 * l + r, 192 * (2 * h + l) + 12 * p + 6 * c + r)
            for p in range(PLANES)
            for h in range(2)
            for c in range(2)
            for l in range(2)
            for r in range(6)
        ),
    )


def rows_by_group():
    return moves_of(
        PLANES * TWO_GROUP,
        TWO_SHARE,
        ((TWO_GROUP * p + 12 * k + r, 192 * k + 12 * p + r) for p in range(PLANES) for k in range(3) for r in range(12)),
    )


def rows_by_core():
    return moves_of(
        2 * PACK_ROWS,
        TWO_GROUP,
        ((PACK_ROWS * c + 13 + 6 * k + r, 12 * k + 6 * c + r) for c in range(2) for k in range(3) for r in range(6)),
    )


def column_kernel(place_ref, one_ref, early_ref, moves_ref, *refs):
    out_refs, (rows_ref, moved_ref) = refs[:4], refs[4:]
    rows_ref[:ONE_ROWS] = one_ref[...]
    rows_ref[ONE_ROWS:] = early_ref[...]
    moved_ref[...] = mm(moves_ref[...], rows_ref[...]).astype(BF).reshape(4, 2 * PACK_ROWS, HALF)
    for k, out_ref in enumerate(out_refs):
        out_ref[...] = moved_ref[(place_ref[3] + k) & 3]


def column_moves():
    moves = np.zeros((8 * PACK_ROWS, SUM_ROWS), np.float32)
    for high in range(2):
        for low in range(2):
            for core in range(2):
                at = ((2 * high + low) * 2 + core) * PACK_ROWS
                device = (2 * high + core) * 2 + low
                for rows, start in zip(PACK, SUM_STARTS):
                    for row in range(rows if start is not None else 0):
                        moves[at + row, start + device * rows + row] = 1.0
                    at += rows
    return moves


def call(kernel, name, args, outs, scratch, flops, room):
    place = {
        "s": pl.BlockSpec(memory_space=pltpu.SMEM),
        "v": pl.BlockSpec(memory_space=pltpu.VMEM),
        "a": pl.BlockSpec(memory_space=pl.ANY),
    }
    moved = sum(a.size * a.dtype.itemsize for a, _ in args)
    return pl.pallas_call(
        kernel,
        out_shape=[jax.ShapeDtypeStruct(shape, dtype) for shape, dtype, _ in outs],
        in_specs=[place[w] for _, w in args],
        out_specs=[place[w] for _, _, w in outs],
        scratch_shapes=scratch,
        compiler_params=pltpu.CompilerParams(vmem_limit_bytes=room * 2**20),
        cost_estimate=pl.CostEstimate(flops=int(flops), bytes_accessed=int(moved), transcendentals=0),
        name=name,
    )(*[a for a, _ in args])


def swap(block, axis):
    return lax.ppermute(block, axis, [(0, 1), (1, 0)])


def step(block, axis, steps):
    return lax.ppermute(block, axis, [((i + steps) % 4, i) for i in range(4)])


def sum_line(blocks, axis):
    total = blocks[0].astype(F32)
    for k in (1, 2, 3):
        total = total + step(blocks[k], axis, 4 - k).astype(F32)
    return total


def sum_part(blocks, first, second):
    line = blocks[0].astype(F32)
    for k in (1, 2, 3):
        line = line + step(blocks[k], first, 4 - k).astype(F32)
    total = line[0]
    for k in (1, 2, 3):
        total = total + step(line[k].astype(BF), second, 4 - k).astype(F32)
    return total.astype(BF)


def regroup(block, pack):
    at, parts = 0, []
    for rows in pack:
        parts.append(block[:, at : at + rows].reshape(-1, HALF))
        at += rows
    return parts


def pick_table(indices, table):
    match = indices[:, None] == jnp.arange(table.shape[0], dtype=jnp.int32)[None, :]
    return jnp.sum(jnp.where(match, table[None, :], 0.0), axis=1)


def per_device(
    inputs,
    skipped,
    cotangent,
    timestep,
    class_ids,
    time_weight,
    class_weight,
    skip_weight,
    skip_bias,
    first_gain,
    first_shift,
    triple_weight,
    merge_weight,
    merge_bias,
    second_gain,
    second_shift,
    expand_weight,
    expand_bias,
    contract_weight,
    contract_bias,
):
    core_index = lax.axis_index("c").astype(jnp.int32)
    core = core_index[None]
    place = jnp.stack([core_index] + [lax.axis_index(axis).astype(jnp.int32) for axis in ("y", "x", ("h", "l"))])


    inputs, skipped, cotangent = (a.reshape(TOKENS, D) for a in (inputs, skipped, cotangent))
    sem = pltpu.SemaphoreType.DMA
    weight = lambda rows: pltpu.VMEM((PLANES, rows, HALF), BF)
    tokens = lambda width, dtype=BF, where="v": ((PAD, width), dtype, where)
    plane = lambda rows: ((PLANES, rows, HALF), BF, "a")

    vectors = (skip_bias, first_gain, first_shift, merge_bias, second_gain, second_shift, contract_bias, expand_bias)
    row, at = jnp.zeros((1, HALF), F32), 0
    for vector in vectors:
        row = row + jnp.pad(vector.astype(F32)[None, :], ((0, 0), (at, HALF - at - vector.shape[0])))
        at += vector.shape[0]
    flat = dict(
        skip=skip_weight, triple=triple_weight, merge=merge_weight, expand=expand_weight, contract=contract_weight
    )
    flat = {name: a.reshape(-1, 128) for name, a in flat.items()}

    (packed,) = call(
        pack_kernel,
        "pack",
        [(flat[n], "a") for n in NAMES] + [(row, "v")],
        [((8, PACK_ROWS, HALF), BF, "v")],
        [pltpu.VMEM((2, PACK_ROWS, HALF), F32)]
        + [pltpu.VMEM(flat[n].shape, dtype) for dtype in (BF, F32) for n in NAMES]
        + [sem((len(NAMES),))],
        1e6,
        58,
    )
    column = regroup(lax.all_to_all(packed, COLUMN, 0, 0, tiled=True), PACK)
    first = jnp.concatenate(column[:2] + [jnp.zeros((8, HALF), BF)] + column[2:5], axis=0)
    second = jnp.concatenate(column[5:], axis=0)
    second_own = lax.all_gather(second, PLANE, axis=0, tiled=True).reshape(PLANES, SECOND_ROWS, HALF)
    first_own = lax.all_to_all(
        jnp.broadcast_to(first[None], (PLANES, FIRST_ROWS, HALF)), PLANE, 0, 0, tiled=True
    )
    first_own, timestep = lax.optimization_barrier((first_own, timestep))
    scale = pick_table(timestep, time_weight) * pick_table(class_ids, class_weight)
    first_other = swap(first_own, "c")
    after, gift = call(
        prepare_kernel,
        "prepare",
        [(core, "s"), (scale, "s"), (inputs, "v"), (skipped, "v"), (cotangent, "v")],
        [tokens(D), tokens(2 * D + HALF)],
        [],
        1e6,
        8,
    )
    gift_came = swap(gift, "c")

    (spots,) = call(
        spots_kernel, "vectors", [(first_own, "a")], [((16, D), F32, "v")], [weight(16), sem((1,))], 2e8, 8
    )
    united, normed, query, pair = call(
        first_kernel,
        "skip_and_triple",
        [(core, "s"), (gift, "v"), (first_own, "a"), (first_other, "a"), (spots, "v")],
        [tokens(D, F32), tokens(D), tokens(D), tokens(2 * D)],
        [weight(96), weight(96), weight(144), weight(144), sem((4,))],
        2 * PAD * D * (2 * D + 3 * D),
        16,
    )
    pair, gift_came = lax.optimization_barrier((pair, gift_came))
    pair_came = swap(pair, "l")
    normed_came = swap(normed, "c")
    second_own, pair_came, normed_came = lax.optimization_barrier((second_own, pair_came, normed_came))
    second_other = swap(second_own, "c")
    mixed, totals = call(
        attend_kernel,
        "attention",
        [(query, "v"), (pair, "v"), (pair_came, "v")],
        [tokens(D), tokens(128, F32)],
        [],
        2 * PAD * D * 2 * KEYS,
        58,
    )
    mixed_came = swap(mixed, "c")
    output, middle_grad, early_vectors, forward_gift, forward_kept = call(
        forward_kernel,
        "feed_forward",
        [
            (core, "s"),
            (scale, "s"),
            (mixed, "v"),
            (united, "v"),
            (cotangent, "v"),
            (after, "v"),
            (second_own, "a"),
            (second_other, "a"),
            (spots, "v"),
        ],
        [((TOKENS, D), BF, "v"), tokens(D, F32), ((16, D), F32, "v"), tokens(GIFT), tokens(FF // 2)],
        [weight(192)] * 4
        + [weight(48)] * 2
        + [pltpu.VMEM((PAD, FF), F32), pltpu.VMEM((PAD, FF), BF), sem((12,))],
        2 * PAD * D * FF * 4,
        58,
    )
    forward_came = swap(forward_gift, "c")
    query_grad, pair_grad, pair_sent = call(
        backward_kernel,
        "attention_backward",
        [
            (core, "s"),
            (middle_grad, "v"),
            (query, "v"),
            (pair, "v"),
            (pair_came, "v"),
            (totals, "v"),
            (second_own, "a"),
            (second_other, "a"),
        ],
        [tokens(D), tokens(2 * D, F32), tokens(2 * D)],
        [pltpu.VMEM((PAD, D), BF), weight(48), weight(48), sem((2,))],
        2 * PAD * D * (D + 5 * KEYS),
        58,
    )
    grad_came = swap(pair_sent, "l")
    (early_grads,) = call(
        early_kernel,
        "early_gradients",
        [
            (core, "s"),
            (forward_gift, "a"),
            (forward_came, "a"),
            (forward_kept, "a"),
            (after, "v"),
            (gift_came, "a"),
            (mixed, "a"),
            (mixed_came, "a"),
            (middle_grad, "a"),
        ],
        [plane(EARLY_ROWS)],
        [pltpu.VMEM((PAD, GIFT), BF)] * 2
        + [pltpu.VMEM((PAD, width), BF) for width in (FF // 2, HALF, D, D)]
        + [pltpu.VMEM((PAD, D), F32), weight(EARLY_ROWS), sem((9,)), sem((6,))],
        2 * PAD * D * FF * 2,
        58,
    )
    early_sum = lax.psum_scatter(early_grads.reshape(PLANES * EARLY_ROWS, HALF), PLANE, scatter_dimension=0, tiled=True)
    early_vectors, query_grad = lax.optimization_barrier((early_vectors, query_grad))
    by_z = jnp.asarray(features_by_z(), BF)
    query_incoming, early_rows, moved, moved_came = call(
        query_kernel,
        "query_backward",
        [
            (core, "s"),
            (query_grad, "v"),
            (early_vectors, "v"),
            (normed, "v"),
            (normed_came, "v"),
            (by_z, "v"),
            (first_own, "a"),
            (first_other, "a"),
        ],
        [tokens(D, F32), ((128, 128), F32, "v"), tokens(D), tokens(D)],
        [weight(48)] * 2 + [sem((2,))],
        2 * PAD * D * D,
        24,
    )
    united_low, late_vectors, triple_kept, late_gift = call(
        triple_kernel,
        "triple_backward",
        [
            (core, "s"),
            (united, "v"),
            (middle_grad, "v"),
            (query_grad, "v"),
            (pair_grad, "v"),
            (grad_came, "v"),
            (query_incoming, "v"),
            (first_own, "a"),
            (first_other, "a"),
            (spots, "v"),
        ],
        [tokens(D), ((8, D), F32, "v"), tokens(3 * HALF), tokens(4 * HALF)],
        [weight(96)] * 2 + [sem((2,))],
        2 * PAD * D * (2 * D),
        16,
    )
    late_came = swap(late_gift, "c")
    input_grad, skip_grad = call(
        skip_kernel,
        "skip_backward",
        [(core, "s"), (united_low, "v"), (first_own, "a"), (first_other, "a")],
        [((TOKENS, D), BF, "v"), ((TOKENS, D), BF, "v")],
        [weight(96), weight(96), sem((2,))],
        2 * PAD * D * (2 * D),
        12,
    )
    late_came, input_grad, skip_grad = lax.optimization_barrier((late_came, input_grad, skip_grad))
    late = call(
        late_kernel,
        "late_gradients",
        [
            (place, "s"),
            (gift, "v"),
            (gift_came, "v"),
            (moved, "v"),
            (moved_came, "v"),
            (united_low, "v"),
            (triple_kept, "v"),
            (late_came, "v"),
            (early_rows, "v"),
            (late_vectors, "v"),
        ],
        [((4, ONE_ROWS, HALF), BF, "a")] * 4 + [((TWO_SHARE, HALF), BF, "a")] * 4,
        [weight(ONE_ROWS), pltpu.VMEM((4, TWO_SHARE, HALF), BF), sem((8,))],
        2 * PAD * D * (5 * D),
        58,
    )
    one_sum = sum_part(late[:4], "x", "y")
    share = sum_line(late[4:], ("h", "l")).astype(BF)
    groups = call(
        group_kernel,
        "by_group",
        [(place, "s"), (share, "v"), (jnp.asarray(rows_by_group(), BF), "v")],
        [((4, TWO_GROUP, HALF), BF, "v")] * 4,
        [pltpu.VMEM((PLANES, TWO_GROUP, HALF), BF)],
        2 * PLANES * TWO_GROUP * TWO_SHARE * HALF,
        12,
    )
    two_sum = mm(jnp.asarray(rows_by_core(), BF), sum_part(groups, "x", "y"))

    early_sum, two_sum = lax.optimization_barrier((early_sum, two_sum))

    column = call(
        column_kernel,
        "by_device",
        [(place, "s"), (one_sum, "v"), (early_sum, "v"), (jnp.asarray(column_moves(), BF), "v")],
        [((2 * PACK_ROWS, HALF), BF, "v")] * 4,
        [pltpu.VMEM((SUM_ROWS, HALF), BF), pltpu.VMEM((4, 2 * PACK_ROWS, HALF), BF)],
        2 * SUM_ROWS * SUM_ROWS * HALF,
        12,
    )
    total = sum_line(column, ("h", "l")) + two_sum
    mine, sent = order(core_index, total[:PACK_ROWS], total[PACK_ROWS:])
    low, high = order(core_index, mine, swap(sent, "c"))
    rows_of = lambda name: ((flat[name].shape[0], 128), F32, "v")
    skip_out, triple_out, expand_out, contract_out, merge_out, vector_out = call(
        unpack_kernel,
        "by_weight",
        [(low, "v"), (high, "v")],
        [rows_of(name) for name in NAMES] + [((1, 128), F32, "v")],
        [],
        1e6,
        8,
    )
    vector_out = vector_out[0]
    spot = lambda j: vector_out[6 * j : 6 * j + 6]
    return (
        output[None],
        input_grad[None],
        skip_grad[None],
        skip_out.reshape(-1),
        spot(0),
        spot(1),
        spot(2),
        triple_out.reshape(-1),
        merge_out.reshape(-1),
        spot(3),
        spot(4),
        spot(5),
        expand_out.reshape(-1),
        vector_out[42:66],
        contract_out.reshape(-1),
        spot(6),
    )


def solution(mesh):
    fine = jax.sharding.Mesh(mesh.devices.reshape(4, 4, 2, 2, 2), ("y", "x", "h", "c", "l"))
    images = ("y", "x", "h", "c")
    everything = images + ("l",)
    tokens, shard = P(images, "l", None), P(everything)
    return jax.shard_map(
        per_device,
        mesh=fine,
        in_specs=(tokens,) * 3 + (P(images),) * 2 + (P(),) * 2 + (shard,) * 13,
        out_specs=(tokens,) * 3 + (shard,) * 13,
        check_vma=False,
    )
```

```python
import functools
import math

import jax
import jax.numpy as jnp
import numpy as np
from jax import lax
from jax.experimental import pallas as pl
from jax.experimental.pallas import tpu as pltpu
from jax.sharding import PartitionSpec as P

D = 768
HEADS = 12
HEAD_DIM = 64
FF = 3072
HALF = D // 2
STRIPS = FF // D
TOKENS = 129
PAD = 144
KEYS = 2 * PAD
PLANES = 16
PLANE = ("y", "x")
COLUMN = ("h", "c", "l")
SKIP, SPOTS, TRIPLE = 0, 96, 112
EXPAND, CONTRACT, MERGE = 0, 192, 384
FIRST_ROWS, SECOND_ROWS = 256, 432
ONE_ROWS = 112
TWO_SHARE, TWO_GROUP = 3 * D // 4, 48
EARLY_ROWS = 448
FIRST_PACK, SECOND_PACK = (12, 1, 6, 6, 6), (6, 6, 6, 6, 24, 6)
PACK = FIRST_PACK + SECOND_PACK
PACK_ROWS = 88
NAMES = ("skip", "triple", "expand", "contract", "merge")
SUM_ROWS = ONE_ROWS + EARLY_ROWS
SUM_STARTS = (0, 96, None, None, None) + tuple(ONE_ROWS + at for at in (0, 48, 96, 144, 192, 384))
epsilon = 1e-05
score_scale = 1.0 / math.sqrt(HEAD_DIM)
BF, F32 = jnp.bfloat16, jnp.float32
ATTEND = FF + FF // 2
NORMED = ATTEND + HALF
GIFT = NORMED + D


def mm(left, right):
    return jnp.dot(left, right, preferred_element_type=F32)


def mm_t(left, right):
    return lax.dot_general(left, right, (((1,), (1,)), ((), ())), preferred_element_type=F32)


def t_mm(left, right):
    return lax.dot_general(left, right, (((0,), (0,)), ((), ())), preferred_element_type=F32)


def order(core, one, two):
    return jnp.where(core == 0, one, two), jnp.where(core == 0, two, one)


def split(core, block):
    return order(core, block[:, :HALF], block[:, HALF:])


def norm_stats(values):
    mean_value = jnp.mean(values, axis=-1, keepdims=True)
    centered = values - mean_value
    variance = jnp.mean(centered * centered, axis=-1, keepdims=True)
    inverse = lax.rsqrt(variance + epsilon)
    return centered * inverse, inverse


def norm_backward(incoming, scaled, inverse, gain):
    weighted = incoming * gain
    first_mean = jnp.mean(weighted, axis=-1, keepdims=True)
    second_mean = jnp.mean(weighted * scaled, axis=-1, keepdims=True)
    value_grad = inverse * (weighted - first_mean - scaled * second_mean)
    return (
        value_grad,
        jnp.sum(incoming * scaled, axis=0, keepdims=True),
        jnp.sum(incoming, axis=0, keepdims=True),
    )


def padded(block):
    return jnp.concatenate([block, jnp.zeros((PAD - TOKENS, block.shape[1]), block.dtype)], axis=0)


def load(pairs, sems):
    copies = [pltpu.make_async_copy(s, d, sems.at[k]) for k, (s, d) in enumerate(pairs)]
    for copy in copies:
        copy.start()
    return copies


def matrix(ref, at, rows):
    return ref[:, at : at + rows, :].reshape(PLANES * rows, HALF)


def spot_masks(width):
    lanes = lax.broadcasted_iota(jnp.int32, (128, D), 0)
    spots = lax.broadcasted_iota(jnp.int32, (128, D), 1)
    return lanes, lax.rem(spots, width), lax.div(spots, width)


def steps_to(place_ref, plane):
    return (plane // 4 - place_ref[1]) & 3, (plane % 4 - place_ref[2]) & 3


def wait(copies):
    for copy in copies:
        copy.wait()


def tiles_of(matrix_name):
    count, strips, across = {"skip": (6, 1, 6), "triple": (18, 1, 6), "merge": (6, 1, 6), "expand": (24, STRIPS, 24), "contract": (6, 1, 6)}[matrix_name]
    for tile in range(count):
        block, inside = divmod(tile, across)
        half, rest = divmod(inside, across // 2)
        yield tile, half, block + rest // 3, rest % 3


def pack_kernel(*refs):
    count = len(NAMES)
    sources, (row_ref, out_ref, rows_ref), scratch = refs[:count], refs[count : count + 3], refs[count + 3 :]
    low, scratch, sems = scratch[:count], scratch[count : 2 * count], scratch[2 * count]
    copies = load(list(zip(sources, low)), sems)
    at = 0
    for name, held, ref, copy in zip(NAMES, scratch, low, copies):
        copy.wait()
        held[...] = ref[...].astype(F32)
        tiles = list(tiles_of(name))
        rows = held.shape[0] // len(tiles)
        for tile, half, strip, spot in tiles:
            first = at + strip * rows
            rows_ref[half, first : first + rows, 128 * spot : 128 * spot + 128] = held[pl.ds(tile, rows, stride=len(tiles)), :]
        at += rows * (1 + max(t[2] for t in tiles))
        if name == "skip":
            rows_ref[0, at : at + 1, :] = row_ref[...]
            rows_ref[1, at : at + 1, :] = row_ref[...]
            at += 1
    rows_ref[:, at:PACK_ROWS, :] = jnp.zeros((2, PACK_ROWS - at, HALF), F32)
    for half in range(2):
        packed = rows_ref[half].astype(BF)
        for device in range(8):
            if device // 2 % 2 == half:
                out_ref[device] = packed


def unpack_kernel(low_ref, high_ref, *refs):
    outs = dict(zip(NAMES, refs))
    at = 0
    for name in NAMES:
        tiles = list(tiles_of(name))
        rows = outs[name].shape[0] // len(tiles)
        for tile, half, strip, spot in tiles:
            first = at + strip * rows
            source = high_ref if half else low_ref
            outs[name][pl.ds(tile, rows, stride=len(tiles)), :] = source[first : first + rows, 128 * spot : 128 * spot + 128]
        at += rows * (1 + max(t[2] for t in tiles))
        if name == "skip":
            refs[5][...] = low_ref[at : at + 1, :128] + high_ref[at : at + 1, :128]
            at += 1


def prepare_kernel(core_ref, scale_ref, in_ref, skip_ref, cotangent_ref, after_ref, gift_ref):
    gift_ref[:, :D] = padded(in_ref[...])
    gift_ref[:, D : 2 * D] = padded(skip_ref[...])
    after = padded(cotangent_ref[...].astype(F32) * scale_ref[0]).astype(BF)
    after_ref[...] = after
    gift_ref[:, 2 * D :] = split(core_ref[0], after)[1]


def spots_kernel(first_ref, out_ref, rows_ref, sems):
    wait(load([(first_ref.at[:, SPOTS : SPOTS + 16, :], rows_ref)], sems))
    held = rows_ref[:, :, :128].astype(F32)[:, :8].reshape(128, 128).astype(BF)
    for j in range(7):
        lanes, place, owner = spot_masks(6)
        one_hot = (lanes - 6 * j == place).astype(BF)
        spread = jnp.where(owner == lanes, mm(held, one_hot), 0.0)
        out_ref[j : j + 1, :] = jnp.sum(spread, axis=0, keepdims=True)
    out_ref[7:8, :] = jnp.zeros((1, D), F32)
    lanes, place, owner = spot_masks(24)
    spread = mm(held, (lanes - 42 == place).astype(BF))
    for m in range(STRIPS):
        out_ref[8 + m : 9 + m, :] = jnp.sum(jnp.where(owner + 32 * m == lanes, spread, 0.0), axis=0, keepdims=True)
    out_ref[12:16, :] = jnp.zeros((4, D), F32)


def first_kernel(core_ref, joined_ref, own_ref, other_ref, spots_ref, united_ref, normed_ref, query_ref, pair_ref, so, ss, to, ts, sems):
    core = core_ref[0]
    copies = load(
        [
            (own_ref.at[:, SKIP : SKIP + 96, :], so),
            (other_ref.at[:, SKIP : SKIP + 96, :], ss),
            (own_ref.at[:, TRIPLE : TRIPLE + 144, :], to),
            (other_ref.at[:, TRIPLE : TRIPLE + 144, :], ts),
        ],
        sems,
    )
    joined = joined_ref[:, : 2 * D]
    copies[0].wait()
    one = mm(joined, matrix(so, 0, 96))
    copies[1].wait()
    two = mm(joined, matrix(ss, 0, 96))
    united = jnp.concatenate(order(core, one, two), axis=1) + spots_ref[0:1, :]
    united_ref[...] = united
    scaled, _ = norm_stats(united)
    normed = (scaled * spots_ref[1:2, :] + spots_ref[2:3, :]).astype(BF)
    normed_ref[...] = normed
    copies[2].wait()
    copies[3].wait()
    for k in range(3):
        one = mm(normed, matrix(to, 48 * k, 48))
        two = mm(normed, matrix(ts, 48 * k, 48))
        block = jnp.concatenate(order(core, one, two), axis=1).astype(BF)
        if k == 0:
            query_ref[...] = block
        else:
            pair_ref[:, (k - 1) * D : k * D] = block


def key_mask():
    spots = lax.broadcasted_iota(jnp.int32, (1, KEYS), 1)
    return (spots < TOKENS) | ((spots >= PAD) & (spots < PAD + TOKENS))


def attend_kernel(query_ref, pair_ref, came_ref, mixed_ref, total_ref):
    mask = key_mask()
    total_ref[...] = jnp.zeros((PAD, 128), F32)
    for pair in range(HEADS // 2):
        at = slice(128 * pair, 128 * pair + 128)
        late = slice(D + 128 * pair, D + 128 * pair + 128)
        query = query_ref[:, at]
        keys = jnp.concatenate([pair_ref[:, at], came_ref[:, at]], axis=0)
        values = jnp.concatenate([pair_ref[:, late], came_ref[:, late]], axis=0)
        done = []
        for side in range(2):
            head = slice(HEAD_DIM * side, HEAD_DIM * side + HEAD_DIM)
            scores = mm_t(query[:, head], keys[:, head]) * score_scale
            scores = jnp.where(mask, scores, -1e30)
            largest = jnp.max(scores, axis=-1, keepdims=True)
            powered = jnp.exp(scores - largest)
            totals = jnp.sum(powered, axis=-1, keepdims=True)
            total_ref[:, 2 * pair + side : 2 * pair + side + 1] = largest + jnp.log(totals)
            soft_low = (powered / totals).astype(BF)
            done.append(mm(soft_low, values[:, head]))
        mixed_ref[:, at] = jnp.concatenate(done, axis=1).astype(BF)


def forward_kernel(core_ref, scale_ref, mixed_ref, united_ref, cotangent_ref, after_ref, own_ref, other_ref, spots_ref, out_ref, middle_grad_ref, vector_ref, gift_ref, kept_ref, eo, es, co, cs, mo, ms, slope_ref, low_ref, sems):
    core = core_ref[0]
    copies = load(
        [
            (own_ref.at[:, MERGE : MERGE + 48, :], mo),
            (other_ref.at[:, MERGE : MERGE + 48, :], ms),
            *[
                (ref.at[:, 48 * k : 48 * k + 48, :], to.at[:, 48 * k : 48 * k + 48, :])
                for k in range(STRIPS)
                for ref, to in ((own_ref, eo), (other_ref, es))
            ],
            (own_ref.at[:, CONTRACT : CONTRACT + 192, :], co),
            (other_ref.at[:, CONTRACT : CONTRACT + 192, :], cs),
        ],
        sems,
    )
    after = after_ref[...]
    vector_ref[...] = jnp.zeros((16, D), F32)
    vector_ref[6:7, :] = jnp.sum(after.astype(F32), axis=0, keepdims=True)
    after_own, after_other = split(core, after)
    mixed = mixed_ref[...]
    wait(copies[:2])
    one, two = mm(mixed, matrix(mo, 0, 48)), mm(mixed, matrix(ms, 0, 48))
    middle = united_ref[...] + jnp.concatenate(order(core, one, two), axis=1) + spots_ref[3:4, :]
    scaled, inverse = norm_stats(middle)
    normed = (scaled * spots_ref[4:5, :] + spots_ref[5:6, :]).astype(BF)
    gift_ref[:, NORMED:] = normed
    for k in range(STRIPS):
        wait(copies[2 + 2 * k : 4 + 2 * k])
        one, two = order(core, mm(normed, matrix(eo, 48 * k, 48)), mm(normed, matrix(es, 48 * k, 48)))
        for side, block in ((0, one), (1, two)):
            at = side * STRIPS * HALF + k * HALF
            bias = spots_ref[8 + at // D : 9 + at // D, at % D : at % D + HALF]
            block = block + bias
            cumulative = 0.5 * (1.0 + lax.erf(block * (1.0 / math.sqrt(2.0))))
            density = jnp.exp(-0.5 * block * block) * (1.0 / math.sqrt(2.0 * math.pi))
            gift_ref[:, at : at + HALF] = (block * cumulative).astype(BF)
            slope_ref[:, at : at + HALF] = cumulative + block * density
    wait(copies[2 + 2 * STRIPS :])
    active = gift_ref[:, :FF]
    one, two = mm(active, matrix(co, 0, 192)), mm(active, matrix(cs, 0, 192))
    output = middle + jnp.concatenate(order(core, one, two), axis=1) + spots_ref[6:7, :]
    out_ref[...] = output[:TOKENS].astype(BF)
    for j in range(2 * STRIPS):
        at, planes = slice(HALF * j, HALF * j + HALF), slice(2 * j, 2 * j + 2)
        back = mm_t(after_own, co[planes, :, :].reshape(HALF, HALF)) + mm_t(after_other, cs[planes, :, :].reshape(HALF, HALF))
        low = (back * slope_ref[:, at]).astype(BF)
        low_ref[:, at] = low
        row = 8 + j // 2
        vector_ref[row : row + 1, HALF * (j % 2) : HALF * (j % 2) + HALF] = jnp.sum(low.astype(F32), axis=0, keepdims=True)
    incoming = jnp.zeros((PAD, D), F32)
    for k in range(STRIPS):
        one, two = order(
            core,
            low_ref[:, k * HALF : (k + 1) * HALF],
            low_ref[:, (STRIPS + k) * HALF : (STRIPS + k + 1) * HALF],
        )
        kept_ref[:, k * HALF : (k + 1) * HALF] = one
        gift_ref[:, FF + k * HALF : FF + (k + 1) * HALF] = two
        incoming = incoming + mm_t(one, matrix(eo, 48 * k, 48)) + mm_t(two, matrix(es, 48 * k, 48))
    back_two, gain_grad, shift_grad = norm_backward(incoming, scaled, inverse, spots_ref[4:5, :])
    vector_ref[4:5, :] = gain_grad
    vector_ref[5:6, :] = shift_grad
    middle_grad = padded(cotangent_ref[...].astype(F32) * scale_ref[0]) + back_two
    middle_grad_ref[...] = middle_grad
    attend = middle_grad.astype(BF)
    vector_ref[3:4, :] = jnp.sum(attend.astype(F32), axis=0, keepdims=True)
    gift_ref[:, ATTEND:NORMED] = split(core, attend)[1]


def early_kernel(core_ref, gift_any, came_any, kept_any, after_ref, first_came_any, mixed_any, mixed_came_any, middle_grad_any, grad_ref, gift_ref, came_ref, kept_ref, after_came_ref, mixed_ref, mixed_came_ref, middle_grad_ref, go, sems, out_sems):
    core = core_ref[0]
    copies = load(
        [
            (gift_any.at[:, :FF], gift_ref.at[:, :FF]),
            (came_any.at[:, :FF], came_ref.at[:, :FF]),
            (first_came_any.at[:, 2 * D :], after_came_ref),
            (gift_any.at[:, NORMED:], gift_ref.at[:, NORMED:]),
            (came_any.at[:, FF:], came_ref.at[:, FF:]),
            (kept_any, kept_ref),
            (mixed_any, mixed_ref),
            (mixed_came_any, mixed_came_ref),
            (middle_grad_any, middle_grad_ref),
        ],
        sems,
    )
    wait(copies[:3])
    after, after_came = split(core, after_ref[...])[0], after_came_ref[...]
    for j in range(2 * STRIPS):
        at, planes = slice(HALF * j, HALF * j + HALF), slice(2 * j, 2 * j + 2)
        grad = t_mm(gift_ref[:, at], after) + t_mm(came_ref[:, at], after_came)
        go[planes, CONTRACT : CONTRACT + 192, :] = grad.astype(BF).reshape(2, 192, HALF)
    rows = lambda at, to: (go.at[:, at:to, :], grad_ref.at[:, at:to, :])
    sends = load([rows(CONTRACT, CONTRACT + 192)], out_sems)
    wait(copies[3:])
    attend = split(core, middle_grad_ref[...].astype(BF))[0]
    grad = t_mm(mixed_ref[...], attend) + t_mm(mixed_came_ref[...], came_ref[:, ATTEND:NORMED])
    go[:, MERGE : MERGE + 48, :] = grad.astype(BF).reshape(PLANES, 48, HALF)
    go[:, MERGE + 48 :, :] = jnp.zeros((PLANES, EARLY_ROWS - MERGE - 48, HALF), BF)
    sends += load([rows(MERGE, EARLY_ROWS)], out_sems.at[1:])
    normed, normed_came = gift_ref[:, NORMED:], came_ref[:, NORMED:]
    for k in range(STRIPS):
        grad = t_mm(normed, kept_ref[:, k * HALF : (k + 1) * HALF]) + t_mm(
            normed_came, came_ref[:, FF + k * HALF : FF + (k + 1) * HALF]
        )
        go[:, EXPAND + 48 * k : EXPAND + 48 * (k + 1), :] = grad.astype(BF).reshape(PLANES, 48, HALF)
        sends += load([rows(EXPAND + 48 * k, EXPAND + 48 * (k + 1))], out_sems.at[2 + k :])
    wait(sends)


def backward_kernel(core_ref, middle_grad_ref, query_ref, pair_ref, came_ref, total_ref, own_ref, other_ref, query_grad_ref, pair_grad_ref, sent_ref, mixed_grad_ref, mo, ms, sems):
    core = core_ref[0]
    copies = load(
        [(own_ref.at[:, MERGE : MERGE + 48, :], mo), (other_ref.at[:, MERGE : MERGE + 48, :], ms)], sems
    )
    attend_own, attend_other = split(core, middle_grad_ref[...].astype(BF))
    mask = key_mask()
    copies[0].wait()
    copies[1].wait()
    mixed_grad_ref[...] = (mm_t(attend_own, matrix(mo, 0, 48)) + mm_t(attend_other, matrix(ms, 0, 48))).astype(BF)
    for pair in range(HEADS // 2):
        at = slice(128 * pair, 128 * pair + 128)
        late = slice(D + 128 * pair, D + 128 * pair + 128)
        query, mixed_grad = query_ref[:, at], mixed_grad_ref[:, at]
        keys = jnp.concatenate([pair_ref[:, at], came_ref[:, at]], axis=0)
        values = jnp.concatenate([pair_ref[:, late], came_ref[:, late]], axis=0)
        query_parts, key_parts, value_parts = [], [], []
        for side in range(2):
            head = slice(HEAD_DIM * side, HEAD_DIM * side + HEAD_DIM)
            scores = mm_t(query[:, head], keys[:, head]) * score_scale
            scores = jnp.where(mask, scores, -1e30)
            soft = jnp.exp(scores - total_ref[:, 2 * pair + side : 2 * pair + side + 1])
            soft_grad = mm_t(mixed_grad[:, head], values[:, head])
            inner = jnp.sum(soft * soft_grad, axis=-1, keepdims=True)
            scores_grad = (soft * (soft_grad - inner)).astype(BF)
            query_parts.append(mm(scores_grad, keys[:, head]))
            key_parts.append(t_mm(scores_grad, query[:, head]))
            value_parts.append(t_mm(soft.astype(BF), mixed_grad[:, head]))
        query_grad_ref[:, at] = (jnp.concatenate(query_parts, axis=1) * score_scale).astype(BF)
        key_grad = jnp.concatenate(key_parts, axis=1) * score_scale
        value_grad = jnp.concatenate(value_parts, axis=1)
        pair_grad_ref[:, at] = key_grad[:PAD]
        pair_grad_ref[:, late] = value_grad[:PAD]
        sent_ref[:, at] = key_grad[PAD:].astype(BF)
        sent_ref[:, late] = value_grad[PAD:].astype(BF)


def scatter(place_ref, ref, block, at, by_y):
    rows = block.shape[0] // PLANES
    for plane in range(PLANES):
        step_y, step_x = steps_to(place_ref, plane)
        spot = 4 * step_y + step_x if by_y else 4 * step_x + step_y
        ref[spot, at : at + rows, :] = block[plane * rows : (plane + 1) * rows]


def vector_rows(vectors, places):
    rows = jnp.zeros((128, 128), F32)
    for vector, at in zip(vectors, places):
        lanes, place, owner = spot_masks(6)
        spread = jnp.where(owner == lanes, vector, 0.0).astype(BF)
        rows = rows + mm_t(spread, (lanes - at == place).astype(BF))
    return rows


def query_kernel(core_ref, query_grad_ref, early_ref, normed_ref, normed_came_ref, own_ref, other_ref, incoming_ref, rows_ref, moved_ref, moved_came_ref, to, ts, sems):
    copies = load(
        [(own_ref.at[:, TRIPLE : TRIPLE + 48, :], to), (other_ref.at[:, TRIPLE : TRIPLE + 48, :], ts)], sems
    )
    rows = vector_rows([early_ref[j : j + 1, :] for j in range(3, 7)], (18, 24, 30, 36))
    lanes, place, owner = spot_masks(24)
    for m in range(STRIPS):
        spread = jnp.where(owner + 32 * m == lanes, early_ref[8 + m : 9 + m, :], 0.0).astype(BF)
        rows = rows + mm_t(spread, (lanes - 42 == place).astype(BF))
    rows_ref[...] = rows
    one, two = split(core_ref[0], query_grad_ref[...])
    wait(copies)
    incoming_ref[...] = mm_t(one, matrix(to, 0, 48)) + mm_t(two, matrix(ts, 0, 48))
    row = lax.broadcasted_iota(jnp.int32, (D, 128), 0)
    plane, inside = lax.div(row, 48), lax.rem(row, 48)
    high, core, low, entry = lax.div(inside, 24), lax.div(lax.rem(inside, 24), 12), lax.div(lax.rem(inside, 12), 6), lax.rem(inside, 6)
    by_z = one_hot(192 * (2 * high + low) + 12 * plane + 6 * core + entry, D)
    moved_ref[...] = mm(normed_ref[...], by_z).astype(BF)
    moved_came_ref[...] = mm(normed_came_ref[...], by_z).astype(BF)


def triple_kernel(core_ref, united_ref, middle_grad_ref, query_grad_ref, pair_grad_ref, came_ref, incoming_ref, own_ref, other_ref, spots_ref, low_ref, vector_ref, kept_ref, gift_ref, to, ts, sems):
    core = core_ref[0]
    copies = load(
        [(own_ref.at[:, TRIPLE + 48 : TRIPLE + 144, :], to), (other_ref.at[:, TRIPLE + 48 : TRIPLE + 144, :], ts)], sems
    )
    scaled, inverse = norm_stats(united_ref[...])
    incoming = incoming_ref[...]
    wait(copies)
    for k in range(3):
        if k == 0:
            block = query_grad_ref[...]
        else:
            at = slice((k - 1) * D, k * D)
            block = (pair_grad_ref[:, at] + came_ref[:, at].astype(F32)).astype(BF)
        one, two = split(core, block)
        kept_ref[:, k * HALF : (k + 1) * HALF] = one
        gift_ref[:, k * HALF : (k + 1) * HALF] = two
        if k:
            incoming = incoming + mm_t(one, matrix(to, 48 * (k - 1), 48)) + mm_t(two, matrix(ts, 48 * (k - 1), 48))
    back_one, gain_grad, shift_grad = norm_backward(incoming, scaled, inverse, spots_ref[1:2, :])
    united_low = (middle_grad_ref[...] + back_one).astype(BF)
    low_ref[...] = united_low
    gift_ref[:, 3 * HALF :] = split(core, united_low)[1]
    vector_ref[0:1, :] = jnp.sum(united_low.astype(F32), axis=0, keepdims=True)
    vector_ref[1:2, :] = gain_grad
    vector_ref[2:3, :] = shift_grad
    vector_ref[3:8, :] = jnp.zeros((5, D), F32)


def skip_kernel(core_ref, low_ref, own_ref, other_ref, in_grad_ref, skip_grad_ref, so, ss, sems):
    copies = load(
        [(own_ref.at[:, SKIP : SKIP + 96, :], so), (other_ref.at[:, SKIP : SKIP + 96, :], ss)], sems
    )
    low_own, low_other = split(core_ref[0], low_ref[...])
    wait(copies)
    for half, grad_ref in ((0, in_grad_ref), (1, skip_grad_ref)):
        planes = slice(8 * half, 8 * half + 8)
        back = mm_t(low_own, so[planes, :, :].reshape(D, HALF)) + mm_t(low_other, ss[planes, :, :].reshape(D, HALF))
        grad_ref[...] = back[:TOKENS].astype(BF)


def late_kernel(place_ref, joined_ref, first_came_ref, normed_ref, normed_came_ref, low_ref, kept_ref, came_ref, early_ref, vector_ref, *refs):
    one_refs, two_refs, (go, gt, sems) = refs[:4], refs[4:8], refs[8:]
    for k in range(3):
        at = slice(k * HALF, (k + 1) * HALF)
        grad = (t_mm(normed_ref[...], kept_ref[:, at]) + t_mm(normed_came_ref[...], came_ref[:, at])).astype(BF)
        for z in range(4):
            gt[(z - place_ref[3]) & 3, 192 * k : 192 * k + 192, :] = grad[192 * z : 192 * z + 192]
    sends = load([(gt.at[k], two_refs[k]) for k in range(4)], sems.at[:4])
    low, low_came = split(place_ref[0], low_ref[...])[0], came_ref[:, 3 * HALF :]
    grad = t_mm(joined_ref[:, : 2 * D], low) + t_mm(first_came_ref[:, : 2 * D], low_came)
    scatter(place_ref, go, grad.astype(BF), SKIP, False)
    rows = early_ref[...] + vector_rows([vector_ref[j : j + 1, :] for j in range(3)], (0, 6, 12))
    rows = jnp.concatenate([rows.reshape(PLANES, 8, 128), jnp.zeros((PLANES, 8, 128), F32)], axis=1)
    rows = jnp.concatenate([rows, jnp.zeros((PLANES, 16, HALF - 128), F32)], axis=2)
    scatter(place_ref, go, rows.reshape(PLANES * 16, HALF).astype(BF), 96, False)
    wait(sends)
    wait(load([(go.at[4 * k : 4 * k + 4], one_refs[k]) for k in range(4)], sems.at[4:]))


def one_hot(spots, columns):
    lanes = lax.broadcasted_iota(jnp.int32, spots.shape, 1)
    tiles = [(spots == lanes + 128 * t).astype(F32) for t in range(-(-columns // 128))]
    return jnp.concatenate(tiles, axis=1)[:, :columns].astype(BF)


def group_kernel(place_ref, share_ref, *refs):
    outs, rows_ref = refs[:4], refs[4]
    row = lax.broadcasted_iota(jnp.int32, (PLANES * TWO_GROUP, 128), 0)
    group, inside = lax.div(row, TWO_GROUP), lax.rem(row, TWO_GROUP)
    spots = jnp.where(inside < 36, 192 * lax.div(inside, 12) + 12 * group + lax.rem(inside, 12), -1)
    rows_ref[...] = mm(one_hot(spots, TWO_SHARE), share_ref[...]).astype(BF).reshape(PLANES, TWO_GROUP, HALF)
    for k, out_ref in enumerate(outs):
        for n in range(4):
            out_ref[n] = rows_ref[4 * ((place_ref[1] + n) & 3) + ((place_ref[2] + k) & 3)]


def moves_of(rows, columns, pairs):
    moves = np.zeros((rows, columns), np.float32)
    for row, column in pairs:
        moves[row, column] = 1.0
    return moves


def rows_by_core():
    return moves_of(
        2 * PACK_ROWS,
        TWO_GROUP,
        ((PACK_ROWS * c + 13 + 6 * k + r, 12 * k + 6 * c + r) for c in range(2) for k in range(3) for r in range(6)),
    )


def column_kernel(place_ref, one_ref, early_ref, moves_ref, *refs):
    out_refs, (rows_ref, moved_ref) = refs[:4], refs[4:]
    rows_ref[:ONE_ROWS] = one_ref[...]
    rows_ref[ONE_ROWS:] = early_ref[...]
    moved_ref[...] = mm(moves_ref[...], rows_ref[...]).astype(BF).reshape(4, 2 * PACK_ROWS, HALF)
    for k, out_ref in enumerate(out_refs):
        out_ref[...] = moved_ref[(place_ref[3] + k) & 3]


def column_moves():
    moves = np.zeros((8 * PACK_ROWS, SUM_ROWS), np.float32)
    for high in range(2):
        for low in range(2):
            for core in range(2):
                at = ((2 * high + low) * 2 + core) * PACK_ROWS
                device = (2 * high + core) * 2 + low
                for rows, start in zip(PACK, SUM_STARTS):
                    for row in range(rows if start is not None else 0):
                        moves[at + row, start + device * rows + row] = 1.0
                    at += rows
    return moves


def call(kernel, name, args, outs, scratch, flops, room):
    place = {
        "s": pl.BlockSpec(memory_space=pltpu.SMEM),
        "v": pl.BlockSpec(memory_space=pltpu.VMEM),
        "a": pl.BlockSpec(memory_space=pl.ANY),
    }
    moved = sum(a.size * a.dtype.itemsize for a, _ in args)
    return pl.pallas_call(
        kernel,
        out_shape=[jax.ShapeDtypeStruct(shape, dtype) for shape, dtype, _ in outs],
        in_specs=[place[w] for _, w in args],
        out_specs=[place[w] for _, _, w in outs],
        scratch_shapes=scratch,
        compiler_params=pltpu.CompilerParams(vmem_limit_bytes=room * 2**20),
        cost_estimate=pl.CostEstimate(flops=int(flops), bytes_accessed=int(moved), transcendentals=0),
        name=name,
    )(*[a for a, _ in args])


def swap(block, axis):
    return lax.ppermute(block, axis, [(0, 1), (1, 0)])


def step(block, axis, steps):
    return lax.ppermute(block, axis, [((i + steps) % 4, i) for i in range(4)])


def sum_line(blocks, axis):
    total = blocks[0].astype(F32)
    for k in (1, 2, 3):
        total = total + step(blocks[k], axis, 4 - k).astype(F32)
    return total


def sum_part(blocks, first, second):
    line = blocks[0].astype(F32)
    for k in (1, 2, 3):
        line = line + step(blocks[k], first, 4 - k).astype(F32)
    total = line[0]
    for k in (1, 2, 3):
        total = total + step(line[k].astype(BF), second, 4 - k).astype(F32)
    return total.astype(BF)


def regroup(block, pack):
    at, parts = 0, []
    for rows in pack:
        parts.append(block[:, at : at + rows].reshape(-1, HALF))
        at += rows
    return parts


def pick_table(indices, table):
    match = indices[:, None] == jnp.arange(table.shape[0], dtype=jnp.int32)[None, :]
    return jnp.sum(jnp.where(match, table[None, :], 0.0), axis=1)


def per_device(
    inputs,
    skipped,
    cotangent,
    timestep,
    class_ids,
    time_weight,
    class_weight,
    skip_weight,
    skip_bias,
    first_gain,
    first_shift,
    triple_weight,
    merge_weight,
    merge_bias,
    second_gain,
    second_shift,
    expand_weight,
    expand_bias,
    contract_weight,
    contract_bias,
):
    core_index = lax.axis_index("c").astype(jnp.int32)
    core = core_index[None]
    place = jnp.stack([core_index] + [lax.axis_index(axis).astype(jnp.int32) for axis in ("y", "x", ("h", "l"))])


    inputs, skipped, cotangent = (a.reshape(TOKENS, D) for a in (inputs, skipped, cotangent))
    sem = pltpu.SemaphoreType.DMA
    weight = lambda rows: pltpu.VMEM((PLANES, rows, HALF), BF)
    tokens = lambda width, dtype=BF, where="v": ((PAD, width), dtype, where)
    plane = lambda rows: ((PLANES, rows, HALF), BF, "a")

    vectors = (skip_bias, first_gain, first_shift, merge_bias, second_gain, second_shift, contract_bias, expand_bias)
    row, at = jnp.zeros((1, HALF), F32), 0
    for vector in vectors:
        row = row + jnp.pad(vector.astype(F32)[None, :], ((0, 0), (at, HALF - at - vector.shape[0])))
        at += vector.shape[0]
    flat = dict(
        skip=skip_weight, triple=triple_weight, merge=merge_weight, expand=expand_weight, contract=contract_weight
    )
    flat = {name: a.reshape(-1, 128) for name, a in flat.items()}

    (packed,) = call(
        pack_kernel,
        "pack",
        [(flat[n], "a") for n in NAMES] + [(row, "v")],
        [((8, PACK_ROWS, HALF), BF, "v")],
        [pltpu.VMEM((2, PACK_ROWS, HALF), F32)]
        + [pltpu.VMEM(flat[n].shape, dtype) for dtype in (BF, F32) for n in NAMES]
        + [sem((len(NAMES),))],
        1e6,
        58,
    )
    column = regroup(lax.all_to_all(packed, COLUMN, 0, 0, tiled=True), PACK)
    first = jnp.concatenate(column[:2] + [jnp.zeros((8, HALF), BF)] + column[2:5], axis=0)
    second = jnp.concatenate(column[5:], axis=0)
    second_own = lax.all_gather(second, PLANE, axis=0, tiled=True).reshape(PLANES, SECOND_ROWS, HALF)
    first_own = lax.all_to_all(
        jnp.broadcast_to(first[None], (PLANES, FIRST_ROWS, HALF)), PLANE, 0, 0, tiled=True
    )
    first_own, timestep = lax.optimization_barrier((first_own, timestep))
    scale = pick_table(timestep, time_weight) * pick_table(class_ids, class_weight)
    first_other = swap(first_own, "c")
    after, gift = call(
        prepare_kernel,
        "prepare",
        [(core, "s"), (scale, "s"), (inputs, "v"), (skipped, "v"), (cotangent, "v")],
        [tokens(D), tokens(2 * D + HALF)],
        [],
        1e6,
        8,
    )
    gift_came = swap(gift, "c")

    (spots,) = call(
        spots_kernel, "vectors", [(first_own, "a")], [((16, D), F32, "v")], [weight(16), sem((1,))], 2e8, 8
    )
    united, normed, query, pair = call(
        first_kernel,
        "skip_and_triple",
        [(core, "s"), (gift, "v"), (first_own, "a"), (first_other, "a"), (spots, "v")],
        [tokens(D, F32), tokens(D), tokens(D), tokens(2 * D)],
        [weight(96), weight(96), weight(144), weight(144), sem((4,))],
        2 * PAD * D * (2 * D + 3 * D),
        16,
    )
    pair, gift_came = lax.optimization_barrier((pair, gift_came))
    pair_came = swap(pair, "l")
    normed_came = swap(normed, "c")
    second_own, pair_came, normed_came = lax.optimization_barrier((second_own, pair_came, normed_came))
    second_other = swap(second_own, "c")
    mixed, totals = call(
        attend_kernel,
        "attention",
        [(query, "v"), (pair, "v"), (pair_came, "v")],
        [tokens(D), tokens(128, F32)],
        [],
        2 * PAD * D * 2 * KEYS,
        58,
    )
    mixed_came = swap(mixed, "c")
    output, middle_grad, early_vectors, forward_gift, forward_kept = call(
        forward_kernel,
        "feed_forward",
        [
            (core, "s"),
            (scale, "s"),
            (mixed, "v"),
            (united, "v"),
            (cotangent, "v"),
            (after, "v"),
            (second_own, "a"),
            (second_other, "a"),
            (spots, "v"),
        ],
        [((TOKENS, D), BF, "v"), tokens(D, F32), ((16, D), F32, "v"), tokens(GIFT), tokens(FF // 2)],
        [weight(192)] * 4
        + [weight(48)] * 2
        + [pltpu.VMEM((PAD, FF), F32), pltpu.VMEM((PAD, FF), BF), sem((12,))],
        2 * PAD * D * FF * 4,
        58,
    )
    forward_came = swap(forward_gift, "c")
    query_grad, pair_grad, pair_sent = call(
        backward_kernel,
        "attention_backward",
        [
            (core, "s"),
            (middle_grad, "v"),
            (query, "v"),
            (pair, "v"),
            (pair_came, "v"),
            (totals, "v"),
            (second_own, "a"),
            (second_other, "a"),
        ],
        [tokens(D), tokens(2 * D, F32), tokens(2 * D)],
        [pltpu.VMEM((PAD, D), BF), weight(48), weight(48), sem((2,))],
        2 * PAD * D * (D + 5 * KEYS),
        58,
    )
    grad_came = swap(pair_sent, "l")
    (early_grads,) = call(
        early_kernel,
        "early_gradients",
        [
            (core, "s"),
            (forward_gift, "a"),
            (forward_came, "a"),
            (forward_kept, "a"),
            (after, "v"),
            (gift_came, "a"),
            (mixed, "a"),
            (mixed_came, "a"),
            (middle_grad, "a"),
        ],
        [plane(EARLY_ROWS)],
        [pltpu.VMEM((PAD, GIFT), BF)] * 2
        + [pltpu.VMEM((PAD, width), BF) for width in (FF // 2, HALF, D, D)]
        + [pltpu.VMEM((PAD, D), F32), weight(EARLY_ROWS), sem((9,)), sem((6,))],
        2 * PAD * D * FF * 2,
        58,
    )
    early_sum = lax.psum_scatter(early_grads.reshape(PLANES * EARLY_ROWS, HALF), PLANE, scatter_dimension=0, tiled=True)
    early_vectors, query_grad = lax.optimization_barrier((early_vectors, query_grad))
    query_incoming, early_rows, moved, moved_came = call(
        query_kernel,
        "query_backward",
        [
            (core, "s"),
            (query_grad, "v"),
            (early_vectors, "v"),
            (normed, "v"),
            (normed_came, "v"),
            (first_own, "a"),
            (first_other, "a"),
        ],
        [tokens(D, F32), ((128, 128), F32, "v"), tokens(D), tokens(D)],
        [weight(48)] * 2 + [sem((2,))],
        2 * PAD * D * D,
        24,
    )
    united_low, late_vectors, triple_kept, late_gift = call(
        triple_kernel,
        "triple_backward",
        [
            (core, "s"),
            (united, "v"),
            (middle_grad, "v"),
            (query_grad, "v"),
            (pair_grad, "v"),
            (grad_came, "v"),
            (query_incoming, "v"),
            (first_own, "a"),
            (first_other, "a"),
            (spots, "v"),
        ],
        [tokens(D), ((8, D), F32, "v"), tokens(3 * HALF), tokens(4 * HALF)],
        [weight(96)] * 2 + [sem((2,))],
        2 * PAD * D * (2 * D),
        16,
    )
    late_came = swap(late_gift, "c")
    input_grad, skip_grad = call(
        skip_kernel,
        "skip_backward",
        [(core, "s"), (united_low, "v"), (first_own, "a"), (first_other, "a")],
        [((TOKENS, D), BF, "v"), ((TOKENS, D), BF, "v")],
        [weight(96), weight(96), sem((2,))],
        2 * PAD * D * (2 * D),
        12,
    )
    late_came, input_grad, skip_grad = lax.optimization_barrier((late_came, input_grad, skip_grad))
    late = call(
        late_kernel,
        "late_gradients",
        [
            (place, "s"),
            (gift, "v"),
            (gift_came, "v"),
            (moved, "v"),
            (moved_came, "v"),
            (united_low, "v"),
            (triple_kept, "v"),
            (late_came, "v"),
            (early_rows, "v"),
            (late_vectors, "v"),
        ],
        [((4, ONE_ROWS, HALF), BF, "a")] * 4 + [((TWO_SHARE, HALF), BF, "a")] * 4,
        [weight(ONE_ROWS), pltpu.VMEM((4, TWO_SHARE, HALF), BF), sem((8,))],
        2 * PAD * D * (5 * D),
        58,
    )
    one_sum = sum_part(late[:4], "x", "y")
    share = sum_line(late[4:], ("h", "l")).astype(BF)
    groups = call(
        group_kernel,
        "by_group",
        [(place, "s"), (share, "v")],
        [((4, TWO_GROUP, HALF), BF, "v")] * 4,
        [pltpu.VMEM((PLANES, TWO_GROUP, HALF), BF)],
        2 * PLANES * TWO_GROUP * TWO_SHARE * HALF,
        12,
    )
    two_sum = mm(jnp.asarray(rows_by_core(), BF), sum_part(groups, "x", "y"))

    early_sum, two_sum = lax.optimization_barrier((early_sum, two_sum))

    column = call(
        column_kernel,
        "by_device",
        [(place, "s"), (one_sum, "v"), (early_sum, "v"), (jnp.asarray(column_moves(), BF), "v")],
        [((2 * PACK_ROWS, HALF), BF, "v")] * 4,
        [pltpu.VMEM((SUM_ROWS, HALF), BF), pltpu.VMEM((4, 2 * PACK_ROWS, HALF), BF)],
        2 * SUM_ROWS * SUM_ROWS * HALF,
        12,
    )
    total = sum_line(column, ("h", "l")) + two_sum
    mine, sent = order(core_index, total[:PACK_ROWS], total[PACK_ROWS:])
    low, high = order(core_index, mine, swap(sent, "c"))
    rows_of = lambda name: ((flat[name].shape[0], 128), F32, "v")
    skip_out, triple_out, expand_out, contract_out, merge_out, vector_out = call(
        unpack_kernel,
        "by_weight",
        [(low, "v"), (high, "v")],
        [rows_of(name) for name in NAMES] + [((1, 128), F32, "v")],
        [],
        1e6,
        8,
    )
    vector_out = vector_out[0]
    spot = lambda j: vector_out[6 * j : 6 * j + 6]
    return (
        output[None],
        input_grad[None],
        skip_grad[None],
        skip_out.reshape(-1),
        spot(0),
        spot(1),
        spot(2),
        triple_out.reshape(-1),
        merge_out.reshape(-1),
        spot(3),
        spot(4),
        spot(5),
        expand_out.reshape(-1),
        vector_out[42:66],
        contract_out.reshape(-1),
        spot(6),
    )


def solution(mesh):
    fine = jax.sharding.Mesh(mesh.devices.reshape(4, 4, 2, 2, 2), ("y", "x", "h", "c", "l"))
    images = ("y", "x", "h", "c")
    everything = images + ("l",)
    tokens, shard = P(images, "l", None), P(everything)
    return jax.shard_map(
        per_device,
        mesh=fine,
        in_specs=(tokens,) * 3 + (P(images),) * 2 + (P(),) * 2 + (shard,) * 13,
        out_specs=(tokens,) * 3 + (shard,) * 13,
        check_vma=False,
    )
```

```python
import functools
import math

import jax
import jax.numpy as jnp
import numpy as np
from jax import lax
from jax.experimental import pallas as pl
from jax.experimental.pallas import tpu as pltpu
from jax.sharding import PartitionSpec as P

D = 768
HEADS = 12
HEAD_DIM = 64
FF = 3072
HALF = D // 2
STRIPS = FF // D
TOKENS = 129
PAD = 144
KEYS = 2 * PAD
PLANES = 16
PLANE = ("y", "x")
COLUMN = ("h", "c", "l")
SKIP, SPOTS, TRIPLE = 0, 96, 112
EXPAND, CONTRACT, MERGE = 0, 192, 384
FIRST_ROWS, SECOND_ROWS = 256, 432
ONE_ROWS = 112
TWO_SHARE, TWO_GROUP = 3 * D // 4, 48
EARLY_ROWS = 448
FIRST_PACK, SECOND_PACK = (12, 1, 6, 6, 6), (6, 6, 6, 6, 24, 6)
PACK = FIRST_PACK + SECOND_PACK
PACK_ROWS = 88
NAMES = ("skip", "triple", "expand", "contract", "merge")
SUM_ROWS = ONE_ROWS + EARLY_ROWS
SUM_STARTS = (0, 96, None, None, None) + tuple(ONE_ROWS + at for at in (0, 48, 96, 144, 192, 384))
epsilon = 1e-05
score_scale = 1.0 / math.sqrt(HEAD_DIM)
BF, F32 = jnp.bfloat16, jnp.float32
ATTEND = FF + FF // 2
NORMED = ATTEND + HALF
GIFT = NORMED + D


def mm(left, right):
    return jnp.dot(left, right, preferred_element_type=F32)


def mm_t(left, right):
    return lax.dot_general(left, right, (((1,), (1,)), ((), ())), preferred_element_type=F32)


def t_mm(left, right):
    return lax.dot_general(left, right, (((0,), (0,)), ((), ())), preferred_element_type=F32)


def order(core, one, two):
    return jnp.where(core == 0, one, two), jnp.where(core == 0, two, one)


def split(core, block):
    return order(core, block[:, :HALF], block[:, HALF:])


def norm_stats(values):
    mean_value = jnp.mean(values, axis=-1, keepdims=True)
    centered = values - mean_value
    variance = jnp.mean(centered * centered, axis=-1, keepdims=True)
    inverse = lax.rsqrt(variance + epsilon)
    return centered * inverse, inverse


def norm_backward(incoming, scaled, inverse, gain):
    weighted = incoming * gain
    first_mean = jnp.mean(weighted, axis=-1, keepdims=True)
    second_mean = jnp.mean(weighted * scaled, axis=-1, keepdims=True)
    value_grad = inverse * (weighted - first_mean - scaled * second_mean)
    return (
        value_grad,
        jnp.sum(incoming * scaled, axis=0, keepdims=True),
        jnp.sum(incoming, axis=0, keepdims=True),
    )


def padded(block):
    return jnp.concatenate([block, jnp.zeros((PAD - TOKENS, block.shape[1]), block.dtype)], axis=0)


def load(pairs, sems):
    copies = [pltpu.make_async_copy(s, d, sems.at[k]) for k, (s, d) in enumerate(pairs)]
    for copy in copies:
        copy.start()
    return copies


def matrix(ref, at, rows):
    return ref[:, at : at + rows, :].reshape(PLANES * rows, HALF)


def spot_masks(width):
    lanes = lax.broadcasted_iota(jnp.int32, (128, D), 0)
    spots = lax.broadcasted_iota(jnp.int32, (128, D), 1)
    return lanes, lax.rem(spots, width), lax.div(spots, width)


def steps_to(place_ref, plane):
    return (plane // 4 - place_ref[1]) & 3, (plane % 4 - place_ref[2]) & 3


def wait(copies):
    for copy in copies:
        copy.wait()


def tiles_of(matrix_name):
    count, strips, across = {"skip": (6, 1, 6), "triple": (18, 1, 6), "merge": (6, 1, 6), "expand": (24, STRIPS, 24), "contract": (6, 1, 6)}[matrix_name]
    for tile in range(count):
        block, inside = divmod(tile, across)
        half, rest = divmod(inside, across // 2)
        yield tile, half, block + rest // 3, rest % 3


def pack_kernel(*refs):
    count = len(NAMES)
    sources, (row_ref, out_ref, rows_ref), scratch = refs[:count], refs[count : count + 3], refs[count + 3 :]
    low, scratch, sems = scratch[:count], scratch[count : 2 * count], scratch[2 * count]
    copies = load(list(zip(sources, low)), sems)
    at = 0
    for name, held, ref, copy in zip(NAMES, scratch, low, copies):
        copy.wait()
        held[...] = ref[...].astype(F32)
        tiles = list(tiles_of(name))
        rows = held.shape[0] // len(tiles)
        for tile, half, strip, spot in tiles:
            first = at + strip * rows
            rows_ref[half, first : first + rows, 128 * spot : 128 * spot + 128] = held[pl.ds(tile, rows, stride=len(tiles)), :]
        at += rows * (1 + max(t[2] for t in tiles))
        if name == "skip":
            rows_ref[0, at : at + 1, :] = row_ref[...]
            rows_ref[1, at : at + 1, :] = row_ref[...]
            at += 1
    rows_ref[:, at:PACK_ROWS, :] = jnp.zeros((2, PACK_ROWS - at, HALF), F32)
    for half in range(2):
        packed = rows_ref[half].astype(BF)
        for device in range(8):
            if device // 2 % 2 == half:
                out_ref[device] = packed


def unpack_kernel(low_ref, high_ref, *refs):
    outs = dict(zip(NAMES, refs))
    at = 0
    for name in NAMES:
        tiles = list(tiles_of(name))
        rows = outs[name].shape[0] // len(tiles)
        for tile, half, strip, spot in tiles:
            first = at + strip * rows
            source = high_ref if half else low_ref
            outs[name][pl.ds(tile, rows, stride=len(tiles)), :] = source[first : first + rows, 128 * spot : 128 * spot + 128]
        at += rows * (1 + max(t[2] for t in tiles))
        if name == "skip":
            refs[5][...] = low_ref[at : at + 1, :128] + high_ref[at : at + 1, :128]
            at += 1


def prepare_kernel(core_ref, scale_ref, in_ref, skip_ref, cotangent_ref, after_ref, gift_ref):
    gift_ref[:, :D] = padded(in_ref[...])
    gift_ref[:, D : 2 * D] = padded(skip_ref[...])
    after = padded(cotangent_ref[...].astype(F32) * scale_ref[0]).astype(BF)
    after_ref[...] = after
    gift_ref[:, 2 * D :] = split(core_ref[0], after)[1]


def spots_kernel(first_ref, out_ref, rows_ref, sems):
    wait(load([(first_ref.at[:, SPOTS : SPOTS + 16, :], rows_ref)], sems))
    held = rows_ref[:, :, :128].astype(F32)[:, :8].reshape(128, 128).astype(BF)
    for j in range(7):
        lanes, place, owner = spot_masks(6)
        one_hot = (lanes - 6 * j == place).astype(BF)
        spread = jnp.where(owner == lanes, mm(held, one_hot), 0.0)
        out_ref[j : j + 1, :] = jnp.sum(spread, axis=0, keepdims=True)
    out_ref[7:8, :] = jnp.zeros((1, D), F32)
    lanes, place, owner = spot_masks(24)
    spread = mm(held, (lanes - 42 == place).astype(BF))
    for m in range(STRIPS):
        out_ref[8 + m : 9 + m, :] = jnp.sum(jnp.where(owner + 32 * m == lanes, spread, 0.0), axis=0, keepdims=True)
    out_ref[12:16, :] = jnp.zeros((4, D), F32)


def first_kernel(core_ref, joined_ref, own_ref, other_ref, spots_ref, united_ref, normed_ref, query_ref, pair_ref, so, ss, to, ts, sems):
    core = core_ref[0]
    copies = load(
        [
            (own_ref.at[:, SKIP : SKIP + 96, :], so),
            (other_ref.at[:, SKIP : SKIP + 96, :], ss),
            (own_ref.at[:, TRIPLE : TRIPLE + 144, :], to),
            (other_ref.at[:, TRIPLE : TRIPLE + 144, :], ts),
        ],
        sems,
    )
    joined = joined_ref[:, : 2 * D]
    copies[0].wait()
    one = mm(joined, matrix(so, 0, 96))
    copies[1].wait()
    two = mm(joined, matrix(ss, 0, 96))
    united = jnp.concatenate(order(core, one, two), axis=1) + spots_ref[0:1, :]
    united_ref[...] = united
    scaled, _ = norm_stats(united)
    normed = (scaled * spots_ref[1:2, :] + spots_ref[2:3, :]).astype(BF)
    normed_ref[...] = normed
    copies[2].wait()
    copies[3].wait()
    for k in range(3):
        one = mm(normed, matrix(to, 48 * k, 48))
        two = mm(normed, matrix(ts, 48 * k, 48))
        block = jnp.concatenate(order(core, one, two), axis=1).astype(BF)
        if k == 0:
            query_ref[...] = block
        else:
            pair_ref[:, (k - 1) * D : k * D] = block


def key_mask():
    spots = lax.broadcasted_iota(jnp.int32, (1, KEYS), 1)
    return (spots < TOKENS) | ((spots >= PAD) & (spots < PAD + TOKENS))


def attend_kernel(query_ref, pair_ref, came_ref, mixed_ref, total_ref):
    mask = key_mask()
    total_ref[...] = jnp.zeros((PAD, 128), F32)
    for pair in range(HEADS // 2):
        at = slice(128 * pair, 128 * pair + 128)
        late = slice(D + 128 * pair, D + 128 * pair + 128)
        query = query_ref[:, at]
        keys = jnp.concatenate([pair_ref[:, at], came_ref[:, at]], axis=0)
        values = jnp.concatenate([pair_ref[:, late], came_ref[:, late]], axis=0)
        done = []
        for side in range(2):
            head = slice(HEAD_DIM * side, HEAD_DIM * side + HEAD_DIM)
            scores = mm_t(query[:, head], keys[:, head]) * score_scale
            scores = jnp.where(mask, scores, -1e30)
            largest = jnp.max(scores, axis=-1, keepdims=True)
            powered = jnp.exp(scores - largest)
            totals = jnp.sum(powered, axis=-1, keepdims=True)
            total_ref[:, 2 * pair + side : 2 * pair + side + 1] = largest + jnp.log(totals)
            soft_low = (powered / totals).astype(BF)
            done.append(mm(soft_low, values[:, head]))
        mixed_ref[:, at] = jnp.concatenate(done, axis=1).astype(BF)


def forward_kernel(core_ref, scale_ref, mixed_ref, united_ref, cotangent_ref, after_ref, own_ref, other_ref, spots_ref, out_ref, middle_grad_ref, vector_ref, gift_ref, kept_ref, eo, es, co, cs, mo, ms, slope_ref, low_ref, sems):
    core = core_ref[0]
    copies = load(
        [
            (own_ref.at[:, MERGE : MERGE + 48, :], mo),
            (other_ref.at[:, MERGE : MERGE + 48, :], ms),
            *[
                (ref.at[:, 48 * k : 48 * k + 48, :], to.at[:, 48 * k : 48 * k + 48, :])
                for k in range(STRIPS)
                for ref, to in ((own_ref, eo), (other_ref, es))
            ],
            (own_ref.at[:, CONTRACT : CONTRACT + 192, :], co),
            (other_ref.at[:, CONTRACT : CONTRACT + 192, :], cs),
        ],
        sems,
    )
    after = after_ref[...]
    vector_ref[...] = jnp.zeros((16, D), F32)
    vector_ref[6:7, :] = jnp.sum(after.astype(F32), axis=0, keepdims=True)
    after_own, after_other = split(core, after)
    mixed = mixed_ref[...]
    wait(copies[:2])
    one, two = mm(mixed, matrix(mo, 0, 48)), mm(mixed, matrix(ms, 0, 48))
    middle = united_ref[...] + jnp.concatenate(order(core, one, two), axis=1) + spots_ref[3:4, :]
    scaled, inverse = norm_stats(middle)
    normed = (scaled * spots_ref[4:5, :] + spots_ref[5:6, :]).astype(BF)
    gift_ref[:, NORMED:] = normed
    for k in range(STRIPS):
        wait(copies[2 + 2 * k : 4 + 2 * k])
        one, two = order(core, mm(normed, matrix(eo, 48 * k, 48)), mm(normed, matrix(es, 48 * k, 48)))
        for side, block in ((0, one), (1, two)):
            at = side * STRIPS * HALF + k * HALF
            bias = spots_ref[8 + at // D : 9 + at // D, at % D : at % D + HALF]
            block = block + bias
            cumulative = 0.5 * (1.0 + lax.erf(block * (1.0 / math.sqrt(2.0))))
            density = jnp.exp(-0.5 * block * block) * (1.0 / math.sqrt(2.0 * math.pi))
            gift_ref[:, at : at + HALF] = (block * cumulative).astype(BF)
            slope_ref[:, at : at + HALF] = cumulative + block * density
    wait(copies[2 + 2 * STRIPS :])
    active = gift_ref[:, :FF]
    one, two = mm(active, matrix(co, 0, 192)), mm(active, matrix(cs, 0, 192))
    output = middle + jnp.concatenate(order(core, one, two), axis=1) + spots_ref[6:7, :]
    out_ref[...] = output[:TOKENS].astype(BF)
    for j in range(2 * STRIPS):
        at, planes = slice(HALF * j, HALF * j + HALF), slice(2 * j, 2 * j + 2)
        back = mm_t(after_own, co[planes, :, :].reshape(HALF, HALF)) + mm_t(after_other, cs[planes, :, :].reshape(HALF, HALF))
        low = (back * slope_ref[:, at]).astype(BF)
        low_ref[:, at] = low
        row = 8 + j // 2
        vector_ref[row : row + 1, HALF * (j % 2) : HALF * (j % 2) + HALF] = jnp.sum(low.astype(F32), axis=0, keepdims=True)
    incoming = jnp.zeros((PAD, D), F32)
    for k in range(STRIPS):
        one, two = order(
            core,
            low_ref[:, k * HALF : (k + 1) * HALF],
            low_ref[:, (STRIPS + k) * HALF : (STRIPS + k + 1) * HALF],
        )
        kept_ref[:, k * HALF : (k + 1) * HALF] = one
        gift_ref[:, FF + k * HALF : FF + (k + 1) * HALF] = two
        incoming = incoming + mm_t(one, matrix(eo, 48 * k, 48)) + mm_t(two, matrix(es, 48 * k, 48))
    back_two, gain_grad, shift_grad = norm_backward(incoming, scaled, inverse, spots_ref[4:5, :])
    vector_ref[4:5, :] = gain_grad
    vector_ref[5:6, :] = shift_grad
    middle_grad = padded(cotangent_ref[...].astype(F32) * scale_ref[0]) + back_two
    middle_grad_ref[...] = middle_grad
    attend = middle_grad.astype(BF)
    vector_ref[3:4, :] = jnp.sum(attend.astype(F32), axis=0, keepdims=True)
    gift_ref[:, ATTEND:NORMED] = split(core, attend)[1]


def early_kernel(core_ref, gift_any, came_any, kept_any, after_ref, first_came_any, mixed_any, mixed_came_any, middle_grad_any, grad_ref, gift_ref, came_ref, kept_ref, after_came_ref, mixed_ref, mixed_came_ref, middle_grad_ref, go, sems, out_sems):
    core = core_ref[0]
    copies = load(
        [
            (gift_any.at[:, :FF], gift_ref.at[:, :FF]),
            (came_any.at[:, :FF], came_ref.at[:, :FF]),
            (first_came_any.at[:, 2 * D :], after_came_ref),
            (gift_any.at[:, NORMED:], gift_ref.at[:, NORMED:]),
            (came_any.at[:, FF:], came_ref.at[:, FF:]),
            (kept_any, kept_ref),
            (mixed_any, mixed_ref),
            (mixed_came_any, mixed_came_ref),
            (middle_grad_any, middle_grad_ref),
        ],
        sems,
    )
    wait(copies[:3])
    after, after_came = split(core, after_ref[...])[0], after_came_ref[...]
    for j in range(2 * STRIPS):
        at, planes = slice(HALF * j, HALF * j + HALF), slice(2 * j, 2 * j + 2)
        grad = t_mm(gift_ref[:, at], after) + t_mm(came_ref[:, at], after_came)
        go[planes, CONTRACT : CONTRACT + 192, :] = grad.astype(BF).reshape(2, 192, HALF)
    rows = lambda at, to: (go.at[:, at:to, :], grad_ref.at[:, at:to, :])
    sends = load([rows(CONTRACT, CONTRACT + 192)], out_sems)
    wait(copies[3:])
    attend = split(core, middle_grad_ref[...].astype(BF))[0]
    grad = t_mm(mixed_ref[...], attend) + t_mm(mixed_came_ref[...], came_ref[:, ATTEND:NORMED])
    go[:, MERGE : MERGE + 48, :] = grad.astype(BF).reshape(PLANES, 48, HALF)
    go[:, MERGE + 48 :, :] = jnp.zeros((PLANES, EARLY_ROWS - MERGE - 48, HALF), BF)
    sends += load([rows(MERGE, EARLY_ROWS)], out_sems.at[1:])
    normed, normed_came = gift_ref[:, NORMED:], came_ref[:, NORMED:]
    for k in range(STRIPS):
        grad = t_mm(normed, kept_ref[:, k * HALF : (k + 1) * HALF]) + t_mm(
            normed_came, came_ref[:, FF + k * HALF : FF + (k + 1) * HALF]
        )
        go[:, EXPAND + 48 * k : EXPAND + 48 * (k + 1), :] = grad.astype(BF).reshape(PLANES, 48, HALF)
        sends += load([rows(EXPAND + 48 * k, EXPAND + 48 * (k + 1))], out_sems.at[2 + k :])
    wait(sends)


def backward_kernel(core_ref, middle_grad_ref, query_ref, pair_ref, came_ref, total_ref, own_ref, other_ref, query_grad_ref, pair_grad_ref, sent_ref, mixed_grad_ref, mo, ms, sems):
    core = core_ref[0]
    copies = load(
        [(own_ref.at[:, MERGE : MERGE + 48, :], mo), (other_ref.at[:, MERGE : MERGE + 48, :], ms)], sems
    )
    attend_own, attend_other = split(core, middle_grad_ref[...].astype(BF))
    mask = key_mask()
    copies[0].wait()
    copies[1].wait()
    mixed_grad_ref[...] = (mm_t(attend_own, matrix(mo, 0, 48)) + mm_t(attend_other, matrix(ms, 0, 48))).astype(BF)
    for pair in range(HEADS // 2):
        at = slice(128 * pair, 128 * pair + 128)
        late = slice(D + 128 * pair, D + 128 * pair + 128)
        query, mixed_grad = query_ref[:, at], mixed_grad_ref[:, at]
        keys = jnp.concatenate([pair_ref[:, at], came_ref[:, at]], axis=0)
        values = jnp.concatenate([pair_ref[:, late], came_ref[:, late]], axis=0)
        query_parts, key_parts, value_parts = [], [], []
        for side in range(2):
            head = slice(HEAD_DIM * side, HEAD_DIM * side + HEAD_DIM)
            scores = mm_t(query[:, head], keys[:, head]) * score_scale
            scores = jnp.where(mask, scores, -1e30)
            soft = jnp.exp(scores - total_ref[:, 2 * pair + side : 2 * pair + side + 1])
            soft_grad = mm_t(mixed_grad[:, head], values[:, head])
            inner = jnp.sum(soft * soft_grad, axis=-1, keepdims=True)
            scores_grad = (soft * (soft_grad - inner)).astype(BF)
            query_parts.append(mm(scores_grad, keys[:, head]))
            key_parts.append(t_mm(scores_grad, query[:, head]))
            value_parts.append(t_mm(soft.astype(BF), mixed_grad[:, head]))
        query_grad_ref[:, at] = (jnp.concatenate(query_parts, axis=1) * score_scale).astype(BF)
        key_grad = jnp.concatenate(key_parts, axis=1) * score_scale
        value_grad = jnp.concatenate(value_parts, axis=1)
        pair_grad_ref[:, at] = key_grad[:PAD]
        pair_grad_ref[:, late] = value_grad[:PAD]
        sent_ref[:, at] = key_grad[PAD:].astype(BF)
        sent_ref[:, late] = value_grad[PAD:].astype(BF)


def scatter(place_ref, ref, block, at, by_y):
    rows = block.shape[0] // PLANES
    for plane in range(PLANES):
        step_y, step_x = steps_to(place_ref, plane)
        spot = 4 * step_y + step_x if by_y else 4 * step_x + step_y
        ref[spot, at : at + rows, :] = block[plane * rows : (plane + 1) * rows]


def vector_rows(vectors, places):
    rows = jnp.zeros((128, 128), F32)
    for vector, at in zip(vectors, places):
        lanes, place, owner = spot_masks(6)
        spread = jnp.where(owner == lanes, vector, 0.0).astype(BF)
        rows = rows + mm_t(spread, (lanes - at == place).astype(BF))
    return rows


def query_kernel(core_ref, query_grad_ref, early_ref, normed_ref, normed_came_ref, by_z_ref, own_ref, other_ref, incoming_ref, rows_ref, moved_ref, moved_came_ref, to, ts, sems):
    copies = load(
        [(own_ref.at[:, TRIPLE : TRIPLE + 48, :], to), (other_ref.at[:, TRIPLE : TRIPLE + 48, :], ts)], sems
    )
    rows = vector_rows([early_ref[j : j + 1, :] for j in range(3, 7)], (18, 24, 30, 36))
    lanes, place, owner = spot_masks(24)
    for m in range(STRIPS):
        spread = jnp.where(owner + 32 * m == lanes, early_ref[8 + m : 9 + m, :], 0.0).astype(BF)
        rows = rows + mm_t(spread, (lanes - 42 == place).astype(BF))
    rows_ref[...] = rows
    one, two = split(core_ref[0], query_grad_ref[...])
    wait(copies)
    incoming_ref[...] = mm_t(one, matrix(to, 0, 48)) + mm_t(two, matrix(ts, 0, 48))
    moved_ref[...] = mm(normed_ref[...], by_z_ref[...]).astype(BF)
    moved_came_ref[...] = mm(normed_came_ref[...], by_z_ref[...]).astype(BF)


def triple_kernel(core_ref, united_ref, middle_grad_ref, query_grad_ref, pair_grad_ref, came_ref, incoming_ref, own_ref, other_ref, spots_ref, low_ref, vector_ref, kept_ref, gift_ref, to, ts, sems):
    core = core_ref[0]
    copies = load(
        [(own_ref.at[:, TRIPLE + 48 : TRIPLE + 144, :], to), (other_ref.at[:, TRIPLE + 48 : TRIPLE + 144, :], ts)], sems
    )
    scaled, inverse = norm_stats(united_ref[...])
    incoming = incoming_ref[...]
    wait(copies)
    for k in range(3):
        if k == 0:
            block = query_grad_ref[...]
        else:
            at = slice((k - 1) * D, k * D)
            block = (pair_grad_ref[:, at] + came_ref[:, at].astype(F32)).astype(BF)
        one, two = split(core, block)
        kept_ref[:, k * HALF : (k + 1) * HALF] = one
        gift_ref[:, k * HALF : (k + 1) * HALF] = two
        if k:
            incoming = incoming + mm_t(one, matrix(to, 48 * (k - 1), 48)) + mm_t(two, matrix(ts, 48 * (k - 1), 48))
    back_one, gain_grad, shift_grad = norm_backward(incoming, scaled, inverse, spots_ref[1:2, :])
    united_low = (middle_grad_ref[...] + back_one).astype(BF)
    low_ref[...] = united_low
    gift_ref[:, 3 * HALF :] = split(core, united_low)[1]
    vector_ref[0:1, :] = jnp.sum(united_low.astype(F32), axis=0, keepdims=True)
    vector_ref[1:2, :] = gain_grad
    vector_ref[2:3, :] = shift_grad
    vector_ref[3:8, :] = jnp.zeros((5, D), F32)


def skip_kernel(core_ref, low_ref, own_ref, other_ref, in_grad_ref, skip_grad_ref, so, ss, sems):
    copies = load(
        [(own_ref.at[:, SKIP : SKIP + 96, :], so), (other_ref.at[:, SKIP : SKIP + 96, :], ss)], sems
    )
    low_own, low_other = split(core_ref[0], low_ref[...])
    wait(copies)
    for half, grad_ref in ((0, in_grad_ref), (1, skip_grad_ref)):
        planes = slice(8 * half, 8 * half + 8)
        back = mm_t(low_own, so[planes, :, :].reshape(D, HALF)) + mm_t(low_other, ss[planes, :, :].reshape(D, HALF))
        grad_ref[...] = back[:TOKENS].astype(BF)


def late_kernel(place_ref, joined_ref, first_came_ref, normed_ref, normed_came_ref, low_ref, kept_ref, came_ref, early_ref, vector_ref, *refs):
    one_refs, two_refs, (go, gt, sems) = refs[:4], refs[4:8], refs[8:]
    for k in range(3):
        at = slice(k * HALF, (k + 1) * HALF)
        grad = (t_mm(normed_ref[...], kept_ref[:, at]) + t_mm(normed_came_ref[...], came_ref[:, at])).astype(BF)
        for z in range(4):
            gt[(z - place_ref[3]) & 3, 192 * k : 192 * k + 192, :] = grad[192 * z : 192 * z + 192]
    sends = load([(gt.at[k], two_refs[k]) for k in range(4)], sems.at[:4])
    low, low_came = split(place_ref[0], low_ref[...])[0], came_ref[:, 3 * HALF :]
    grad = t_mm(joined_ref[:, : 2 * D], low) + t_mm(first_came_ref[:, : 2 * D], low_came)
    scatter(place_ref, go, grad.astype(BF), SKIP, False)
    rows = early_ref[...] + vector_rows([vector_ref[j : j + 1, :] for j in range(3)], (0, 6, 12))
    rows = jnp.concatenate([rows.reshape(PLANES, 8, 128), jnp.zeros((PLANES, 8, 128), F32)], axis=1)
    rows = jnp.concatenate([rows, jnp.zeros((PLANES, 16, HALF - 128), F32)], axis=2)
    scatter(place_ref, go, rows.reshape(PLANES * 16, HALF).astype(BF), 96, False)
    wait(sends)
    wait(load([(go.at[4 * k : 4 * k + 4], one_refs[k]) for k in range(4)], sems.at[4:]))


def group_kernel(place_ref, share_ref, moves_ref, *refs):
    outs, rows_ref = refs[:4], refs[4]
    rows_ref[...] = mm(moves_ref[...], share_ref[...]).astype(BF).reshape(PLANES, TWO_GROUP, HALF)
    for k, out_ref in enumerate(outs):
        for n in range(4):
            out_ref[n] = rows_ref[4 * ((place_ref[1] + n) & 3) + ((place_ref[2] + k) & 3)]


def moves_of(rows, columns, pairs):
    moves = np.zeros((rows, columns), np.float32)
    for row, column in pairs:
        moves[row, column] = 1.0
    return moves


def features_by_z():
    return moves_of(
        D,
        D,
        (
            (48 * p + 24 * h + 12 * c + 6 * l + r, 192 * (2 * h + l) + 12 * p + 6 * c + r)
            for p in range(PLANES)
            for h in range(2)
            for c in range(2)
            for l in range(2)
            for r in range(6)
        ),
    )


def rows_by_group():
    return moves_of(
        PLANES * TWO_GROUP,
        TWO_SHARE,
        ((TWO_GROUP * p + 12 * k + r, 192 * k + 12 * p + r) for p in range(PLANES) for k in range(3) for r in range(12)),
    )


def rows_by_core():
    return moves_of(
        2 * PACK_ROWS,
        TWO_GROUP,
        ((PACK_ROWS * c + 13 + 6 * k + r, 12 * k + 6 * c + r) for c in range(2) for k in range(3) for r in range(6)),
    )


def column_kernel(place_ref, one_ref, early_ref, moves_ref, *refs):
    out_refs, (rows_ref, moved_ref) = refs[:4], refs[4:]
    rows_ref[:ONE_ROWS] = one_ref[...]
    rows_ref[ONE_ROWS:] = early_ref[...]
    moved_ref[...] = mm(moves_ref[...], rows_ref[...]).astype(BF).reshape(4, 2 * PACK_ROWS, HALF)
    for k, out_ref in enumerate(out_refs):
        out_ref[...] = moved_ref[(place_ref[3] + k) & 3]


def column_moves():
    moves = np.zeros((8 * PACK_ROWS, SUM_ROWS), np.float32)
    for high in range(2):
        for low in range(2):
            for core in range(2):
                at = ((2 * high + low) * 2 + core) * PACK_ROWS
                device = (2 * high + core) * 2 + low
                for rows, start in zip(PACK, SUM_STARTS):
                    for row in range(rows if start is not None else 0):
                        moves[at + row, start + device * rows + row] = 1.0
                    at += rows
    return moves


def call(kernel, name, args, outs, scratch, flops, room):
    place = {
        "s": pl.BlockSpec(memory_space=pltpu.SMEM),
        "v": pl.BlockSpec(memory_space=pltpu.VMEM),
        "a": pl.BlockSpec(memory_space=pl.ANY),
    }
    moved = sum(a.size * a.dtype.itemsize for a, _ in args)
    return pl.pallas_call(
        kernel,
        out_shape=[jax.ShapeDtypeStruct(shape, dtype) for shape, dtype, _ in outs],
        in_specs=[place[w] for _, w in args],
        out_specs=[place[w] for _, _, w in outs],
        scratch_shapes=scratch,
        compiler_params=pltpu.CompilerParams(vmem_limit_bytes=room * 2**20),
        cost_estimate=pl.CostEstimate(flops=int(flops), bytes_accessed=int(moved), transcendentals=0),
        name=name,
    )(*[a for a, _ in args])


def swap(block, axis):
    return lax.ppermute(block, axis, [(0, 1), (1, 0)])


def step(block, axis, steps):
    return lax.ppermute(block, axis, [((i + steps) % 4, i) for i in range(4)])


def sum_line(blocks, axis):
    total = blocks[0].astype(F32)
    for k in (1, 2, 3):
        total = total + step(blocks[k], axis, 4 - k).astype(F32)
    return total


def sum_part(blocks, first, second):
    line = blocks[0].astype(F32)
    for k in (1, 2, 3):
        line = line + step(blocks[k], first, 4 - k).astype(F32)
    total = line[0]
    for k in (1, 2, 3):
        total = total + step(line[k].astype(BF), second, 4 - k).astype(F32)
    return total.astype(BF)


def regroup(block, pack):
    at, parts = 0, []
    for rows in pack:
        parts.append(block[:, at : at + rows].reshape(-1, HALF))
        at += rows
    return parts


def pick_table(indices, table):
    match = indices[:, None] == jnp.arange(table.shape[0], dtype=jnp.int32)[None, :]
    return jnp.sum(jnp.where(match, table[None, :], 0.0), axis=1)


def per_device(
    inputs,
    skipped,
    cotangent,
    timestep,
    class_ids,
    time_weight,
    class_weight,
    skip_weight,
    skip_bias,
    first_gain,
    first_shift,
    triple_weight,
    merge_weight,
    merge_bias,
    second_gain,
    second_shift,
    expand_weight,
    expand_bias,
    contract_weight,
    contract_bias,
):
    core_index = lax.axis_index("c").astype(jnp.int32)
    core = core_index[None]
    place = jnp.stack([core_index] + [lax.axis_index(axis).astype(jnp.int32) for axis in ("y", "x", ("h", "l"))])


    inputs, skipped, cotangent = (a.reshape(TOKENS, D) for a in (inputs, skipped, cotangent))
    sem = pltpu.SemaphoreType.DMA
    weight = lambda rows: pltpu.VMEM((PLANES, rows, HALF), BF)
    tokens = lambda width, dtype=BF, where="v": ((PAD, width), dtype, where)
    plane = lambda rows: ((PLANES, rows, HALF), BF, "a")

    vectors = (skip_bias, first_gain, first_shift, merge_bias, second_gain, second_shift, contract_bias, expand_bias)
    row, at = jnp.zeros((1, HALF), F32), 0
    for vector in vectors:
        row = row + jnp.pad(vector.astype(F32)[None, :], ((0, 0), (at, HALF - at - vector.shape[0])))
        at += vector.shape[0]
    flat = dict(
        skip=skip_weight, triple=triple_weight, merge=merge_weight, expand=expand_weight, contract=contract_weight
    )
    flat = {name: a.reshape(-1, 128) for name, a in flat.items()}

    (packed,) = call(
        pack_kernel,
        "pack",
        [(flat[n], "a") for n in NAMES] + [(row, "v")],
        [((8, PACK_ROWS, HALF), BF, "v")],
        [pltpu.VMEM((2, PACK_ROWS, HALF), F32)]
        + [pltpu.VMEM(flat[n].shape, dtype) for dtype in (BF, F32) for n in NAMES]
        + [sem((len(NAMES),))],
        1e6,
        58,
    )
    column = regroup(lax.all_to_all(packed, COLUMN, 0, 0, tiled=True), PACK)
    first = jnp.concatenate(column[:2] + [jnp.zeros((8, HALF), BF)] + column[2:5], axis=0)
    second = jnp.concatenate(column[5:], axis=0)
    second_own = lax.all_gather(second, PLANE, axis=0, tiled=True).reshape(PLANES, SECOND_ROWS, HALF)
    first_own = lax.all_to_all(
        jnp.broadcast_to(first[None], (PLANES, FIRST_ROWS, HALF)), PLANE, 0, 0, tiled=True
    )
    first_own, timestep = lax.optimization_barrier((first_own, timestep))
    scale = pick_table(timestep, time_weight) * pick_table(class_ids, class_weight)
    first_other = swap(first_own, "c")
    after, gift = call(
        prepare_kernel,
        "prepare",
        [(core, "s"), (scale, "s"), (inputs, "v"), (skipped, "v"), (cotangent, "v")],
        [tokens(D), tokens(2 * D + HALF)],
        [],
        1e6,
        8,
    )
    gift_came = swap(gift, "c")

    (spots,) = call(
        spots_kernel, "vectors", [(first_own, "a")], [((16, D), F32, "v")], [weight(16), sem((1,))], 2e8, 8
    )
    united, normed, query, pair = call(
        first_kernel,
        "skip_and_triple",
        [(core, "s"), (gift, "v"), (first_own, "a"), (first_other, "a"), (spots, "v")],
        [tokens(D, F32), tokens(D), tokens(D), tokens(2 * D)],
        [weight(96), weight(96), weight(144), weight(144), sem((4,))],
        2 * PAD * D * (2 * D + 3 * D),
        16,
    )
    pair, gift_came = lax.optimization_barrier((pair, gift_came))
    pair_came = swap(pair, "l")
    normed_came = swap(normed, "c")
    second_own, pair_came, normed_came = lax.optimization_barrier((second_own, pair_came, normed_came))
    second_other = swap(second_own, "c")
    mixed, totals = call(
        attend_kernel,
        "attention",
        [(query, "v"), (pair, "v"), (pair_came, "v")],
        [tokens(D), tokens(128, F32)],
        [],
        2 * PAD * D * 2 * KEYS,
        58,
    )
    mixed_came = swap(mixed, "c")
    mixed, mixed_came = lax.optimization_barrier((mixed, mixed_came))
    output, middle_grad, early_vectors, forward_gift, forward_kept = call(
        forward_kernel,
        "feed_forward",
        [
            (core, "s"),
            (scale, "s"),
            (mixed, "v"),
            (united, "v"),
            (cotangent, "v"),
            (after, "v"),
            (second_own, "a"),
            (second_other, "a"),
            (spots, "v"),
        ],
        [((TOKENS, D), BF, "v"), tokens(D, F32), ((16, D), F32, "v"), tokens(GIFT), tokens(FF // 2)],
        [weight(192)] * 4
        + [weight(48)] * 2
        + [pltpu.VMEM((PAD, FF), F32), pltpu.VMEM((PAD, FF), BF), sem((12,))],
        2 * PAD * D * FF * 4,
        58,
    )
    forward_came = swap(forward_gift, "c")
    query_grad, pair_grad, pair_sent = call(
        backward_kernel,
        "attention_backward",
        [
            (core, "s"),
            (middle_grad, "v"),
            (query, "v"),
            (pair, "v"),
            (pair_came, "v"),
            (totals, "v"),
            (second_own, "a"),
            (second_other, "a"),
        ],
        [tokens(D), tokens(2 * D, F32), tokens(2 * D)],
        [pltpu.VMEM((PAD, D), BF), weight(48), weight(48), sem((2,))],
        2 * PAD * D * (D + 5 * KEYS),
        58,
    )
    grad_came = swap(pair_sent, "l")
    (early_grads,) = call(
        early_kernel,
        "early_gradients",
        [
            (core, "s"),
            (forward_gift, "a"),
            (forward_came, "a"),
            (forward_kept, "a"),
            (after, "v"),
            (gift_came, "a"),
            (mixed, "a"),
            (mixed_came, "a"),
            (middle_grad, "a"),
        ],
        [plane(EARLY_ROWS)],
        [pltpu.VMEM((PAD, GIFT), BF)] * 2
        + [pltpu.VMEM((PAD, width), BF) for width in (FF // 2, HALF, D, D)]
        + [pltpu.VMEM((PAD, D), F32), weight(EARLY_ROWS), sem((9,)), sem((6,))],
        2 * PAD * D * FF * 2,
        58,
    )
    early_sum = lax.psum_scatter(early_grads.reshape(PLANES * EARLY_ROWS, HALF), PLANE, scatter_dimension=0, tiled=True)
    early_vectors, query_grad = lax.optimization_barrier((early_vectors, query_grad))
    by_z = jnp.asarray(features_by_z(), BF)
    query_incoming, early_rows, moved, moved_came = call(
        query_kernel,
        "query_backward",
        [
            (core, "s"),
            (query_grad, "v"),
            (early_vectors, "v"),
            (normed, "v"),
            (normed_came, "v"),
            (by_z, "v"),
            (first_own, "a"),
            (first_other, "a"),
        ],
        [tokens(D, F32), ((128, 128), F32, "v"), tokens(D), tokens(D)],
        [weight(48)] * 2 + [sem((2,))],
        2 * PAD * D * D,
        24,
    )
    united_low, late_vectors, triple_kept, late_gift = call(
        triple_kernel,
        "triple_backward",
        [
            (core, "s"),
            (united, "v"),
            (middle_grad, "v"),
            (query_grad, "v"),
            (pair_grad, "v"),
            (grad_came, "v"),
            (query_incoming, "v"),
            (first_own, "a"),
            (first_other, "a"),
            (spots, "v"),
        ],
        [tokens(D), ((8, D), F32, "v"), tokens(3 * HALF), tokens(4 * HALF)],
        [weight(96)] * 2 + [sem((2,))],
        2 * PAD * D * (2 * D),
        16,
    )
    late_came = swap(late_gift, "c")
    input_grad, skip_grad = call(
        skip_kernel,
        "skip_backward",
        [(core, "s"), (united_low, "v"), (first_own, "a"), (first_other, "a")],
        [((TOKENS, D), BF, "v"), ((TOKENS, D), BF, "v")],
        [weight(96), weight(96), sem((2,))],
        2 * PAD * D * (2 * D),
        12,
    )
    late_came, input_grad, skip_grad = lax.optimization_barrier((late_came, input_grad, skip_grad))
    late = call(
        late_kernel,
        "late_gradients",
        [
            (place, "s"),
            (gift, "v"),
            (gift_came, "v"),
            (moved, "v"),
            (moved_came, "v"),
            (united_low, "v"),
            (triple_kept, "v"),
            (late_came, "v"),
            (early_rows, "v"),
            (late_vectors, "v"),
        ],
        [((4, ONE_ROWS, HALF), BF, "a")] * 4 + [((TWO_SHARE, HALF), BF, "a")] * 4,
        [weight(ONE_ROWS), pltpu.VMEM((4, TWO_SHARE, HALF), BF), sem((8,))],
        2 * PAD * D * (5 * D),
        58,
    )
    one_sum = sum_part(late[:4], "x", "y")
    share = sum_line(late[4:], ("h", "l")).astype(BF)
    groups = call(
        group_kernel,
        "by_group",
        [(place, "s"), (share, "v"), (jnp.asarray(rows_by_group(), BF), "v")],
        [((4, TWO_GROUP, HALF), BF, "v")] * 4,
        [pltpu.VMEM((PLANES, TWO_GROUP, HALF), BF)],
        2 * PLANES * TWO_GROUP * TWO_SHARE * HALF,
        12,
    )
    two_sum = mm(jnp.asarray(rows_by_core(), BF), sum_part(groups, "x", "y"))

    early_sum, two_sum = lax.optimization_barrier((early_sum, two_sum))

    column = call(
        column_kernel,
        "by_device",
        [(place, "s"), (one_sum, "v"), (early_sum, "v"), (jnp.asarray(column_moves(), BF), "v")],
        [((2 * PACK_ROWS, HALF), BF, "v")] * 4,
        [pltpu.VMEM((SUM_ROWS, HALF), BF), pltpu.VMEM((4, 2 * PACK_ROWS, HALF), BF)],
        2 * SUM_ROWS * SUM_ROWS * HALF,
        12,
    )
    total = sum_line(column, ("h", "l")) + two_sum
    mine, sent = order(core_index, total[:PACK_ROWS], total[PACK_ROWS:])
    low, high = order(core_index, mine, swap(sent, "c"))
    rows_of = lambda name: ((flat[name].shape[0], 128), F32, "v")
    skip_out, triple_out, expand_out, contract_out, merge_out, vector_out = call(
        unpack_kernel,
        "by_weight",
        [(low, "v"), (high, "v")],
        [rows_of(name) for name in NAMES] + [((1, 128), F32, "v")],
        [],
        1e6,
        8,
    )
    vector_out = vector_out[0]
    spot = lambda j: vector_out[6 * j : 6 * j + 6]
    return (
        output[None],
        input_grad[None],
        skip_grad[None],
        skip_out.reshape(-1),
        spot(0),
        spot(1),
        spot(2),
        triple_out.reshape(-1),
        merge_out.reshape(-1),
        spot(3),
        spot(4),
        spot(5),
        expand_out.reshape(-1),
        vector_out[42:66],
        contract_out.reshape(-1),
        spot(6),
    )


def solution(mesh):
    fine = jax.sharding.Mesh(mesh.devices.reshape(4, 4, 2, 2, 2), ("y", "x", "h", "c", "l"))
    images = ("y", "x", "h", "c")
    everything = images + ("l",)
    tokens, shard = P(images, "l", None), P(everything)
    return jax.shard_map(
        per_device,
        mesh=fine,
        in_specs=(tokens,) * 3 + (P(images),) * 2 + (P(),) * 2 + (shard,) * 13,
        out_specs=(tokens,) * 3 + (shard,) * 13,
        check_vma=False,
    )
```

```python
import functools
import math

import jax
import jax.numpy as jnp
import numpy as np
from jax import lax
from jax.experimental import pallas as pl
from jax.experimental.pallas import tpu as pltpu
from jax.sharding import PartitionSpec as P

D = 768
HEADS = 12
HEAD_DIM = 64
FF = 3072
HALF = D // 2
STRIPS = FF // D
TOKENS = 129
PAD = 144
KEYS = 2 * PAD
PLANES = 16
PLANE = ("y", "x")
COLUMN = ("h", "c", "l")
SKIP, SPOTS, TRIPLE = 0, 96, 112
EXPAND, CONTRACT, MERGE = 0, 192, 384
FIRST_ROWS, SECOND_ROWS = 256, 432
ONE_ROWS = 112
TWO_SHARE, TWO_GROUP = 3 * D // 4, 48
EARLY_ROWS = 448
FIRST_PACK, SECOND_PACK = (12, 1, 6, 6, 6), (6, 6, 6, 6, 24, 6)
PACK = FIRST_PACK + SECOND_PACK
PACK_ROWS = 88
NAMES = ("skip", "triple", "expand", "contract", "merge")
SUM_ROWS = ONE_ROWS + EARLY_ROWS
SUM_STARTS = (0, 96, None, None, None) + tuple(ONE_ROWS + at for at in (0, 48, 96, 144, 192, 384))
epsilon = 1e-05
score_scale = 1.0 / math.sqrt(HEAD_DIM)
BF, F32 = jnp.bfloat16, jnp.float32
ATTEND = FF + FF // 2
NORMED = ATTEND + HALF
GIFT = NORMED + D


def mm(left, right):
    return jnp.dot(left, right, preferred_element_type=F32)


def mm_t(left, right):
    return lax.dot_general(left, right, (((1,), (1,)), ((), ())), preferred_element_type=F32)


def t_mm(left, right):
    return lax.dot_general(left, right, (((0,), (0,)), ((), ())), preferred_element_type=F32)


def order(core, one, two):
    return jnp.where(core == 0, one, two), jnp.where(core == 0, two, one)


def split(core, block):
    return order(core, block[:, :HALF], block[:, HALF:])


def norm_stats(values):
    mean_value = jnp.mean(values, axis=-1, keepdims=True)
    centered = values - mean_value
    variance = jnp.mean(centered * centered, axis=-1, keepdims=True)
    inverse = lax.rsqrt(variance + epsilon)
    return centered * inverse, inverse


def norm_backward(incoming, scaled, inverse, gain):
    weighted = incoming * gain
    first_mean = jnp.mean(weighted, axis=-1, keepdims=True)
    second_mean = jnp.mean(weighted * scaled, axis=-1, keepdims=True)
    value_grad = inverse * (weighted - first_mean - scaled * second_mean)
    return (
        value_grad,
        jnp.sum(incoming * scaled, axis=0, keepdims=True),
        jnp.sum(incoming, axis=0, keepdims=True),
    )


def padded(block):
    return jnp.concatenate([block, jnp.zeros((PAD - TOKENS, block.shape[1]), block.dtype)], axis=0)


def load(pairs, sems):
    copies = [pltpu.make_async_copy(s, d, sems.at[k]) for k, (s, d) in enumerate(pairs)]
    for copy in copies:
        copy.start()
    return copies


def matrix(ref, at, rows):
    return ref[:, at : at + rows, :].reshape(PLANES * rows, HALF)


def spot_masks(width):
    lanes = lax.broadcasted_iota(jnp.int32, (128, D), 0)
    spots = lax.broadcasted_iota(jnp.int32, (128, D), 1)
    return lanes, lax.rem(spots, width), lax.div(spots, width)


def steps_to(place_ref, plane):
    return (plane // 4 - place_ref[1]) & 3, (plane % 4 - place_ref[2]) & 3


def wait(copies):
    for copy in copies:
        copy.wait()


def tiles_of(matrix_name):
    count, strips, across = {"skip": (6, 1, 6), "triple": (18, 1, 6), "merge": (6, 1, 6), "expand": (24, STRIPS, 24), "contract": (6, 1, 6)}[matrix_name]
    for tile in range(count):
        block, inside = divmod(tile, across)
        half, rest = divmod(inside, across // 2)
        yield tile, half, block + rest // 3, rest % 3


def pack_kernel(*refs):
    count = len(NAMES)
    sources, (row_ref, out_ref, rows_ref), scratch = refs[:count], refs[count : count + 3], refs[count + 3 :]
    low, scratch, sems = scratch[:count], scratch[count : 2 * count], scratch[2 * count]
    copies = load(list(zip(sources, low)), sems)
    at = 0
    for name, held, ref, copy in zip(NAMES, scratch, low, copies):
        copy.wait()
        held[...] = ref[...].astype(F32)
        tiles = list(tiles_of(name))
        rows = held.shape[0] // len(tiles)
        for tile, half, strip, spot in tiles:
            first = at + strip * rows
            rows_ref[half, first : first + rows, 128 * spot : 128 * spot + 128] = held[pl.ds(tile, rows, stride=len(tiles)), :]
        at += rows * (1 + max(t[2] for t in tiles))
        if name == "skip":
            rows_ref[0, at : at + 1, :] = row_ref[...]
            rows_ref[1, at : at + 1, :] = row_ref[...]
            at += 1
    rows_ref[:, at:PACK_ROWS, :] = jnp.zeros((2, PACK_ROWS - at, HALF), F32)
    for half in range(2):
        packed = rows_ref[half].astype(BF)
        for device in range(8):
            if device // 2 % 2 == half:
                out_ref[device] = packed


def unpack_kernel(low_ref, high_ref, *refs):
    outs = dict(zip(NAMES, refs))
    at = 0
    for name in NAMES:
        tiles = list(tiles_of(name))
        rows = outs[name].shape[0] // len(tiles)
        for tile, half, strip, spot in tiles:
            first = at + strip * rows
            source = high_ref if half else low_ref
            outs[name][pl.ds(tile, rows, stride=len(tiles)), :] = source[first : first + rows, 128 * spot : 128 * spot + 128]
        at += rows * (1 + max(t[2] for t in tiles))
        if name == "skip":
            refs[5][...] = low_ref[at : at + 1, :128] + high_ref[at : at + 1, :128]
            at += 1


def prepare_kernel(core_ref, scale_ref, in_ref, skip_ref, cotangent_ref, after_ref, gift_ref):
    gift_ref[:, :D] = padded(in_ref[...])
    gift_ref[:, D : 2 * D] = padded(skip_ref[...])
    after = padded(cotangent_ref[...].astype(F32) * scale_ref[0]).astype(BF)
    after_ref[...] = after
    gift_ref[:, 2 * D :] = split(core_ref[0], after)[1]


def spots_kernel(first_ref, out_ref, rows_ref, sems):
    wait(load([(first_ref.at[:, SPOTS : SPOTS + 16, :], rows_ref)], sems))
    held = rows_ref[:, :, :128].astype(F32)[:, :8].reshape(128, 128).astype(BF)
    for j in range(7):
        lanes, place, owner = spot_masks(6)
        one_hot = (lanes - 6 * j == place).astype(BF)
        spread = jnp.where(owner == lanes, mm(held, one_hot), 0.0)
        out_ref[j : j + 1, :] = jnp.sum(spread, axis=0, keepdims=True)
    out_ref[7:8, :] = jnp.zeros((1, D), F32)
    lanes, place, owner = spot_masks(24)
    spread = mm(held, (lanes - 42 == place).astype(BF))
    for m in range(STRIPS):
        out_ref[8 + m : 9 + m, :] = jnp.sum(jnp.where(owner + 32 * m == lanes, spread, 0.0), axis=0, keepdims=True)
    out_ref[12:16, :] = jnp.zeros((4, D), F32)


def first_kernel(core_ref, joined_ref, own_ref, other_ref, spots_ref, united_ref, normed_ref, query_ref, pair_ref, so, ss, to, ts, sems):
    core = core_ref[0]
    copies = load(
        [
            (own_ref.at[:, SKIP : SKIP + 96, :], so),
            (other_ref.at[:, SKIP : SKIP + 96, :], ss),
            (own_ref.at[:, TRIPLE : TRIPLE + 144, :], to),
            (other_ref.at[:, TRIPLE : TRIPLE + 144, :], ts),
        ],
        sems,
    )
    joined = joined_ref[:, : 2 * D]
    copies[0].wait()
    one = mm(joined, matrix(so, 0, 96))
    copies[1].wait()
    two = mm(joined, matrix(ss, 0, 96))
    united = jnp.concatenate(order(core, one, two), axis=1) + spots_ref[0:1, :]
    united_ref[...] = united
    scaled, _ = norm_stats(united)
    normed = (scaled * spots_ref[1:2, :] + spots_ref[2:3, :]).astype(BF)
    normed_ref[...] = normed
    copies[2].wait()
    copies[3].wait()
    for k in range(3):
        one = mm(normed, matrix(to, 48 * k, 48))
        two = mm(normed, matrix(ts, 48 * k, 48))
        block = jnp.concatenate(order(core, one, two), axis=1).astype(BF)
        if k == 0:
            query_ref[...] = block
        else:
            pair_ref[:, (k - 1) * D : k * D] = block


def key_mask():
    spots = lax.broadcasted_iota(jnp.int32, (1, KEYS), 1)
    return (spots < TOKENS) | ((spots >= PAD) & (spots < PAD + TOKENS))


def attend_kernel(query_ref, pair_ref, came_ref, mixed_ref, total_ref):
    mask = key_mask()
    total_ref[...] = jnp.zeros((PAD, 128), F32)
    for pair in range(HEADS // 2):
        at = slice(128 * pair, 128 * pair + 128)
        late = slice(D + 128 * pair, D + 128 * pair + 128)
        query = query_ref[:, at]
        keys = jnp.concatenate([pair_ref[:, at], came_ref[:, at]], axis=0)
        values = jnp.concatenate([pair_ref[:, late], came_ref[:, late]], axis=0)
        done = []
        for side in range(2):
            head = slice(HEAD_DIM * side, HEAD_DIM * side + HEAD_DIM)
            scores = mm_t(query[:, head], keys[:, head]) * score_scale
            scores = jnp.where(mask, scores, -1e30)
            largest = jnp.max(scores, axis=-1, keepdims=True)
            powered = jnp.exp(scores - largest)
            totals = jnp.sum(powered, axis=-1, keepdims=True)
            total_ref[:, 2 * pair + side : 2 * pair + side + 1] = largest + jnp.log(totals)
            soft_low = (powered / totals).astype(BF)
            done.append(mm(soft_low, values[:, head]))
        mixed_ref[:, at] = jnp.concatenate(done, axis=1).astype(BF)


def forward_kernel(core_ref, scale_ref, mixed_ref, united_ref, cotangent_ref, after_ref, own_ref, other_ref, spots_ref, out_ref, middle_grad_ref, vector_ref, gift_ref, kept_ref, eo, es, co, cs, mo, ms, slope_ref, low_ref, sems):
    core = core_ref[0]
    copies = load(
        [
            (own_ref.at[:, MERGE : MERGE + 48, :], mo),
            (other_ref.at[:, MERGE : MERGE + 48, :], ms),
            *[
                (ref.at[:, 48 * k : 48 * k + 48, :], to.at[:, 48 * k : 48 * k + 48, :])
                for k in range(STRIPS)
                for ref, to in ((own_ref, eo), (other_ref, es))
            ],
            (own_ref.at[:, CONTRACT : CONTRACT + 192, :], co),
            (other_ref.at[:, CONTRACT : CONTRACT + 192, :], cs),
        ],
        sems,
    )
    after = after_ref[...]
    vector_ref[...] = jnp.zeros((16, D), F32)
    vector_ref[6:7, :] = jnp.sum(after.astype(F32), axis=0, keepdims=True)
    after_own, after_other = split(core, after)
    mixed = mixed_ref[...]
    wait(copies[:2])
    one, two = mm(mixed, matrix(mo, 0, 48)), mm(mixed, matrix(ms, 0, 48))
    middle = united_ref[...] + jnp.concatenate(order(core, one, two), axis=1) + spots_ref[3:4, :]
    scaled, inverse = norm_stats(middle)
    normed = (scaled * spots_ref[4:5, :] + spots_ref[5:6, :]).astype(BF)
    gift_ref[:, NORMED:] = normed
    for k in range(STRIPS):
        wait(copies[2 + 2 * k : 4 + 2 * k])
        one, two = order(core, mm(normed, matrix(eo, 48 * k, 48)), mm(normed, matrix(es, 48 * k, 48)))
        for side, block in ((0, one), (1, two)):
            at = side * STRIPS * HALF + k * HALF
            bias = spots_ref[8 + at // D : 9 + at // D, at % D : at % D + HALF]
            block = block + bias
            cumulative = 0.5 * (1.0 + lax.erf(block * (1.0 / math.sqrt(2.0))))
            density = jnp.exp(-0.5 * block * block) * (1.0 / math.sqrt(2.0 * math.pi))
            gift_ref[:, at : at + HALF] = (block * cumulative).astype(BF)
            slope_ref[:, at : at + HALF] = cumulative + block * density
    wait(copies[2 + 2 * STRIPS :])
    active = gift_ref[:, :FF]
    one, two = mm(active, matrix(co, 0, 192)), mm(active, matrix(cs, 0, 192))
    output = middle + jnp.concatenate(order(core, one, two), axis=1) + spots_ref[6:7, :]
    out_ref[...] = output[:TOKENS].astype(BF)
    for j in range(2 * STRIPS):
        at, planes = slice(HALF * j, HALF * j + HALF), slice(2 * j, 2 * j + 2)
        back = mm_t(after_own, co[planes, :, :].reshape(HALF, HALF)) + mm_t(after_other, cs[planes, :, :].reshape(HALF, HALF))
        low = (back * slope_ref[:, at]).astype(BF)
        low_ref[:, at] = low
        row = 8 + j // 2
        vector_ref[row : row + 1, HALF * (j % 2) : HALF * (j % 2) + HALF] = jnp.sum(low.astype(F32), axis=0, keepdims=True)
    incoming = jnp.zeros((PAD, D), F32)
    for k in range(STRIPS):
        one, two = order(
            core,
            low_ref[:, k * HALF : (k + 1) * HALF],
            low_ref[:, (STRIPS + k) * HALF : (STRIPS + k + 1) * HALF],
        )
        kept_ref[:, k * HALF : (k + 1) * HALF] = one
        gift_ref[:, FF + k * HALF : FF + (k + 1) * HALF] = two
        incoming = incoming + mm_t(one, matrix(eo, 48 * k, 48)) + mm_t(two, matrix(es, 48 * k, 48))
    back_two, gain_grad, shift_grad = norm_backward(incoming, scaled, inverse, spots_ref[4:5, :])
    vector_ref[4:5, :] = gain_grad
    vector_ref[5:6, :] = shift_grad
    middle_grad = padded(cotangent_ref[...].astype(F32) * scale_ref[0]) + back_two
    middle_grad_ref[...] = middle_grad
    attend = middle_grad.astype(BF)
    vector_ref[3:4, :] = jnp.sum(attend.astype(F32), axis=0, keepdims=True)
    gift_ref[:, ATTEND:NORMED] = split(core, attend)[1]


def early_kernel(core_ref, gift_any, came_any, kept_any, after_ref, first_came_any, mixed_any, mixed_came_any, middle_grad_any, grad_ref, gift_ref, came_ref, kept_ref, after_came_ref, mixed_ref, mixed_came_ref, middle_grad_ref, go, sems, out_sems):
    core = core_ref[0]
    copies = load(
        [
            (gift_any.at[:, :FF], gift_ref.at[:, :FF]),
            (came_any.at[:, :FF], came_ref.at[:, :FF]),
            (first_came_any.at[:, 2 * D :], after_came_ref),
            (gift_any.at[:, NORMED:], gift_ref.at[:, NORMED:]),
            (came_any.at[:, FF:], came_ref.at[:, FF:]),
            (kept_any, kept_ref),
            (mixed_any, mixed_ref),
            (mixed_came_any, mixed_came_ref),
            (middle_grad_any, middle_grad_ref),
        ],
        sems,
    )
    wait(copies[:3])
    after, after_came = split(core, after_ref[...])[0], after_came_ref[...]
    for j in range(2 * STRIPS):
        at, planes = slice(HALF * j, HALF * j + HALF), slice(2 * j, 2 * j + 2)
        grad = t_mm(gift_ref[:, at], after) + t_mm(came_ref[:, at], after_came)
        go[planes, CONTRACT : CONTRACT + 192, :] = grad.astype(BF).reshape(2, 192, HALF)
    rows = lambda at, to: (go.at[:, at:to, :], grad_ref.at[:, at:to, :])
    sends = load([rows(CONTRACT, CONTRACT + 192)], out_sems)
    wait(copies[3:])
    attend = split(core, middle_grad_ref[...].astype(BF))[0]
    grad = t_mm(mixed_ref[...], attend) + t_mm(mixed_came_ref[...], came_ref[:, ATTEND:NORMED])
    go[:, MERGE : MERGE + 48, :] = grad.astype(BF).reshape(PLANES, 48, HALF)
    go[:, MERGE + 48 :, :] = jnp.zeros((PLANES, EARLY_ROWS - MERGE - 48, HALF), BF)
    sends += load([rows(MERGE, EARLY_ROWS)], out_sems.at[1:])
    normed, normed_came = gift_ref[:, NORMED:], came_ref[:, NORMED:]
    for k in range(STRIPS):
        grad = t_mm(normed, kept_ref[:, k * HALF : (k + 1) * HALF]) + t_mm(
            normed_came, came_ref[:, FF + k * HALF : FF + (k + 1) * HALF]
        )
        go[:, EXPAND + 48 * k : EXPAND + 48 * (k + 1), :] = grad.astype(BF).reshape(PLANES, 48, HALF)
        sends += load([rows(EXPAND + 48 * k, EXPAND + 48 * (k + 1))], out_sems.at[2 + k :])
    wait(sends)


def backward_kernel(core_ref, middle_grad_ref, query_ref, pair_ref, came_ref, total_ref, own_ref, other_ref, query_grad_ref, pair_grad_ref, sent_ref, mixed_grad_ref, mo, ms, sems):
    core = core_ref[0]
    copies = load(
        [(own_ref.at[:, MERGE : MERGE + 48, :], mo), (other_ref.at[:, MERGE : MERGE + 48, :], ms)], sems
    )
    attend_own, attend_other = split(core, middle_grad_ref[...].astype(BF))
    mask = key_mask()
    copies[0].wait()
    copies[1].wait()
    mixed_grad_ref[...] = (mm_t(attend_own, matrix(mo, 0, 48)) + mm_t(attend_other, matrix(ms, 0, 48))).astype(BF)
    for pair in range(HEADS // 2):
        at = slice(128 * pair, 128 * pair + 128)
        late = slice(D + 128 * pair, D + 128 * pair + 128)
        query, mixed_grad = query_ref[:, at], mixed_grad_ref[:, at]
        keys = jnp.concatenate([pair_ref[:, at], came_ref[:, at]], axis=0)
        values = jnp.concatenate([pair_ref[:, late], came_ref[:, late]], axis=0)
        query_parts, key_parts, value_parts = [], [], []
        for side in range(2):
            head = slice(HEAD_DIM * side, HEAD_DIM * side + HEAD_DIM)
            scores = mm_t(query[:, head], keys[:, head]) * score_scale
            scores = jnp.where(mask, scores, -1e30)
            soft = jnp.exp(scores - total_ref[:, 2 * pair + side : 2 * pair + side + 1])
            soft_grad = mm_t(mixed_grad[:, head], values[:, head])
            inner = jnp.sum(soft * soft_grad, axis=-1, keepdims=True)
            scores_grad = (soft * (soft_grad - inner)).astype(BF)
            query_parts.append(mm(scores_grad, keys[:, head]))
            key_parts.append(t_mm(scores_grad, query[:, head]))
            value_parts.append(t_mm(soft.astype(BF), mixed_grad[:, head]))
        query_grad_ref[:, at] = (jnp.concatenate(query_parts, axis=1) * score_scale).astype(BF)
        key_grad = jnp.concatenate(key_parts, axis=1) * score_scale
        value_grad = jnp.concatenate(value_parts, axis=1)
        pair_grad_ref[:, at] = key_grad[:PAD]
        pair_grad_ref[:, late] = value_grad[:PAD]
        sent_ref[:, at] = key_grad[PAD:].astype(BF)
        sent_ref[:, late] = value_grad[PAD:].astype(BF)


def scatter(place_ref, ref, block, at, by_y):
    rows = block.shape[0] // PLANES
    for plane in range(PLANES):
        step_y, step_x = steps_to(place_ref, plane)
        spot = 4 * step_y + step_x if by_y else 4 * step_x + step_y
        ref[spot, at : at + rows, :] = block[plane * rows : (plane + 1) * rows]


def vector_rows(vectors, places):
    rows = jnp.zeros((128, 128), F32)
    for vector, at in zip(vectors, places):
        lanes, place, owner = spot_masks(6)
        spread = jnp.where(owner == lanes, vector, 0.0).astype(BF)
        rows = rows + mm_t(spread, (lanes - at == place).astype(BF))
    return rows


def query_kernel(core_ref, query_grad_ref, early_ref, normed_ref, normed_came_ref, by_z_ref, own_ref, other_ref, incoming_ref, rows_ref, moved_ref, moved_came_ref, to, ts, sems):
    copies = load(
        [(own_ref.at[:, TRIPLE : TRIPLE + 48, :], to), (other_ref.at[:, TRIPLE : TRIPLE + 48, :], ts)], sems
    )
    rows = vector_rows([early_ref[j : j + 1, :] for j in range(3, 7)], (18, 24, 30, 36))
    lanes, place, owner = spot_masks(24)
    for m in range(STRIPS):
        spread = jnp.where(owner + 32 * m == lanes, early_ref[8 + m : 9 + m, :], 0.0).astype(BF)
        rows = rows + mm_t(spread, (lanes - 42 == place).astype(BF))
    rows_ref[...] = rows
    one, two = split(core_ref[0], query_grad_ref[...])
    wait(copies)
    incoming_ref[...] = mm_t(one, matrix(to, 0, 48)) + mm_t(two, matrix(ts, 0, 48))
    moved_ref[...] = mm(normed_ref[...], by_z_ref[...]).astype(BF)
    moved_came_ref[...] = mm(normed_came_ref[...], by_z_ref[...]).astype(BF)


def triple_kernel(core_ref, united_ref, middle_grad_ref, query_grad_ref, pair_grad_ref, came_ref, incoming_ref, own_ref, other_ref, spots_ref, low_ref, vector_ref, kept_ref, gift_ref, to, ts, sems):
    core = core_ref[0]
    copies = load(
        [(own_ref.at[:, TRIPLE + 48 : TRIPLE + 144, :], to), (other_ref.at[:, TRIPLE + 48 : TRIPLE + 144, :], ts)], sems
    )
    scaled, inverse = norm_stats(united_ref[...])
    incoming = incoming_ref[...]
    wait(copies)
    for k in range(3):
        if k == 0:
            block = query_grad_ref[...]
        else:
            at = slice((k - 1) * D, k * D)
            block = (pair_grad_ref[:, at] + came_ref[:, at].astype(F32)).astype(BF)
        one, two = split(core, block)
        kept_ref[:, k * HALF : (k + 1) * HALF] = one
        gift_ref[:, k * HALF : (k + 1) * HALF] = two
        if k:
            incoming = incoming + mm_t(one, matrix(to, 48 * (k - 1), 48)) + mm_t(two, matrix(ts, 48 * (k - 1), 48))
    back_one, gain_grad, shift_grad = norm_backward(incoming, scaled, inverse, spots_ref[1:2, :])
    united_low = (middle_grad_ref[...] + back_one).astype(BF)
    low_ref[...] = united_low
    gift_ref[:, 3 * HALF :] = split(core, united_low)[1]
    vector_ref[0:1, :] = jnp.sum(united_low.astype(F32), axis=0, keepdims=True)
    vector_ref[1:2, :] = gain_grad
    vector_ref[2:3, :] = shift_grad
    vector_ref[3:8, :] = jnp.zeros((5, D), F32)


def skip_kernel(core_ref, low_ref, own_ref, other_ref, in_grad_ref, skip_grad_ref, so, ss, sems):
    copies = load(
        [(own_ref.at[:, SKIP : SKIP + 96, :], so), (other_ref.at[:, SKIP : SKIP + 96, :], ss)], sems
    )
    low_own, low_other = split(core_ref[0], low_ref[...])
    wait(copies)
    for half, grad_ref in ((0, in_grad_ref), (1, skip_grad_ref)):
        planes = slice(8 * half, 8 * half + 8)
        back = mm_t(low_own, so[planes, :, :].reshape(D, HALF)) + mm_t(low_other, ss[planes, :, :].reshape(D, HALF))
        grad_ref[...] = back[:TOKENS].astype(BF)


def late_kernel(place_ref, joined_ref, first_came_ref, normed_ref, normed_came_ref, low_ref, kept_ref, came_ref, early_ref, vector_ref, *refs):
    one_refs, two_refs, (go, gt, sems) = refs[:4], refs[4:8], refs[8:]
    for k in range(3):
        at = slice(k * HALF, (k + 1) * HALF)
        grad = (t_mm(normed_ref[...], kept_ref[:, at]) + t_mm(normed_came_ref[...], came_ref[:, at])).astype(BF)
        for z in range(4):
            gt[(z - place_ref[3]) & 3, 192 * k : 192 * k + 192, :] = grad[192 * z : 192 * z + 192]
    sends = load([(gt.at[k], two_refs[k]) for k in range(4)], sems.at[:4])
    low, low_came = split(place_ref[0], low_ref[...])[0], came_ref[:, 3 * HALF :]
    grad = t_mm(joined_ref[:, : 2 * D], low) + t_mm(first_came_ref[:, : 2 * D], low_came)
    scatter(place_ref, go, grad.astype(BF), SKIP, False)
    rows = early_ref[...] + vector_rows([vector_ref[j : j + 1, :] for j in range(3)], (0, 6, 12))
    rows = jnp.concatenate([rows.reshape(PLANES, 8, 128), jnp.zeros((PLANES, 8, 128), F32)], axis=1)
    rows = jnp.concatenate([rows, jnp.zeros((PLANES, 16, HALF - 128), F32)], axis=2)
    scatter(place_ref, go, rows.reshape(PLANES * 16, HALF).astype(BF), 96, False)
    wait(sends)
    wait(load([(go.at[4 * k : 4 * k + 4], one_refs[k]) for k in range(4)], sems.at[4:]))


def group_kernel(place_ref, share_ref, moves_ref, *refs):
    outs, rows_ref = refs[:4], refs[4]
    rows_ref[...] = mm(moves_ref[...], share_ref[...]).astype(BF).reshape(PLANES, TWO_GROUP, HALF)
    for k, out_ref in enumerate(outs):
        for n in range(4):
            out_ref[n] = rows_ref[4 * ((place_ref[1] + n) & 3) + ((place_ref[2] + k) & 3)]


def moves_of(rows, columns, pairs):
    moves = np.zeros((rows, columns), np.float32)
    for row, column in pairs:
        moves[row, column] = 1.0
    return moves


def features_by_z():
    return moves_of(
        D,
        D,
        (
            (48 * p + 24 * h + 12 * c + 6 * l + r, 192 * (2 * h + l) + 12 * p + 6 * c + r)
            for p in range(PLANES)
            for h in range(2)
            for c in range(2)
            for l in range(2)
            for r in range(6)
        ),
    )


def rows_by_group():
    return moves_of(
        PLANES * TWO_GROUP,
        TWO_SHARE,
        ((TWO_GROUP * p + 12 * k + r, 192 * k + 12 * p + r) for p in range(PLANES) for k in range(3) for r in range(12)),
    )


def rows_by_core():
    return moves_of(
        2 * PACK_ROWS,
        TWO_GROUP,
        ((PACK_ROWS * c + 13 + 6 * k + r, 12 * k + 6 * c + r) for c in range(2) for k in range(3) for r in range(6)),
    )


def column_kernel(one_ref, early_ref, moves_ref, out_ref, rows_ref):
    rows_ref[:ONE_ROWS] = one_ref[...]
    rows_ref[ONE_ROWS:] = early_ref[...]
    out_ref[...] = mm(moves_ref[...], rows_ref[...]).astype(BF).reshape(4, 2 * PACK_ROWS, HALF)


def column_moves():
    moves = np.zeros((8 * PACK_ROWS, SUM_ROWS), np.float32)
    for high in range(2):
        for low in range(2):
            for core in range(2):
                at = ((2 * high + low) * 2 + core) * PACK_ROWS
                device = (2 * high + core) * 2 + low
                for rows, start in zip(PACK, SUM_STARTS):
                    for row in range(rows if start is not None else 0):
                        moves[at + row, start + device * rows + row] = 1.0
                    at += rows
    return moves


def call(kernel, name, args, outs, scratch, flops, room):
    place = {
        "s": pl.BlockSpec(memory_space=pltpu.SMEM),
        "v": pl.BlockSpec(memory_space=pltpu.VMEM),
        "a": pl.BlockSpec(memory_space=pl.ANY),
    }
    moved = sum(a.size * a.dtype.itemsize for a, _ in args)
    return pl.pallas_call(
        kernel,
        out_shape=[jax.ShapeDtypeStruct(shape, dtype) for shape, dtype, _ in outs],
        in_specs=[place[w] for _, w in args],
        out_specs=[place[w] for _, _, w in outs],
        scratch_shapes=scratch,
        compiler_params=pltpu.CompilerParams(vmem_limit_bytes=room * 2**20),
        cost_estimate=pl.CostEstimate(flops=int(flops), bytes_accessed=int(moved), transcendentals=0),
        name=name,
    )(*[a for a, _ in args])


def swap(block, axis):
    return lax.ppermute(block, axis, [(0, 1), (1, 0)])


def step(block, axis, steps):
    return lax.ppermute(block, axis, [((i + steps) % 4, i) for i in range(4)])


def sum_line(blocks, axis):
    total = blocks[0].astype(F32)
    for k in (1, 2, 3):
        total = total + step(blocks[k], axis, 4 - k).astype(F32)
    return total


def sum_part(blocks, first, second):
    line = blocks[0].astype(F32)
    for k in (1, 2, 3):
        line = line + step(blocks[k], first, 4 - k).astype(F32)
    total = line[0]
    for k in (1, 2, 3):
        total = total + step(line[k].astype(BF), second, 4 - k).astype(F32)
    return total.astype(BF)


def regroup(block, pack):
    at, parts = 0, []
    for rows in pack:
        parts.append(block[:, at : at + rows].reshape(-1, HALF))
        at += rows
    return parts


def pick_table(indices, table):
    match = indices[:, None] == jnp.arange(table.shape[0], dtype=jnp.int32)[None, :]
    return jnp.sum(jnp.where(match, table[None, :], 0.0), axis=1)


def per_device(
    inputs,
    skipped,
    cotangent,
    timestep,
    class_ids,
    time_weight,
    class_weight,
    skip_weight,
    skip_bias,
    first_gain,
    first_shift,
    triple_weight,
    merge_weight,
    merge_bias,
    second_gain,
    second_shift,
    expand_weight,
    expand_bias,
    contract_weight,
    contract_bias,
):
    core_index = lax.axis_index("c").astype(jnp.int32)
    core = core_index[None]
    place = jnp.stack([core_index] + [lax.axis_index(axis).astype(jnp.int32) for axis in ("y", "x", ("h", "l"))])


    inputs, skipped, cotangent = (a.reshape(TOKENS, D) for a in (inputs, skipped, cotangent))
    sem = pltpu.SemaphoreType.DMA
    weight = lambda rows: pltpu.VMEM((PLANES, rows, HALF), BF)
    tokens = lambda width, dtype=BF, where="v": ((PAD, width), dtype, where)
    plane = lambda rows: ((PLANES, rows, HALF), BF, "a")

    vectors = (skip_bias, first_gain, first_shift, merge_bias, second_gain, second_shift, contract_bias, expand_bias)
    row, at = jnp.zeros((1, HALF), F32), 0
    for vector in vectors:
        row = row + jnp.pad(vector.astype(F32)[None, :], ((0, 0), (at, HALF - at - vector.shape[0])))
        at += vector.shape[0]
    flat = dict(
        skip=skip_weight, triple=triple_weight, merge=merge_weight, expand=expand_weight, contract=contract_weight
    )
    flat = {name: a.reshape(-1, 128) for name, a in flat.items()}

    (packed,) = call(
        pack_kernel,
        "pack",
        [(flat[n], "a") for n in NAMES] + [(row, "v")],
        [((8, PACK_ROWS, HALF), BF, "v")],
        [pltpu.VMEM((2, PACK_ROWS, HALF), F32)]
        + [pltpu.VMEM(flat[n].shape, dtype) for dtype in (BF, F32) for n in NAMES]
        + [sem((len(NAMES),))],
        1e6,
        58,
    )
    column = regroup(lax.all_to_all(packed, COLUMN, 0, 0, tiled=True), PACK)
    first = jnp.concatenate(column[:2] + [jnp.zeros((8, HALF), BF)] + column[2:5], axis=0)
    second = jnp.concatenate(column[5:], axis=0)
    second_own = lax.all_gather(second, PLANE, axis=0, tiled=True).reshape(PLANES, SECOND_ROWS, HALF)
    first_own = lax.all_to_all(
        jnp.broadcast_to(first[None], (PLANES, FIRST_ROWS, HALF)), PLANE, 0, 0, tiled=True
    )
    first_own, timestep = lax.optimization_barrier((first_own, timestep))
    scale = pick_table(timestep, time_weight) * pick_table(class_ids, class_weight)
    first_other = swap(first_own, "c")
    after, gift = call(
        prepare_kernel,
        "prepare",
        [(core, "s"), (scale, "s"), (inputs, "v"), (skipped, "v"), (cotangent, "v")],
        [tokens(D), tokens(2 * D + HALF)],
        [],
        1e6,
        8,
    )
    gift_came = swap(gift, "c")

    (spots,) = call(
        spots_kernel, "vectors", [(first_own, "a")], [((16, D), F32, "v")], [weight(16), sem((1,))], 2e8, 8
    )
    united, normed, query, pair = call(
        first_kernel,
        "skip_and_triple",
        [(core, "s"), (gift, "v"), (first_own, "a"), (first_other, "a"), (spots, "v")],
        [tokens(D, F32), tokens(D), tokens(D), tokens(2 * D)],
        [weight(96), weight(96), weight(144), weight(144), sem((4,))],
        2 * PAD * D * (2 * D + 3 * D),
        16,
    )
    pair, gift_came = lax.optimization_barrier((pair, gift_came))
    pair_came = swap(pair, "l")
    normed_came = swap(normed, "c")
    second_own, pair_came, normed_came = lax.optimization_barrier((second_own, pair_came, normed_came))
    second_other = swap(second_own, "c")
    mixed, totals = call(
        attend_kernel,
        "attention",
        [(query, "v"), (pair, "v"), (pair_came, "v")],
        [tokens(D), tokens(128, F32)],
        [],
        2 * PAD * D * 2 * KEYS,
        58,
    )
    mixed_came = swap(mixed, "c")
    mixed, mixed_came = lax.optimization_barrier((mixed, mixed_came))
    output, middle_grad, early_vectors, forward_gift, forward_kept = call(
        forward_kernel,
        "feed_forward",
        [
            (core, "s"),
            (scale, "s"),
            (mixed, "v"),
            (united, "v"),
            (cotangent, "v"),
            (after, "v"),
            (second_own, "a"),
            (second_other, "a"),
            (spots, "v"),
        ],
        [((TOKENS, D), BF, "v"), tokens(D, F32), ((16, D), F32, "v"), tokens(GIFT), tokens(FF // 2)],
        [weight(192)] * 4
        + [weight(48)] * 2
        + [pltpu.VMEM((PAD, FF), F32), pltpu.VMEM((PAD, FF), BF), sem((12,))],
        2 * PAD * D * FF * 4,
        58,
    )
    forward_came = swap(forward_gift, "c")
    query_grad, pair_grad, pair_sent = call(
        backward_kernel,
        "attention_backward",
        [
            (core, "s"),
            (middle_grad, "v"),
            (query, "v"),
            (pair, "v"),
            (pair_came, "v"),
            (totals, "v"),
            (second_own, "a"),
            (second_other, "a"),
        ],
        [tokens(D), tokens(2 * D, F32), tokens(2 * D)],
        [pltpu.VMEM((PAD, D), BF), weight(48), weight(48), sem((2,))],
        2 * PAD * D * (D + 5 * KEYS),
        58,
    )
    grad_came = swap(pair_sent, "l")
    (early_grads,) = call(
        early_kernel,
        "early_gradients",
        [
            (core, "s"),
            (forward_gift, "a"),
            (forward_came, "a"),
            (forward_kept, "a"),
            (after, "v"),
            (gift_came, "a"),
            (mixed, "a"),
            (mixed_came, "a"),
            (middle_grad, "a"),
        ],
        [plane(EARLY_ROWS)],
        [pltpu.VMEM((PAD, GIFT), BF)] * 2
        + [pltpu.VMEM((PAD, width), BF) for width in (FF // 2, HALF, D, D)]
        + [pltpu.VMEM((PAD, D), F32), weight(EARLY_ROWS), sem((9,)), sem((6,))],
        2 * PAD * D * FF * 2,
        58,
    )
    early_sum = lax.psum_scatter(early_grads.reshape(PLANES * EARLY_ROWS, HALF), PLANE, scatter_dimension=0, tiled=True)
    early_vectors, query_grad = lax.optimization_barrier((early_vectors, query_grad))
    by_z = jnp.asarray(features_by_z(), BF)
    query_incoming, early_rows, moved, moved_came = call(
        query_kernel,
        "query_backward",
        [
            (core, "s"),
            (query_grad, "v"),
            (early_vectors, "v"),
            (normed, "v"),
            (normed_came, "v"),
            (by_z, "v"),
            (first_own, "a"),
            (first_other, "a"),
        ],
        [tokens(D, F32), ((128, 128), F32, "v"), tokens(D), tokens(D)],
        [weight(48)] * 2 + [sem((2,))],
        2 * PAD * D * D,
        24,
    )
    united_low, late_vectors, triple_kept, late_gift = call(
        triple_kernel,
        "triple_backward",
        [
            (core, "s"),
            (united, "v"),
            (middle_grad, "v"),
            (query_grad, "v"),
            (pair_grad, "v"),
            (grad_came, "v"),
            (query_incoming, "v"),
            (first_own, "a"),
            (first_other, "a"),
            (spots, "v"),
        ],
        [tokens(D), ((8, D), F32, "v"), tokens(3 * HALF), tokens(4 * HALF)],
        [weight(96)] * 2 + [sem((2,))],
        2 * PAD * D * (2 * D),
        16,
    )
    late_came = swap(late_gift, "c")
    input_grad, skip_grad = call(
        skip_kernel,
        "skip_backward",
        [(core, "s"), (united_low, "v"), (first_own, "a"), (first_other, "a")],
        [((TOKENS, D), BF, "v"), ((TOKENS, D), BF, "v")],
        [weight(96), weight(96), sem((2,))],
        2 * PAD * D * (2 * D),
        12,
    )
    late_came, input_grad, skip_grad = lax.optimization_barrier((late_came, input_grad, skip_grad))
    late = call(
        late_kernel,
        "late_gradients",
        [
            (place, "s"),
            (gift, "v"),
            (gift_came, "v"),
            (moved, "v"),
            (moved_came, "v"),
            (united_low, "v"),
            (triple_kept, "v"),
            (late_came, "v"),
            (early_rows, "v"),
            (late_vectors, "v"),
        ],
        [((4, ONE_ROWS, HALF), BF, "a")] * 4 + [((TWO_SHARE, HALF), BF, "a")] * 4,
        [weight(ONE_ROWS), pltpu.VMEM((4, TWO_SHARE, HALF), BF), sem((8,))],
        2 * PAD * D * (5 * D),
        58,
    )
    one_sum = sum_part(late[:4], "x", "y")
    share = sum_line(late[4:], ("h", "l")).astype(BF)
    groups = call(
        group_kernel,
        "by_group",
        [(place, "s"), (share, "v"), (jnp.asarray(rows_by_group(), BF), "v")],
        [((4, TWO_GROUP, HALF), BF, "v")] * 4,
        [pltpu.VMEM((PLANES, TWO_GROUP, HALF), BF)],
        2 * PLANES * TWO_GROUP * TWO_SHARE * HALF,
        12,
    )
    two_sum = mm(jnp.asarray(rows_by_core(), BF), sum_part(groups, "x", "y"))

    early_sum, two_sum = lax.optimization_barrier((early_sum, two_sum))

    (column,) = call(
        column_kernel,
        "by_device",
        [(one_sum, "v"), (early_sum, "v"), (jnp.asarray(column_moves(), BF), "v")],
        [((4, 2 * PACK_ROWS, HALF), BF, "v")],
        [pltpu.VMEM((SUM_ROWS, HALF), BF)],
        2 * SUM_ROWS * SUM_ROWS * HALF,
        12,
    )
    total = jnp.sum(lax.all_to_all(column, ("h", "l"), 0, 0, tiled=True).astype(F32), axis=0) + two_sum
    mine, sent = order(core_index, total[:PACK_ROWS], total[PACK_ROWS:])
    low, high = order(core_index, mine, swap(sent, "c"))
    rows_of = lambda name: ((flat[name].shape[0], 128), F32, "v")
    skip_out, triple_out, expand_out, contract_out, merge_out, vector_out = call(
        unpack_kernel,
        "by_weight",
        [(low, "v"), (high, "v")],
        [rows_of(name) for name in NAMES] + [((1, 128), F32, "v")],
        [],
        1e6,
        8,
    )
    vector_out = vector_out[0]
    spot = lambda j: vector_out[6 * j : 6 * j + 6]
    return (
        output[None],
        input_grad[None],
        skip_grad[None],
        skip_out.reshape(-1),
        spot(0),
        spot(1),
        spot(2),
        triple_out.reshape(-1),
        merge_out.reshape(-1),
        spot(3),
        spot(4),
        spot(5),
        expand_out.reshape(-1),
        vector_out[42:66],
        contract_out.reshape(-1),
        spot(6),
    )


def solution(mesh):
    fine = jax.sharding.Mesh(mesh.devices.reshape(4, 4, 2, 2, 2), ("y", "x", "h", "c", "l"))
    images = ("y", "x", "h", "c")
    everything = images + ("l",)
    tokens, shard = P(images, "l", None), P(everything)
    return jax.shard_map(
        per_device,
        mesh=fine,
        in_specs=(tokens,) * 3 + (P(images),) * 2 + (P(),) * 2 + (shard,) * 13,
        out_specs=(tokens,) * 3 + (shard,) * 13,
        check_vma=False,
    )
```
